512 devices in a mesh: section: 8 (over y, x_lo), dp: 64 (over z, x_hi, core).
Axes of the slice: x: 4 (x_hi: 2, x_lo: 2; x = x_hi * 2 + x_lo), y: 4, z: 16, core: 2. Of those that a mesh axis runs over, the one named last changes fastest.
Arguments:
- nodes: bfloat16 [256, 128, 512], P('dp'), may hold values from -120 to 120
- cotangent: bfloat16 [256, 128, 512], P('dp'), may hold values from -0.023925781 to 0.023925781
- w_qkv: bfloat16 [8, 512, 768], P('section'), may hold values from -0.25 to 0.25
- w_out: bfloat16 [8, 256, 512], P('section'), may hold values from -0.375 to 0.375
- tile_lists: int32 [256, 2, 2], P('dp'), may hold values from 0 to 1
- counts: int32 [256, 2], P('dp'), may hold values from 1 to 2
- virtual: int32 [256], P('dp'), may hold values from 0 to 1
Outputs:
- grad_qkv: bfloat16 [8, 512, 768], P('section')
- grad_out: bfloat16 [8, 256, 512], P('section')
The draws below stay inside these ranges and needn't reach their ends.
Inputs may be any that keep to these rules, and one draw needn't show every extreme that they name: `tile_lists`: entries name row tiles of the same batch; entries at or beyond counts are padding.
All inputs are finite; a program needn't handle non-finite values.
Results may differ from the reference program's by a relative error of at most 0.022.
Values may be sent and summed in bfloat16 or wider, within the bound.
No kernel may reach another device: no remote copies, remote signals or barrier semaphores. Data moves between devices by JAX's collectives and lax.ppermute only.
A program may use at most 64 MiB of HBM per device.

```python
import math
import jax
import jax.numpy as jnp
from jax import lax

D = 512
HEADS = 4
KT = 2
ROWS = 128
INNER = 256
RT = 2
LAYERS = 8
BATCHES = 256


def draw_nodes(key, part):
    first_key = jax.random.fold_in(key, 11)
    row_key = jax.random.fold_in(key, 12)
    column_key = jax.random.fold_in(key, 13)
    row_scale = jnp.exp(jax.random.uniform(row_key, (BATCHES, ROWS, 1), jnp.float32, 0.0, math.log(10.0)))
    column_scale = jnp.exp(jax.random.uniform(column_key, (1, 1, D), jnp.float32, 0.0, math.log(10.0)))
    base = jnp.clip(jax.random.normal(first_key, (BATCHES, ROWS, D), jnp.float32), -6.0, 6.0)
    return (base * row_scale * column_scale * 0.2).astype(jnp.bfloat16)


def plant(values, key, low, top_value):
    place = [jax.random.randint(jax.random.fold_in(key, axis), (), 0, length) for axis, length in enumerate(values.shape)]
    widest = values.shape.index(max(values.shape))
    beside = place[:widest] + [(place[widest] + 1) % values.shape[widest]] + place[widest + 1:]
    return values.at[tuple(place)].set(low).at[tuple(beside)].set(top_value)


def steps_of(key, extent, pieces, least, high):
    def one(dim, blocks):
        heights = jax.random.uniform(jax.random.fold_in(jax.random.fold_in(key, 6), dim), (blocks,), jnp.float32, least / len(pieces), high / len(pieces))
        return jnp.repeat(jnp.exp(heights), extent[dim] // blocks).reshape((-1,) + (1,) * (len(extent) - dim - 1))

    factor_of = one(*pieces[0])
    for cut in pieces[1:]:
        factor_of = factor_of * one(*cut)
    return factor_of


def normal_values(own_key, extent, deviation, bound, split=(), kind=jnp.bfloat16):
    level = steps_of(own_key, extent, split, -0.22, 0.18) if split else 1.0
    array = jax.random.normal(own_key, extent, jnp.float32) * deviation * level
    return jnp.minimum(jnp.maximum(array, -bound), bound).astype(kind)


def setup_inputs(seed: int = 0) -> dict:
    seeds = jax.random.split(jax.random.key(seed), 8)
    nodes = draw_nodes(jax.random.fold_in(seeds[7], 71), 0)
    cotangent = normal_values(seeds[1], (BATCHES, ROWS, D), 0.004, 0.023925781, ((0, 64),))
    w_qkv = normal_values(seeds[2], (LAYERS, D, 3 * INNER), D ** -0.5, 0.25, ((0, 8),))
    w_out = normal_values(seeds[3], (LAYERS, INNER, D), INNER ** -0.5, 0.375, ((0, 8),))
    tile_lists = plant(jax.random.randint(seeds[4], (BATCHES, RT, KT), 0, RT), jax.random.fold_in(seeds[4], 1), 0, RT - 1).astype(jnp.int32)
    counts = plant(jax.random.randint(seeds[5], (BATCHES, RT), 1, KT + 1), jax.random.fold_in(seeds[5], 1), 1, KT).astype(jnp.int32)
    virtual = plant(jax.random.randint(seeds[6], (BATCHES,), 0, RT), jax.random.fold_in(seeds[6], 1), 0, RT - 1).astype(jnp.int32)
    return {"nodes": nodes, "cotangent": cotangent, "w_qkv": w_qkv, "w_out": w_out, "tile_lists": tile_lists, "counts": counts, "virtual": virtual}


EPSILON = 1e-06
TEMPER = 4.0

def unit_norm(values):
    return values * lax.rsqrt(lax.optimization_barrier(jnp.mean(values * values, axis=-1, keepdims=True)) + EPSILON)

def key_tables(tile_list, valid_count, virtual_tile):
    tile_count = tile_list.shape[0]
    first = jnp.broadcast_to(virtual_tile.astype(jnp.int32), (tile_count, 1))
    key_tiles = jnp.concatenate([first, tile_list.astype(jnp.int32)], axis=1)
    slot_index = jnp.arange(tile_list.shape[1] + 1, dtype=jnp.int32)[None, :]
    key_valid = (slot_index == 0) | (slot_index - 1 < valid_count.astype(jnp.int32)[:, None])
    return (key_tiles, key_valid)

def attend_layer(hidden_in, weight_qkv, weight_out, key_tiles, key_valid):
    row_count = hidden_in.shape[0]
    tile_count, listed = key_tiles.shape
    tile_rows = row_count // tile_count
    inner_width = weight_out.shape[0]
    head_size = inner_width // HEADS
    widened = hidden_in.astype(jnp.float32)
    normed = (widened * lax.rsqrt(lax.optimization_barrier(jnp.mean(widened * widened, axis=-1, keepdims=True)) + EPSILON)).astype(jnp.bfloat16)
    projected = jnp.dot(normed, weight_qkv, preferred_element_type=jnp.float32)
    shaped = projected.reshape(tile_count, tile_rows, 3, HEADS, head_size)
    queries = (unit_norm(shaped[:, :, 0]) * (TEMPER / head_size)).astype(jnp.bfloat16)
    key_rows = unit_norm(shaped[:, :, 1]).astype(jnp.bfloat16)
    value_rows = shaped[:, :, 2].astype(jnp.bfloat16)
    gathered_keys = jnp.take(key_rows, key_tiles, axis=0).reshape(tile_count, listed * tile_rows, HEADS, head_size)
    gathered_values = jnp.take(value_rows, key_tiles, axis=0).reshape(tile_count, listed * tile_rows, HEADS, head_size)
    scores = jnp.einsum('tqhd,tkhd->thqk', queries.astype(jnp.float32), gathered_keys.astype(jnp.float32))
    open_keys = jnp.repeat(key_valid, tile_rows, axis=1)[:, None, None, :]
    exponent = jnp.where(open_keys, jnp.exp(scores), 0.0)
    attn = (exponent / lax.optimization_barrier(jnp.sum(exponent, axis=-1, keepdims=True))).astype(jnp.bfloat16)
    mixed = jnp.einsum('thqk,tkhd->tqhd', attn.astype(jnp.float32), gathered_values.astype(jnp.float32))
    mixed = mixed.astype(jnp.bfloat16).reshape(row_count, inner_width)
    return (widened + jnp.dot(mixed, weight_out, preferred_element_type=jnp.float32)).astype(jnp.bfloat16)

def reference(nodes, cotangent, w_qkv, w_out, tile_lists, counts, virtual):

    def per_batch(running, batch_item):
        start_rows, back_rows, tile_list, valid_count, virtual_tile = batch_item
        key_tiles, key_valid = key_tables(tile_list, valid_count, virtual_tile)

        def network(weights_a, weights_b):
            hidden = start_rows
            for position in range(LAYERS):
                hidden = attend_layer(hidden, weights_a[position], weights_b[position], key_tiles, key_valid)
            return hidden
        ignored, pullback = jax.vjp(network, w_qkv, w_out)
        term_qkv, term_out = pullback(back_rows)
        return ((running[0] + term_qkv.astype(jnp.float32), running[1] + term_out.astype(jnp.float32)), None)
    initial = (jnp.zeros(w_qkv.shape, jnp.float32), jnp.zeros(w_out.shape, jnp.float32))
    totals, ignored = lax.scan(per_batch, initial, (nodes, cotangent, tile_lists, counts, virtual))
    return (totals[0].astype(jnp.bfloat16), totals[1].astype(jnp.bfloat16))
```

```python
import functools

import jax
import jax.numpy as jnp
from jax import lax
from jax.experimental import pallas as pl
from jax.experimental.pallas import tpu as pltpu
from jax.sharding import Mesh
from jax.sharding import PartitionSpec as P

HEADS = 4
EPSILON = 1e-06
TEMPER = 4.0
D = 512
INNER = 256
ROWS = 128
HEAD = INNER // HEADS
SCALE = TEMPER / HEAD
STAGE_LAYERS = 4
GROUP = ("yl", "xl")
STASH = ("normed", "inverse", "qkv", "scales", "attn", "mixed")
F32 = jnp.float32
BF16 = jnp.bfloat16


def stash_shapes():
    return {
        "normed": ((STAGE_LAYERS, ROWS, D), BF16),
        "inverse": ((STAGE_LAYERS, ROWS, 1), F32),
        "qkv": ((STAGE_LAYERS, 3, ROWS, INNER), BF16),
        "scales": ((STAGE_LAYERS, 2, ROWS, INNER), F32),
        "attn": ((STAGE_LAYERS, HEADS * ROWS, ROWS), BF16),
        "mixed": ((STAGE_LAYERS, ROWS, INNER), BF16),
    }


def dot(a, b, over_a=1, over_b=0):
    return lax.dot_general(a, b, (((over_a,), (over_b,)), ((), ())), preferred_element_type=F32)


def head_masks():
    lane = lax.broadcasted_iota(jnp.int32, (1, INNER), 1)
    return [jnp.where(lane // HEAD == h, 1.0, 0.0).astype(F32) for h in range(HEADS)]


def head_mean_matrix():
    row = lax.broadcasted_iota(jnp.int32, (INNER, INNER), 0) // HEAD
    col = lax.broadcasted_iota(jnp.int32, (INNER, INNER), 1) // HEAD
    return jnp.where(row == col, 1.0 / HEAD, 0.0).astype(BF16)


def spread(values, masks):
    return jnp.concatenate([values * m.astype(values.dtype) for m in masks], axis=0)


def gathered(stacked, masks):
    total = stacked[:ROWS] * masks[0]
    for h in range(1, HEADS):
        total = total + stacked[h * ROWS : (h + 1) * ROWS] * masks[h]
    return total


def multiplicities(batch, tile_lists, counts, virtual):
    def times(tile, key_tile):
        seen = (virtual[batch] == key_tile).astype(F32)
        for slot in range(2):
            named = tile_lists[batch, tile, slot] == key_tile
            seen = seen + (named & (slot < counts[batch, tile])).astype(F32)
        return seen

    row = lax.broadcasted_iota(jnp.int32, (ROWS, ROWS), 0) < ROWS // 2
    col = lax.broadcasted_iota(jnp.int32, (ROWS, ROWS), 1) < ROWS // 2
    one = jnp.where(
        row,
        jnp.where(col, times(0, 0), times(0, 1)),
        jnp.where(col, times(1, 0), times(1, 1)),
    )
    return jnp.concatenate([one] * HEADS, axis=0)


def forward_layer(layer, hidden, weight, times, masks, mean_matrix, stash):
    widened = hidden.astype(F32)
    inverse = lax.rsqrt(jnp.mean(widened * widened, axis=-1, keepdims=True) + EPSILON)
    normed = (widened * inverse).astype(BF16)
    q = dot(normed, weight(0))
    k = dot(normed, weight(1))
    v = dot(normed, weight(2)).astype(BF16)
    scale_q = lax.rsqrt(dot((q * q).astype(BF16), mean_matrix) + EPSILON) * SCALE
    scale_k = lax.rsqrt(dot((k * k).astype(BF16), mean_matrix) + EPSILON)
    qn = (q * scale_q).astype(BF16)
    kn = (k * scale_k).astype(BF16)
    scores = dot(spread(qn, masks), kn, 1, 1)
    exponent = jnp.exp(scores) * times
    attn = (exponent * (1.0 / jnp.sum(exponent, axis=-1, keepdims=True))).astype(BF16)
    mixed = gathered(dot(attn, v), masks).astype(BF16)
    stash["normed"][layer] = normed
    stash["inverse"][layer] = inverse
    stash["qkv"][layer, 0] = qn
    stash["qkv"][layer, 1] = kn
    stash["qkv"][layer, 2] = v
    stash["scales"][layer, 0] = scale_q
    stash["scales"][layer, 1] = scale_k
    stash["attn"][layer] = attn
    stash["mixed"][layer] = mixed
    out = weight(3)
    added = jnp.concatenate([dot(mixed, out[:INNER]), dot(mixed, out[INNER:])], axis=1)
    return (widened + added).astype(BF16)


def backward_layer(layer, grad, weight, masks, mean_matrix, stash, put):
    normed = stash["normed"][layer]
    inverse = stash["inverse"][layer]
    qn = stash["qkv"][layer, 0]
    kn = stash["qkv"][layer, 1]
    v = stash["qkv"][layer, 2]
    attn = stash["attn"][layer]
    mixed = stash["mixed"][layer]
    out = weight(3)
    low, high = grad[:, :INNER], grad[:, INNER:]
    grad_mixed = (dot(low, out[:INNER], 1, 1) + dot(high, out[INNER:], 1, 1)).astype(BF16)
    stacked = spread(grad_mixed, masks)
    grad_attn = dot(stacked, v, 1, 1)
    attn_wide = attn.astype(F32)
    inner = jnp.sum(attn_wide * grad_attn, axis=-1, keepdims=True)
    grad_scores = (attn_wide * (grad_attn - inner)).astype(BF16)
    grad_v = dot(attn, stacked, 0, 0).astype(BF16)
    grad_qn = gathered(dot(grad_scores, kn), masks)
    grad_kn = dot(grad_scores, spread(qn, masks), 0, 0)
    qw, kw = qn.astype(F32), kn.astype(F32)
    mean_q = dot((grad_qn * qw).astype(BF16), mean_matrix) * (1.0 / (SCALE * SCALE))
    mean_k = dot((grad_kn * kw).astype(BF16), mean_matrix)
    grad_q = (stash["scales"][layer, 0] * (grad_qn - qw * mean_q)).astype(BF16)
    grad_k = (stash["scales"][layer, 1] * (grad_kn - kw * mean_k)).astype(BF16)
    grad_normed = dot(grad_q, weight(0), 1, 1) + dot(grad_k, weight(1), 1, 1) + dot(grad_v, weight(2), 1, 1)
    wide = normed.astype(F32)
    mean = jnp.mean(grad_normed * wide, axis=-1, keepdims=True)
    result = (grad.astype(F32) + inverse * (grad_normed - wide * mean)).astype(BF16)
    put(0, dot(normed, grad_q, 0, 0).astype(BF16))
    put(1, dot(normed, grad_k, 0, 0).astype(BF16))
    put(2, dot(normed, grad_v, 0, 0).astype(BF16))
    put(3, jnp.concatenate([dot(mixed, low, 0, 0), dot(mixed, high, 0, 0)], axis=0).astype(BF16))
    return result


class Weights:
    def __init__(self, own, near, far, place, sems, me, core):
        self.place, self.me = place, me
        self.copies = []
        for r in range(STAGE_LAYERS):
            pair = []
            for side in range(2):
                if r == 0:
                    source, half = own.at[pl.ds(2 * side, 2)], side
                else:
                    source = near[r - 1] if side == 0 else far[r - 1]
                    half = core if side == 0 else 1 - core
                pair.append(pltpu.make_async_copy(source, place.at[r, half], sems.at[r, side]))
            self.copies.append(pair)

    def start(self):
        for pair in self.copies:
            for copy in pair:
                copy.start()

    def wait(self):
        for pair in self.copies:
            for copy in pair:
                copy.wait()

    def layer(self, index):
        r = index ^ self.me
        return lambda block: self.place[r, block // 2, block % 2]


class Gradients:
    def __init__(self, keep, send, place, sems, core):
        self.place, self.core, self.sems, self.outs = place, core, sems, (keep, send)
        self.copies = []

    def put(self, layer):
        def store(block, value):
            self.place[(block // 2) ^ self.core, layer, block % 2] = value

        return store

    def sent(self, layer):
        for side in range(2):
            copy = pltpu.make_async_copy(
                self.place.at[side, layer], self.outs[side].at[layer], self.sems.at[side, layer]
            )
            copy.start()
            self.copies.append(copy)

    def wait(self):
        for copy in self.copies:
            copy.wait()


def forward_kernel(info, tile_lists, counts, virtual, hidden_in, own, n1, n2, n3, f1, f2, f3, hidden_out, *rest):
    stash = dict(zip(STASH, rest[: len(STASH)]))
    place, sems = rest[len(STASH) :]
    batch, me, core = info[0], info[1], info[2]
    weights = Weights(own, (n1, n2, n3), (f1, f2, f3), place, sems, me, core)
    weights.start()
    masks, mean_matrix = head_masks(), head_mean_matrix()
    times = multiplicities(batch, tile_lists, counts, virtual)
    weights.wait()
    hidden = hidden_in[0]
    for layer in range(STAGE_LAYERS):
        hidden = forward_layer(layer, hidden, weights.layer(layer), times, masks, mean_matrix, stash)
    hidden_out[...] = hidden


def both_kernel(info, tile_lists, counts, virtual, hidden_in, grad_in, own, n1, n2, n3, f1, f2, f3, grad_out, keep, send, *rest):
    stash = dict(zip(STASH, rest[: len(STASH)]))
    place, sems, grads_place, grads_sems = rest[len(STASH) :]
    batch, me, core = info[0], info[1], info[2]
    weights = Weights(own, (n1, n2, n3), (f1, f2, f3), place, sems, me, core)
    weights.start()
    masks, mean_matrix = head_masks(), head_mean_matrix()
    times = multiplicities(batch, tile_lists, counts, virtual)
    grads = Gradients(keep, send, grads_place, grads_sems, core)
    weights.wait()
    hidden = hidden_in[...]
    for layer in range(STAGE_LAYERS):
        hidden = forward_layer(layer, hidden, weights.layer(layer), times, masks, mean_matrix, stash)
    grad = grad_in[0]
    for layer in reversed(range(STAGE_LAYERS)):
        grad = backward_layer(layer, grad, weights.layer(layer), masks, mean_matrix, stash, grads.put(layer))
        grads.sent(layer)
    grad_out[...] = grad
    grads.wait()


def backward_kernel(info, grad_in, *rest):
    stash = dict(zip(STASH, rest[: len(STASH)]))
    own, n1, n2, n3, f1, f2, f3, keep, send, place, sems, grads_place, grads_sems = rest[len(STASH) :]
    me, core = info[1], info[2]
    weights = Weights(own, (n1, n2, n3), (f1, f2, f3), place, sems, me, core)
    weights.start()
    masks, mean_matrix = head_masks(), head_mean_matrix()
    grads = Gradients(keep, send, grads_place, grads_sems, core)
    weights.wait()
    grad = grad_in[...]
    for layer in reversed(range(STAGE_LAYERS)):
        grad = backward_layer(layer, grad, weights.layer(layer), masks, mean_matrix, stash, grads.put(layer))
        grads.sent(layer)
    grads.wait()


def whole(shape):
    return pl.BlockSpec(shape, lambda *_: (0,) * len(shape))


def batch_block():
    return pl.BlockSpec((1, ROWS, D), lambda step, info, *_: (info[0], 0, 0))


ANYWHERE = pl.BlockSpec(memory_space=pl.ANY)
WEIGHT_SCRATCH = [
    pltpu.VMEM((STAGE_LAYERS, 2, 2, D, INNER), BF16),
    pltpu.SemaphoreType.DMA((STAGE_LAYERS, 2)),
]
GRAD_SCRATCH = [
    pltpu.VMEM((2, STAGE_LAYERS, 2, D, INNER), BF16),
    pltpu.SemaphoreType.DMA((2, STAGE_LAYERS)),
]
GRAD_HALF = jax.ShapeDtypeStruct((STAGE_LAYERS, 2, D, INNER), BF16)
HIDDEN = jax.ShapeDtypeStruct((ROWS, D), BF16)


def call(kernel, prefetched, in_specs, out_specs, out_shape, scratch, args):
    return pl.pallas_call(
        kernel,
        grid_spec=pltpu.PrefetchScalarGridSpec(
            num_scalar_prefetch=prefetched,
            grid=(1,),
            in_specs=in_specs,
            out_specs=out_specs,
            scratch_shapes=scratch,
        ),
        out_shape=out_shape,
        compiler_params=pltpu.CompilerParams(vmem_limit_bytes=48 * 2**20),
    )(*args)


def run_forward(info, tables, nodes, weights):
    shapes = stash_shapes()
    return call(
        forward_kernel,
        4,
        [batch_block()] + [ANYWHERE] * 7,
        [whole((ROWS, D))] + [whole(shapes[n][0]) for n in STASH],
        [HIDDEN] + [jax.ShapeDtypeStruct(*shapes[n]) for n in STASH],
        WEIGHT_SCRATCH,
        (info, *tables, nodes, *weights),
    )


def run_both(info, tables, hidden, cotangent, weights):
    shapes = stash_shapes()
    return call(
        both_kernel,
        4,
        [whole((ROWS, D)), batch_block()] + [ANYWHERE] * 7,
        [whole((ROWS, D)), ANYWHERE, ANYWHERE],
        [HIDDEN, GRAD_HALF, GRAD_HALF],
        [pltpu.VMEM(*shapes[n]) for n in STASH] + WEIGHT_SCRATCH + GRAD_SCRATCH,
        (info, *tables, hidden, cotangent, *weights),
    )


def run_backward(info, grad, stash, weights):
    shapes = stash_shapes()
    return call(
        backward_kernel,
        1,
        [whole((ROWS, D))] + [whole(shapes[n][0]) for n in STASH] + [ANYWHERE] * 7,
        [ANYWHERE, ANYWHERE],
        [GRAD_HALF, GRAD_HALF],
        WEIGHT_SCRATCH + GRAD_SCRATCH,
        (info, grad, *stash, *weights),
    )


def swapped(value, axis):
    return lax.ppermute(value, axis, [(0, 1), (1, 0)])


def fetched(half, flip_y, flip_x):
    axes = ("yl", "xl", "xh", "core")
    pairs = []
    for y in range(2):
        for x in range(2):
            for upper in range(2):
                for core in range(2):
                    there = upper ^ (core if flip_x else 0)
                    source = ((y * 2 + x) * 2 + upper) * 2 + core
                    target = (((y ^ flip_y) * 2 + (x ^ flip_x)) * 2 + there) * 2 + core
                    pairs.append((source, target))
    return lax.ppermute(half, axes, pairs)


def per_device(nodes, cotangent, w_qkv, w_out, tile_lists, counts, virtual):
    stage = lax.axis_index("yh")
    y, x, core = lax.axis_index("yl"), lax.axis_index("xl"), lax.axis_index("core")
    me = y * 2 + x
    batch = jnp.where(stage == 0, y, 1 - y) * 2 + x
    info = jnp.stack([batch, me, core]).astype(jnp.int32)
    tables = (tile_lists, counts, virtual)
    qkv, out = w_qkv[0], w_out[0]
    blocks = [qkv[:, i * INNER : (i + 1) * INNER] for i in range(3)]
    blocks.append(jnp.concatenate([out[:, :INNER], out[:, INNER:]], axis=0))
    own = jnp.stack(blocks)
    half = jnp.where(core == 0, own[:2], own[2:])
    near3 = fetched(half, 1, 1)
    near2 = fetched(half, 1, 0)
    near1 = fetched(half, 0, 1)
    near = (near1, near2, near3)
    far = tuple(swapped(value, "core") for value in near)
    weights = (own, *near, *far)

    hidden, *stash = run_forward(info, tables, nodes, weights)
    across = [(0, 3), (1, 2), (2, 1), (3, 0)]
    hidden = lax.ppermute(hidden, ("yh", "yl"), across)

    empty = jnp.zeros((STAGE_LAYERS, 2, D, INNER), BF16)
    grad, keep, send = lax.cond(
        stage == 1,
        lambda: tuple(run_both(info, tables, hidden, cotangent, weights)),
        lambda: (jnp.zeros((ROWS, D), BF16), empty, empty),
    )
    grad = lax.ppermute(grad, ("yh", "yl"), across)
    keep, send = lax.cond(
        stage == 0,
        lambda: tuple(run_backward(info, grad, stash, weights)),
        lambda: (keep, send),
    )

    def added(value, axis):
        return jnp.sum(value.astype(F32), axis=axis).astype(BF16)

    depth = lax.axis_size("z")
    total = (keep.astype(F32) + swapped(send, "core").astype(F32)).astype(BF16)
    total = lax.all_to_all(total.reshape(8, D, INNER), ("yl", "xl", "xh"), 0, 0, tiled=True)
    total = added(total, 0).reshape(depth, D // depth, INNER)
    total = added(lax.all_to_all(total, "z", 0, 0, tiled=True), 0)
    total = lax.all_to_all(jnp.broadcast_to(total, (depth, *total.shape)), "z", 0, 0, tiled=True)
    total = jnp.broadcast_to(total.reshape(1, D, INNER), (4, D, INNER))
    total = lax.all_to_all(total, ("core", "xh"), 0, 0, tiled=True)
    grad_qkv = jnp.concatenate([total[0], total[1], total[2]], axis=1)
    grad_out = jnp.concatenate([total[3, :INNER], total[3, INNER:]], axis=1)
    return (grad_qkv[None], grad_out[None])


def solution(mesh):
    depth = mesh.shape["dp"] // 4
    names = ("yh", "yl", "xl", "z", "xh", "core")
    cut = Mesh(mesh.devices.reshape(2, 2, 2, depth, 2, 2), names)
    section, dp = P(("yh", "yl", "xl")), P(("z", "xh", "core"))
    return jax.shard_map(
        per_device,
        mesh=cut,
        in_specs=(dp, dp, section, section, dp, dp, dp),
        out_specs=(section, section),
        check_vma=False,
    )
```

```python
import jax
import jax.numpy as jnp
from jax import lax
from jax.experimental import pallas as pl
from jax.experimental.pallas import tpu as pltpu
from jax.sharding import Mesh
from jax.sharding import PartitionSpec as P

HEADS = 4
EPSILON = 1e-06
TEMPER = 4.0
D = 512
INNER = 256
ROWS = 128
HEAD = INNER // HEADS
SCALE = TEMPER / HEAD
STAGE_LAYERS = 4
F32 = jnp.float32
BF16 = jnp.bfloat16
STASH = {
    "normed": ((ROWS, D), BF16),
    "inverse": ((ROWS, ROWS), F32),
    "qkv": ((3, ROWS, INNER), BF16),
    "scales": ((2, ROWS, INNER), F32),
    "attn": ((HEADS * ROWS, ROWS), BF16),
    "mixed": ((ROWS, INNER), BF16),
}
TERMS = {
    "normed": ((ROWS, D), BF16),
    "mixed": ((ROWS, INNER), BF16),
    "grad_qkv": ((ROWS, 3 * INNER), BF16),
    "grad_out": ((ROWS, D), BF16),
}


def dot(a, b, over_a=1, over_b=0):
    return lax.dot_general(a, b, (((over_a,), (over_b,)), ((), ())), preferred_element_type=F32)


def head_masks():
    lane = lax.broadcasted_iota(jnp.int32, (1, INNER), 1)
    return [jnp.where(lane // HEAD == h, 1.0, 0.0).astype(F32) for h in range(HEADS)]


def head_mean_matrix():
    row = lax.broadcasted_iota(jnp.int32, (INNER, INNER), 0) // HEAD
    col = lax.broadcasted_iota(jnp.int32, (INNER, INNER), 1) // HEAD
    return jnp.where(row == col, 1.0 / HEAD, 0.0).astype(BF16)


def spread(values, masks):
    return jnp.concatenate([values * m.astype(values.dtype) for m in masks], axis=0)


def gathered(stacked, masks):
    total = stacked[:ROWS] * masks[0]
    for h in range(1, HEADS):
        total = total + stacked[h * ROWS : (h + 1) * ROWS] * masks[h]
    return total


def multiplicities(batch, tile_lists, counts, virtual):
    def times(tile, key_tile):
        seen = (virtual[batch] == key_tile).astype(F32)
        for slot in range(2):
            named = tile_lists[batch, tile, slot] == key_tile
            seen = seen + (named & (slot < counts[batch, tile])).astype(F32)
        return seen

    row = lax.broadcasted_iota(jnp.int32, (ROWS, ROWS), 0) < ROWS // 2
    col = lax.broadcasted_iota(jnp.int32, (ROWS, ROWS), 1) < ROWS // 2
    one = jnp.where(
        row,
        jnp.where(col, times(0, 0), times(0, 1)),
        jnp.where(col, times(1, 0), times(1, 1)),
    )
    return jnp.concatenate([one] * HEADS, axis=0)


def forward_layer(layer, hidden, weight, times, masks, mean_matrix, stash):
    widened = hidden.astype(F32)
    inverse = lax.rsqrt(jnp.mean(widened * widened, axis=-1, keepdims=True) + EPSILON)
    normed = (widened * inverse).astype(BF16)
    q = dot(normed, weight(0))
    k = dot(normed, weight(1))
    v = dot(normed, weight(2)).astype(BF16)
    scale_q = lax.rsqrt(dot((q * q).astype(BF16), mean_matrix) + EPSILON) * SCALE
    scale_k = lax.rsqrt(dot((k * k).astype(BF16), mean_matrix) + EPSILON)
    qn = (q * scale_q).astype(BF16)
    kn = (k * scale_k).astype(BF16)
    scores = dot(spread(qn, masks), kn, 1, 1)
    exponent = jnp.exp(scores) * times
    attn = (exponent * (1.0 / jnp.sum(exponent, axis=-1, keepdims=True))).astype(BF16)
    mixed = gathered(dot(attn, v), masks).astype(BF16)
    stash["normed"][layer] = normed
    stash["inverse"][layer] = jnp.broadcast_to(inverse, (ROWS, ROWS))
    stash["qkv"][layer, 0] = qn
    stash["qkv"][layer, 1] = kn
    stash["qkv"][layer, 2] = v
    stash["scales"][layer, 0] = scale_q
    stash["scales"][layer, 1] = scale_k
    stash["attn"][layer] = attn
    stash["mixed"][layer] = mixed
    out = weight(3)
    added = jnp.concatenate([dot(mixed, out[:INNER]), dot(mixed, out[INNER:])], axis=1)
    return (widened + added).astype(BF16)


def backward_layer(layer, grad, weight, masks, mean_matrix, stash):
    inverse = stash["inverse"][layer][:, :1]
    qn = stash["qkv"][layer, 0]
    kn = stash["qkv"][layer, 1]
    v = stash["qkv"][layer, 2]
    attn = stash["attn"][layer]
    out = weight(3)
    low, high = grad[:, :INNER], grad[:, INNER:]
    grad_mixed = (dot(low, out[:INNER], 1, 1) + dot(high, out[INNER:], 1, 1)).astype(BF16)
    stacked = spread(grad_mixed, masks)
    grad_attn = dot(stacked, v, 1, 1)
    attn_wide = attn.astype(F32)
    inner = jnp.sum(attn_wide * grad_attn, axis=-1, keepdims=True)
    grad_scores = (attn_wide * (grad_attn - inner)).astype(BF16)
    grad_v = dot(attn, stacked, 0, 0).astype(BF16)
    grad_qn = gathered(dot(grad_scores, kn), masks)
    grad_kn = dot(grad_scores, spread(qn, masks), 0, 0)
    qw, kw = qn.astype(F32), kn.astype(F32)
    mean_q = dot((grad_qn * qw).astype(BF16), mean_matrix) * (1.0 / (SCALE * SCALE))
    mean_k = dot((grad_kn * kw).astype(BF16), mean_matrix)
    grad_q = (stash["scales"][layer, 0] * (grad_qn - qw * mean_q)).astype(BF16)
    grad_k = (stash["scales"][layer, 1] * (grad_kn - kw * mean_k)).astype(BF16)
    grad_normed = dot(grad_q, weight(0), 1, 1) + dot(grad_k, weight(1), 1, 1) + dot(grad_v, weight(2), 1, 1)
    wide = stash["normed"][layer].astype(F32)
    mean = jnp.mean(grad_normed * wide, axis=-1, keepdims=True)
    result = (grad.astype(F32) + inverse * (grad_normed - wide * mean)).astype(BF16)
    return result, jnp.concatenate([grad_q, grad_k, grad_v], axis=1)


class Weights:
    def __init__(self, own, beside, near2, far2, near3, far3, place, sems, me, core, order):
        self.place, self.me, self.order = place, me, order

        def halves(r, near, far):
            return [(near, place.at[r, pl.ds(2 * core, 2)]), (far, place.at[r, pl.ds(2 * (1 - core), 2)])]

        pairs = [
            [(own, place.at[0])],
            [(beside, place.at[1])],
            halves(2, near2, far2),
            halves(3, near3, far3),
        ]
        self.copies = [
            [pltpu.make_async_copy(src, dst, sems.at[r, i]) for i, (src, dst) in enumerate(listed)]
            for r, listed in enumerate(pairs)
        ]

    def each(self, layer, act):
        for r in range(STAGE_LAYERS):

            @pl.when((layer ^ self.me) == r)
            def _(r=r):
                for copy in self.copies[r]:
                    act(copy)

    def start(self):
        for layer in self.order:
            self.each(layer, lambda copy: copy.start())

    def wait(self, layer):
        self.each(layer, lambda copy: copy.wait())

    def layer(self, index):
        r = index ^ self.me
        return lambda block: self.place[r, block]


class Sheets:
    def __init__(self, names, outside, inside, sems, inward):
        self.copies = []
        for layer in range(STAGE_LAYERS):
            listed = []
            for i in range(len(names)):
                a, b = outside[i].at[layer], inside[i].at[layer]
                listed.append(pltpu.make_async_copy(*((a, b) if inward else (b, a)), sems.at[i, layer]))
            self.copies.append(listed)
        self.refs = dict(zip(names, inside))

    def start(self, layer):
        for copy in self.copies[layer]:
            copy.start()

    def wait(self, layer):
        for copy in self.copies[layer]:
            copy.wait()


def weight_gradients(layer, normed, mixed, grad_qkv, grad_out, place, core):
    full = dot(normed, grad_qkv, 0, 0).astype(BF16)
    for block in range(3):
        place[(block // 2) ^ core, layer, block % 2] = full[:, block * INNER : (block + 1) * INNER]
    last = dot(mixed, grad_out, 0, 0).astype(BF16)
    place[1 ^ core, layer, 1, :INNER] = last[:, :INNER]
    place[1 ^ core, layer, 1, INNER:] = last[:, INNER:]


def pack_kernel(info, qkv, out, own, half, sems):
    blocks = [[(qkv.at[0, :, pl.ds(b * INNER, INNER)], slice(None))] for b in range(3)]
    blocks.append([(out.at[0, :, pl.ds(i * INNER, INNER)], pl.ds(i * INNER, INNER)) for i in range(2)])
    copies = []
    for block in range(4):
        for i, (source, rows) in enumerate(blocks[block]):
            copies.append(pltpu.make_async_copy(source, own.at[block, rows], sems.at[0, block + i]))
    for copy in copies:
        copy.start()
    for side in range(2):

        @pl.when(info[2] == side)
        def _(side=side):
            chosen = []
            for slot in range(2):
                for i, (source, rows) in enumerate(blocks[2 * side + slot]):
                    chosen.append(pltpu.make_async_copy(source, half.at[slot, rows], sems.at[1, slot + i]))
            for copy in chosen:
                copy.start()
            for copy in chosen:
                copy.wait()

    for copy in copies:
        copy.wait()


def forward_kernel(info, tile_lists, counts, virtual, hidden_in, *rest):
    weights = Weights(*rest[:6], *rest[-4:-2], info[1], info[2], range(STAGE_LAYERS))
    hidden_out, outside, inside = rest[6], rest[7 : 7 + len(STASH)], rest[7 + len(STASH) : 7 + 2 * len(STASH)]
    sheets = Sheets(STASH, outside, inside, rest[-2], False)
    weights.start()
    masks, mean_matrix = head_masks(), head_mean_matrix()
    times = rest[-1]
    times[...] = multiplicities(info[0], tile_lists, counts, virtual)
    hidden = hidden_in[0]
    for layer in range(STAGE_LAYERS):
        weights.wait(layer)
        hidden = forward_layer(layer, hidden, weights.layer(layer), times[...], masks, mean_matrix, sheets.refs)
        sheets.start(layer)
    hidden_out[...] = hidden
    for layer in range(STAGE_LAYERS):
        sheets.wait(layer)


def chain_kernel(info, tile_lists, counts, virtual, hidden_in, grad_in, *rest):
    weights = Weights(*rest[:6], *rest[-4:-2], info[1], info[2], range(STAGE_LAYERS))
    grad_out, outside = rest[6], rest[7 : 7 + len(TERMS)]
    stash = dict(zip(STASH, rest[7 + len(TERMS) :][: len(STASH)]))
    extra = rest[7 + len(TERMS) + len(STASH) :][:2]
    sheets = Sheets(TERMS, outside, (stash["normed"], stash["mixed"], *extra), rest[-2], False)
    weights.start()
    masks, mean_matrix = head_masks(), head_mean_matrix()
    times = rest[-1]
    times[...] = multiplicities(info[0], tile_lists, counts, virtual)
    hidden = hidden_in[...]
    for layer in range(STAGE_LAYERS):
        weights.wait(layer)
        hidden = forward_layer(layer, hidden, weights.layer(layer), times[...], masks, mean_matrix, stash)
    grad = grad_in[0]
    for layer in reversed(range(STAGE_LAYERS)):
        sheets.refs["grad_out"][layer] = grad
        grad, grad_qkv = backward_layer(layer, grad, weights.layer(layer), masks, mean_matrix, stash)
        sheets.refs["grad_qkv"][layer] = grad_qkv
        sheets.start(layer)
    grad_out[...] = grad
    for layer in range(STAGE_LAYERS):
        sheets.wait(layer)


def gradient_kernel(info, *rest):
    outside, (keep, send), inside = rest[: len(TERMS)], rest[len(TERMS) :][:2], rest[len(TERMS) + 2 : -3]
    place, in_sems, out_sems = rest[-3:]
    sheets = Sheets(TERMS, outside, inside, in_sems, True)
    results = Sheets(("keep", "send"), (keep, send), (place.at[0], place.at[1]), out_sems, False)
    for layer in range(STAGE_LAYERS):
        sheets.start(layer)
    for layer in range(STAGE_LAYERS):
        sheets.wait(layer)
        weight_gradients(layer, *(sheets.refs[n][layer] for n in TERMS), place, info[2])
        results.start(layer)
    for layer in range(STAGE_LAYERS):
        results.wait(layer)


def backward_kernel(info, grad_in, *rest):
    order = tuple(reversed(range(STAGE_LAYERS)))
    count = len(STASH)
    outside, given, (keep, send) = rest[:count], rest[count:][:6], rest[count + 6 :][:2]
    inside = rest[count + 8 :][:count]
    weight_place, weight_sems, place, in_sems, out_sems = rest[-5:]
    weights = Weights(*given, weight_place, weight_sems, info[1], info[2], order)
    sheets = Sheets(STASH, outside, inside, in_sems, True)
    results = Sheets(("keep", "send"), (keep, send), (place.at[0], place.at[1]), out_sems, False)
    for layer in order:
        sheets.start(layer)
        weights.each(layer, lambda copy: copy.start())
    masks, mean_matrix = head_masks(), head_mean_matrix()
    grad = grad_in[...]
    for layer in order:
        sheets.wait(layer)
        weights.wait(layer)
        before = grad
        grad, grad_qkv = backward_layer(layer, grad, weights.layer(layer), masks, mean_matrix, sheets.refs)
        weight_gradients(
            layer, sheets.refs["normed"][layer], sheets.refs["mixed"][layer], grad_qkv, before, place, info[2]
        )
        results.start(layer)
    for layer in order:
        results.wait(layer)


ANYWHERE = pl.BlockSpec(memory_space=pl.ANY)
HIDDEN = jax.ShapeDtypeStruct((ROWS, D), BF16)
HIDDEN_BLOCK = pl.BlockSpec((ROWS, D), lambda *_: (0, 0))
BATCH_BLOCK = pl.BlockSpec((1, ROWS, D), lambda step, info, *_: (info[0], 0, 0))
GRAD_HALF = jax.ShapeDtypeStruct((STAGE_LAYERS, 2, D, INNER), BF16)
WEIGHT_SCRATCH = [
    pltpu.VMEM((STAGE_LAYERS, 4, D, INNER), BF16),
    pltpu.SemaphoreType.DMA((STAGE_LAYERS, 2)),
]
GRAD_PLACE = pltpu.VMEM((2, STAGE_LAYERS, 2, D, INNER), BF16)
TIMES = pltpu.VMEM((HEADS * ROWS, ROWS), F32)


def layered(sizes, make):
    return [make((STAGE_LAYERS, *shape), kind) for shape, kind in sizes.values()]


def semaphores(count):
    return pltpu.SemaphoreType.DMA((count, STAGE_LAYERS))


def call(kernel, prefetched, in_specs, out_specs, out_shape, scratch, args):
    return pl.pallas_call(
        kernel,
        grid_spec=pltpu.PrefetchScalarGridSpec(
            num_scalar_prefetch=prefetched,
            grid=(1,),
            in_specs=in_specs,
            out_specs=out_specs,
            scratch_shapes=scratch,
        ),
        out_shape=out_shape,
        compiler_params=pltpu.CompilerParams(vmem_limit_bytes=48 * 2**20),
    )(*args)


def run_pack(info, w_qkv, w_out):
    shapes = [jax.ShapeDtypeStruct((blocks, D, INNER), BF16) for blocks in (4, 2)]
    sems = [pltpu.SemaphoreType.DMA((2, 5))]
    return call(pack_kernel, 1, [ANYWHERE] * 2, [ANYWHERE] * 2, shapes, sems, (info, w_qkv, w_out))


def run_forward(info, tables, nodes, weights):
    return call(
        forward_kernel,
        4,
        [BATCH_BLOCK] + [ANYWHERE] * 6,
        [HIDDEN_BLOCK] + [ANYWHERE] * len(STASH),
        [HIDDEN] + layered(STASH, jax.ShapeDtypeStruct),
        layered(STASH, pltpu.VMEM) + WEIGHT_SCRATCH + [semaphores(len(STASH)), TIMES],
        (info, *tables, nodes, *weights),
    )


def run_chain(info, tables, hidden, cotangent, weights):
    return call(
        chain_kernel,
        4,
        [HIDDEN_BLOCK, BATCH_BLOCK] + [ANYWHERE] * 6,
        [HIDDEN_BLOCK] + [ANYWHERE] * len(TERMS),
        [HIDDEN] + layered(TERMS, jax.ShapeDtypeStruct),
        layered(STASH, pltpu.VMEM) + layered(TERMS, pltpu.VMEM)[2:] + WEIGHT_SCRATCH + [semaphores(len(TERMS)), TIMES],
        (info, *tables, hidden, cotangent, *weights),
    )


def run_gradients(info, terms):
    return call(
        gradient_kernel,
        1,
        [ANYWHERE] * len(TERMS),
        [ANYWHERE] * 2,
        [GRAD_HALF] * 2,
        layered(TERMS, pltpu.VMEM) + [GRAD_PLACE, semaphores(len(TERMS)), semaphores(2)],
        (info, *terms),
    )


def run_backward(info, grad, stash, weights):
    return call(
        backward_kernel,
        1,
        [HIDDEN_BLOCK] + [ANYWHERE] * (len(STASH) + 6),
        [ANYWHERE] * 2,
        [GRAD_HALF] * 2,
        layered(STASH, pltpu.VMEM) + WEIGHT_SCRATCH + [GRAD_PLACE, semaphores(len(STASH)), semaphores(2)],
        (info, grad, *stash, *weights),
    )


def swapped(value, axis):
    return lax.ppermute(value, axis, [(0, 1), (1, 0)])


def fetched(value, flip_y, flip_x):
    axes = ("yl", "xl", "xh", "core")
    pairs = []
    for y in range(2):
        for x in range(2):
            for upper in range(2):
                for core in range(2):
                    there = upper ^ (core if flip_x else 0)
                    source = ((y * 2 + x) * 2 + upper) * 2 + core
                    target = (((y ^ flip_y) * 2 + (x ^ flip_x)) * 2 + there) * 2 + core
                    pairs.append((source, target))
    return lax.ppermute(value, axes, pairs)


def per_device(nodes, cotangent, w_qkv, w_out, tile_lists, counts, virtual):
    stage = lax.axis_index("yh")
    y, x, core = lax.axis_index("yl"), lax.axis_index("xl"), lax.axis_index("core")
    me = y * 2 + x
    batch = jnp.where(stage == 0, y, 1 - y) * 2 + x
    info = jnp.stack([batch, me, core]).astype(jnp.int32)
    tables = (tile_lists, counts, virtual)
    own, half = run_pack(info, w_qkv, w_out)
    near2 = fetched(half, 1, 0)
    near3 = fetched(half, 1, 1)
    beside = fetched(own, 0, 1)
    far2, far3 = swapped(near2, "core"), swapped(near3, "core")
    weights = (own, beside, near2, far2, near3, far3)

    hidden, *stash = run_forward(info, tables, nodes, weights)
    across = [(0, 3), (1, 2), (2, 1), (3, 0)]
    hidden = lax.ppermute(hidden, ("yh", "yl"), across)
    grad, *terms = run_chain(info, tables, hidden, cotangent, weights)
    grad = lax.ppermute(grad, ("yh", "yl"), across)
    keep, send = lax.cond(
        stage == 0,
        lambda: tuple(run_backward(info, grad, stash, weights)),
        lambda: tuple(run_gradients(info, terms)),
    )

    def added(value, axis):
        return jnp.sum(value.astype(F32), axis=axis).astype(BF16)

    def repeated(value, times):
        return jnp.broadcast_to(value, (times, *value.shape))

    far, near = lax.axis_size("zh"), lax.axis_size("zl")
    piece = D // (far * near)
    total = (keep.astype(F32) + swapped(send, "core").astype(F32)).astype(BF16)
    total = lax.all_to_all(total.reshape(8, D, INNER), ("yl", "xl", "xh"), 0, 0, tiled=True)
    total = added(total, 0).reshape(far * near, piece, INNER)
    total = added(lax.all_to_all(total, ("zl", "zh"), 0, 0, tiled=True), 0)
    total = lax.all_to_all(repeated(total, far), "zh", 0, 0, tiled=True)
    total = lax.all_to_all(repeated(total, 2 * near), ("xh", "zl"), 0, 0, tiled=True)
    mine = total.reshape(2, D, INNER)
    other = swapped(mine, "core")
    first, second = jnp.where(core == 0, mine, other), jnp.where(core == 0, other, mine)
    grad_qkv = jnp.concatenate([first[0], first[1], second[0]], axis=1)
    grad_out = jnp.concatenate([second[1, :INNER], second[1, INNER:]], axis=1)
    return (grad_qkv[None], grad_out[None])


def solution(mesh):
    depth = mesh.shape["dp"] // 4
    near = min(depth, 4)
    names = ("yh", "yl", "xl", "zh", "zl", "xh", "core")
    cut = Mesh(mesh.devices.reshape(2, 2, 2, depth // near, near, 2, 2), names)
    section, dp = P(("yh", "yl", "xl")), P(("zh", "zl", "xh", "core"))
    return jax.shard_map(
        per_device,
        mesh=cut,
        in_specs=(dp, dp, section, section, dp, dp, dp),
        out_specs=(section, section),
        check_vma=False,
    )
```

```python
import jax
import jax.numpy as jnp
from jax import lax
from jax.experimental import pallas as pl
from jax.experimental.pallas import tpu as pltpu
from jax.sharding import Mesh
from jax.sharding import PartitionSpec as P

HEADS = 4
EPSILON = 1e-06
TEMPER = 4.0
D = 512
INNER = 256
ROWS = 128
HEAD = INNER // HEADS
SCALE = TEMPER / HEAD
STAGE_LAYERS = 4
F32 = jnp.float32
BF16 = jnp.bfloat16
STASH = {
    "normed": ((ROWS, D), BF16),
    "inverse": ((ROWS, ROWS), F32),
    "qkv": ((3, ROWS, INNER), BF16),
    "scales": ((2, ROWS, INNER), F32),
    "attn": ((HEADS * ROWS, ROWS), BF16),
    "mixed": ((ROWS, INNER), BF16),
}
TERMS = {
    "normed": ((ROWS, D), BF16),
    "mixed": ((ROWS, INNER), BF16),
    "grad_qkv": ((ROWS, 3 * INNER), BF16),
    "grad_out": ((ROWS, D), BF16),
}


def dot(a, b, over_a=1, over_b=0):
    return lax.dot_general(a, b, (((over_a,), (over_b,)), ((), ())), preferred_element_type=F32)


def head_masks():
    lane = lax.broadcasted_iota(jnp.int32, (1, INNER), 1)
    return [jnp.where(lane // HEAD == h, 1.0, 0.0).astype(F32) for h in range(HEADS)]


def head_mean_matrix():
    row = lax.broadcasted_iota(jnp.int32, (INNER, INNER), 0) // HEAD
    col = lax.broadcasted_iota(jnp.int32, (INNER, INNER), 1) // HEAD
    return jnp.where(row == col, 1.0 / HEAD, 0.0).astype(BF16)


def spread(values, masks):
    return jnp.concatenate([values * m.astype(values.dtype) for m in masks], axis=0)


def gathered(stacked, masks):
    total = stacked[:ROWS] * masks[0]
    for h in range(1, HEADS):
        total = total + stacked[h * ROWS : (h + 1) * ROWS] * masks[h]
    return total


def multiplicities(batch, tile_lists, counts, virtual):
    def times(tile, key_tile):
        seen = (virtual[batch] == key_tile).astype(F32)
        for slot in range(2):
            named = tile_lists[tile, slot, batch] == key_tile
            seen = seen + (named & (slot < counts[tile, batch])).astype(F32)
        return seen

    row = lax.broadcasted_iota(jnp.int32, (ROWS, ROWS), 0) < ROWS // 2
    col = lax.broadcasted_iota(jnp.int32, (ROWS, ROWS), 1) < ROWS // 2
    one = jnp.where(
        row,
        jnp.where(col, times(0, 0), times(0, 1)),
        jnp.where(col, times(1, 0), times(1, 1)),
    )
    return jnp.concatenate([one] * HEADS, axis=0)


def forward_layer(layer, hidden, weight, times, masks, mean_matrix, stash):
    widened = hidden.astype(F32)
    inverse = lax.rsqrt(jnp.mean(widened * widened, axis=-1, keepdims=True) + EPSILON)
    normed = (widened * inverse).astype(BF16)
    q = dot(normed, weight(0))
    k = dot(normed, weight(1))
    v = dot(normed, weight(2)).astype(BF16)
    scale_q = lax.rsqrt(dot((q * q).astype(BF16), mean_matrix) + EPSILON) * SCALE
    scale_k = lax.rsqrt(dot((k * k).astype(BF16), mean_matrix) + EPSILON)
    qn = (q * scale_q).astype(BF16)
    kn = (k * scale_k).astype(BF16)
    scores = dot(spread(qn, masks), kn, 1, 1)
    exponent = jnp.exp(scores) * times
    attn = (exponent * (1.0 / jnp.sum(exponent, axis=-1, keepdims=True))).astype(BF16)
    mixed = gathered(dot(attn, v), masks).astype(BF16)
    stash["normed"][layer] = normed
    stash["inverse"][layer] = jnp.broadcast_to(inverse, (ROWS, ROWS))
    stash["qkv"][layer, 0] = qn
    stash["qkv"][layer, 1] = kn
    stash["qkv"][layer, 2] = v
    stash["scales"][layer, 0] = scale_q
    stash["scales"][layer, 1] = scale_k
    stash["attn"][layer] = attn
    stash["mixed"][layer] = mixed
    out = weight(3)
    added = jnp.concatenate([dot(mixed, out[:INNER]), dot(mixed, out[INNER:])], axis=1)
    return (widened + added).astype(BF16)


def backward_layer(layer, grad, weight, masks, mean_matrix, stash):
    inverse = stash["inverse"][layer][:, :1]
    qn = stash["qkv"][layer, 0]
    kn = stash["qkv"][layer, 1]
    v = stash["qkv"][layer, 2]
    attn = stash["attn"][layer]
    out = weight(3)
    low, high = grad[:, :INNER], grad[:, INNER:]
    grad_mixed = (dot(low, out[:INNER], 1, 1) + dot(high, out[INNER:], 1, 1)).astype(BF16)
    stacked = spread(grad_mixed, masks)
    grad_attn = dot(stacked, v, 1, 1)
    attn_wide = attn.astype(F32)
    inner = jnp.sum(attn_wide * grad_attn, axis=-1, keepdims=True)
    grad_scores = (attn_wide * (grad_attn - inner)).astype(BF16)
    grad_v = dot(attn, stacked, 0, 0).astype(BF16)
    grad_qn = gathered(dot(grad_scores, kn), masks)
    grad_kn = dot(grad_scores, spread(qn, masks), 0, 0)
    qw, kw = qn.astype(F32), kn.astype(F32)
    mean_q = dot((grad_qn * qw).astype(BF16), mean_matrix) * (1.0 / (SCALE * SCALE))
    mean_k = dot((grad_kn * kw).astype(BF16), mean_matrix)
    grad_q = (stash["scales"][layer, 0] * (grad_qn - qw * mean_q)).astype(BF16)
    grad_k = (stash["scales"][layer, 1] * (grad_kn - kw * mean_k)).astype(BF16)
    grad_normed = dot(grad_q, weight(0), 1, 1) + dot(grad_k, weight(1), 1, 1) + dot(grad_v, weight(2), 1, 1)
    wide = stash["normed"][layer].astype(F32)
    mean = jnp.mean(grad_normed * wide, axis=-1, keepdims=True)
    result = (grad.astype(F32) + inverse * (grad_normed - wide * mean)).astype(BF16)
    return result, jnp.concatenate([grad_q, grad_k, grad_v], axis=1)


class Weights:
    def __init__(self, own, beside, near2, far2, near3, far3, place, sems, me, core, order):
        self.place, self.me, self.order = place, me, order

        def halves(r, near, far):
            return [(near, place.at[r, pl.ds(2 * core, 2)]), (far, place.at[r, pl.ds(2 * (1 - core), 2)])]

        pairs = [
            [(own, place.at[0])],
            [(beside, place.at[1])],
            halves(2, near2, far2),
            halves(3, near3, far3),
        ]
        self.copies = [
            [pltpu.make_async_copy(src, dst, sems.at[r, i]) for i, (src, dst) in enumerate(listed)]
            for r, listed in enumerate(pairs)
        ]

    def each(self, layer, act):
        for r in range(STAGE_LAYERS):

            @pl.when((layer ^ self.me) == r)
            def _(r=r):
                for copy in self.copies[r]:
                    act(copy)

    def start(self):
        for layer in self.order:
            self.each(layer, lambda copy: copy.start())

    def wait(self, layer):
        self.each(layer, lambda copy: copy.wait())

    def layer(self, index):
        r = index ^ self.me
        return lambda block: self.place[r, block]


class Sheets:
    def __init__(self, names, outside, inside, sems, inward):
        self.copies = []
        for layer in range(STAGE_LAYERS):
            listed = []
            for i in range(len(names)):
                a, b = outside[i].at[layer], inside[i].at[layer]
                listed.append(pltpu.make_async_copy(*((a, b) if inward else (b, a)), sems.at[i, layer]))
            self.copies.append(listed)
        self.refs = dict(zip(names, inside))

    def start(self, layer):
        for copy in self.copies[layer]:
            copy.start()

    def wait(self, layer):
        for copy in self.copies[layer]:
            copy.wait()


def weight_gradients(layer, normed, mixed, grad_qkv, grad_out, place, core):
    full = dot(normed, grad_qkv, 0, 0).astype(BF16)
    for block in range(3):
        place[(block // 2) ^ core, layer, block % 2] = full[:, block * INNER : (block + 1) * INNER]
    last = dot(mixed, grad_out, 0, 0).astype(BF16)
    place[1 ^ core, layer, 1, :INNER] = last[:, :INNER]
    place[1 ^ core, layer, 1, INNER:] = last[:, INNER:]


def pack_kernel(info, qkv, out, own, half, sems):
    blocks = [[(qkv.at[0, :, pl.ds(b * INNER, INNER)], slice(None))] for b in range(3)]
    blocks.append([(out.at[0, :, pl.ds(i * INNER, INNER)], pl.ds(i * INNER, INNER)) for i in range(2)])
    copies = []
    for block in range(4):
        for i, (source, rows) in enumerate(blocks[block]):
            copies.append(pltpu.make_async_copy(source, own.at[block, rows], sems.at[0, block + i]))
    for copy in copies:
        copy.start()
    for side in range(2):

        @pl.when(info[2] == side)
        def _(side=side):
            chosen = []
            for slot in range(2):
                for i, (source, rows) in enumerate(blocks[2 * side + slot]):
                    chosen.append(pltpu.make_async_copy(source, half.at[slot, rows], sems.at[1, slot + i]))
            for copy in chosen:
                copy.start()
            for copy in chosen:
                copy.wait()

    for copy in copies:
        copy.wait()


def forward_kernel(info, tile_lists, counts, virtual, hidden_in, *rest):
    weights = Weights(*rest[:6], *rest[-4:-2], info[1], info[2], range(STAGE_LAYERS))
    hidden_out, outside, inside = rest[6], rest[7 : 7 + len(STASH)], rest[7 + len(STASH) : 7 + 2 * len(STASH)]
    sheets = Sheets(STASH, outside, inside, rest[-2], False)
    weights.start()
    masks, mean_matrix = head_masks(), head_mean_matrix()
    times = rest[-1]
    times[...] = multiplicities(info[0], tile_lists, counts, virtual)
    hidden = hidden_in[0]
    for layer in range(STAGE_LAYERS):
        weights.wait(layer)
        hidden = forward_layer(layer, hidden, weights.layer(layer), times[...], masks, mean_matrix, sheets.refs)
        sheets.start(layer)
    hidden_out[...] = hidden
    for layer in range(STAGE_LAYERS):
        sheets.wait(layer)


def chain_kernel(info, tile_lists, counts, virtual, hidden_in, grad_in, *rest):
    weights = Weights(*rest[:6], *rest[-4:-2], info[1], info[2], range(STAGE_LAYERS))
    grad_out, outside = rest[6], rest[7 : 7 + len(TERMS)]
    stash = dict(zip(STASH, rest[7 + len(TERMS) :][: len(STASH)]))
    extra = rest[7 + len(TERMS) + len(STASH) :][:2]
    sheets = Sheets(TERMS, outside, (stash["normed"], stash["mixed"], *extra), rest[-2], False)
    weights.start()
    masks, mean_matrix = head_masks(), head_mean_matrix()
    times = rest[-1]
    times[...] = multiplicities(info[0], tile_lists, counts, virtual)
    hidden = hidden_in[...]
    for layer in range(STAGE_LAYERS):
        weights.wait(layer)
        hidden = forward_layer(layer, hidden, weights.layer(layer), times[...], masks, mean_matrix, stash)
    grad = grad_in[0]
    for layer in reversed(range(STAGE_LAYERS)):
        sheets.refs["grad_out"][layer] = grad
        grad, grad_qkv = backward_layer(layer, grad, weights.layer(layer), masks, mean_matrix, stash)
        sheets.refs["grad_qkv"][layer] = grad_qkv
        sheets.start(layer)
    grad_out[...] = grad
    for layer in range(STAGE_LAYERS):
        sheets.wait(layer)


def gradient_kernel(info, *rest):
    outside, (keep, send), inside = rest[: len(TERMS)], rest[len(TERMS) :][:2], rest[len(TERMS) + 2 : -3]
    place, in_sems, out_sems = rest[-3:]
    sheets = Sheets(TERMS, outside, inside, in_sems, True)
    results = Sheets(("keep", "send"), (keep, send), (place.at[0], place.at[1]), out_sems, False)
    for layer in range(STAGE_LAYERS):
        sheets.start(layer)
    for layer in range(STAGE_LAYERS):
        sheets.wait(layer)
        weight_gradients(layer, *(sheets.refs[n][layer] for n in TERMS), place, info[2])
        results.start(layer)
    for layer in range(STAGE_LAYERS):
        results.wait(layer)


def backward_kernel(info, grad_in, *rest):
    order = tuple(reversed(range(STAGE_LAYERS)))
    count = len(STASH)
    outside, given, (keep, send) = rest[:count], rest[count:][:6], rest[count + 6 :][:2]
    inside = rest[count + 8 :][:count]
    weight_place, weight_sems, place, in_sems, out_sems = rest[-5:]
    weights = Weights(*given, weight_place, weight_sems, info[1], info[2], order)
    sheets = Sheets(STASH, outside, inside, in_sems, True)
    results = Sheets(("keep", "send"), (keep, send), (place.at[0], place.at[1]), out_sems, False)
    for layer in order:
        sheets.start(layer)
        weights.each(layer, lambda copy: copy.start())
    masks, mean_matrix = head_masks(), head_mean_matrix()
    grad = grad_in[...]
    for layer in order:
        sheets.wait(layer)
        weights.wait(layer)
        before = grad
        grad, grad_qkv = backward_layer(layer, grad, weights.layer(layer), masks, mean_matrix, sheets.refs)
        weight_gradients(
            layer, sheets.refs["normed"][layer], sheets.refs["mixed"][layer], grad_qkv, before, place, info[2]
        )
        results.start(layer)
    for layer in order:
        results.wait(layer)


ANYWHERE = pl.BlockSpec(memory_space=pl.ANY)
HIDDEN = jax.ShapeDtypeStruct((ROWS, D), BF16)
HIDDEN_BLOCK = pl.BlockSpec((ROWS, D), lambda *_: (0, 0))
BATCH_BLOCK = pl.BlockSpec((1, ROWS, D), lambda step, info, *_: (info[0], 0, 0))
GRAD_HALF = jax.ShapeDtypeStruct((STAGE_LAYERS, 2, D, INNER), BF16)
WEIGHT_SCRATCH = [
    pltpu.VMEM((STAGE_LAYERS, 4, D, INNER), BF16),
    pltpu.SemaphoreType.DMA((STAGE_LAYERS, 2)),
]
GRAD_PLACE = pltpu.VMEM((2, STAGE_LAYERS, 2, D, INNER), BF16)
TIMES = pltpu.VMEM((HEADS * ROWS, ROWS), F32)


def layered(sizes, make):
    return [make((STAGE_LAYERS, *shape), kind) for shape, kind in sizes.values()]


def semaphores(count):
    return pltpu.SemaphoreType.DMA((count, STAGE_LAYERS))


def call(kernel, prefetched, in_specs, out_specs, out_shape, scratch, args):
    return pl.pallas_call(
        kernel,
        grid_spec=pltpu.PrefetchScalarGridSpec(
            num_scalar_prefetch=prefetched,
            grid=(1,),
            in_specs=in_specs,
            out_specs=out_specs,
            scratch_shapes=scratch,
        ),
        out_shape=out_shape,
        compiler_params=pltpu.CompilerParams(vmem_limit_bytes=48 * 2**20),
    )(*args)


def run_pack(info, w_qkv, w_out):
    shapes = [jax.ShapeDtypeStruct((blocks, D, INNER), BF16) for blocks in (4, 2)]
    sems = [pltpu.SemaphoreType.DMA((2, 5))]
    return call(pack_kernel, 1, [ANYWHERE] * 2, [ANYWHERE] * 2, shapes, sems, (info, w_qkv, w_out))


def run_forward(info, tables, nodes, weights):
    return call(
        forward_kernel,
        4,
        [BATCH_BLOCK] + [ANYWHERE] * 6,
        [HIDDEN_BLOCK] + [ANYWHERE] * len(STASH),
        [HIDDEN] + layered(STASH, jax.ShapeDtypeStruct),
        layered(STASH, pltpu.VMEM) + WEIGHT_SCRATCH + [semaphores(len(STASH)), TIMES],
        (info, *tables, nodes, *weights),
    )


def run_chain(info, tables, hidden, cotangent, weights):
    return call(
        chain_kernel,
        4,
        [HIDDEN_BLOCK, BATCH_BLOCK] + [ANYWHERE] * 6,
        [HIDDEN_BLOCK] + [ANYWHERE] * len(TERMS),
        [HIDDEN] + layered(TERMS, jax.ShapeDtypeStruct),
        layered(STASH, pltpu.VMEM) + layered(TERMS, pltpu.VMEM)[2:] + WEIGHT_SCRATCH + [semaphores(len(TERMS)), TIMES],
        (info, *tables, hidden, cotangent, *weights),
    )


def run_gradients(info, terms):
    return call(
        gradient_kernel,
        1,
        [ANYWHERE] * len(TERMS),
        [ANYWHERE] * 2,
        [GRAD_HALF] * 2,
        layered(TERMS, pltpu.VMEM) + [GRAD_PLACE, semaphores(len(TERMS)), semaphores(2)],
        (info, *terms),
    )


def run_backward(info, grad, stash, weights):
    return call(
        backward_kernel,
        1,
        [HIDDEN_BLOCK] + [ANYWHERE] * (len(STASH) + 6),
        [ANYWHERE] * 2,
        [GRAD_HALF] * 2,
        layered(STASH, pltpu.VMEM) + WEIGHT_SCRATCH + [GRAD_PLACE, semaphores(len(STASH)), semaphores(2)],
        (info, grad, *stash, *weights),
    )


def swapped(value, axis):
    return lax.ppermute(value, axis, [(0, 1), (1, 0)])


def fetched(value, flip_y, flip_x):
    axes = ("yl", "xl", "xh", "core")
    pairs = []
    for y in range(2):
        for x in range(2):
            for upper in range(2):
                for core in range(2):
                    there = upper ^ (core if flip_x else 0)
                    source = ((y * 2 + x) * 2 + upper) * 2 + core
                    target = (((y ^ flip_y) * 2 + (x ^ flip_x)) * 2 + there) * 2 + core
                    pairs.append((source, target))
    return lax.ppermute(value, axes, pairs)


def per_device(nodes, cotangent, w_qkv, w_out, tile_lists, counts, virtual):
    stage = lax.axis_index("yh")
    y, x, core = lax.axis_index("yl"), lax.axis_index("xl"), lax.axis_index("core")
    me = y * 2 + x
    batch = jnp.where(stage == 0, y, 1 - y) * 2 + x
    info = jnp.stack([batch, me, core]).astype(jnp.int32)
    tables = (tile_lists.transpose(1, 2, 0), counts.transpose(1, 0), virtual)
    own, half = run_pack(info, w_qkv, w_out)
    near2 = fetched(half, 1, 0)
    near3 = fetched(half, 1, 1)
    beside = fetched(own, 0, 1)
    far2, far3 = swapped(near2, "core"), swapped(near3, "core")
    weights = (own, beside, near2, far2, near3, far3)

    hidden, *stash = run_forward(info, tables, nodes, weights)
    across = [(0, 3), (1, 2), (2, 1), (3, 0)]
    hidden = lax.ppermute(hidden, ("yh", "yl"), across)
    grad, *terms = run_chain(info, tables, hidden, cotangent, weights)
    grad = lax.ppermute(grad, ("yh", "yl"), across)
    keep, send = lax.cond(
        stage == 0,
        lambda: tuple(run_backward(info, grad, stash, weights)),
        lambda: tuple(run_gradients(info, terms)),
    )

    def added(value, axis):
        return jnp.sum(value.astype(F32), axis=axis).astype(BF16)

    def repeated(value, times):
        return jnp.broadcast_to(value, (times, *value.shape))

    far, near = lax.axis_size("zh"), lax.axis_size("zl")
    piece = D // near
    total = (keep.astype(F32) + swapped(send, "core").astype(F32)).astype(BF16)
    total = lax.all_to_all(total.reshape(8, D, INNER), ("yl", "xl", "xh"), 0, 0, tiled=True)
    total = added(total, 0).reshape(near, piece, INNER)
    total = added(lax.all_to_all(total, "zl", 0, 0, tiled=True), 0)
    total = added(lax.all_to_all(repeated(total, far), "zh", 0, 0, tiled=True), 0)
    total = lax.all_to_all(repeated(total, 2 * near), ("xh", "zl"), 0, 0, tiled=True)
    mine = total.reshape(2, D, INNER)
    other = swapped(mine, "core")
    first, second = jnp.where(core == 0, mine, other), jnp.where(core == 0, other, mine)
    grad_qkv = jnp.concatenate([first[0], first[1], second[0]], axis=1)
    grad_out = jnp.concatenate([second[1, :INNER], second[1, INNER:]], axis=1)
    return (grad_qkv[None], grad_out[None])


def solution(mesh):
    depth = mesh.shape["dp"] // 4
    near = min(depth, 4)
    names = ("yh", "yl", "xl", "zh", "zl", "xh", "core")
    cut = Mesh(mesh.devices.reshape(2, 2, 2, depth // near, near, 2, 2), names)
    section, dp = P(("yh", "yl", "xl")), P(("zh", "zl", "xh", "core"))
    return jax.shard_map(
        per_device,
        mesh=cut,
        in_specs=(dp, dp, section, section, dp, dp, dp),
        out_specs=(section, section),
        check_vma=False,
    )
```

```python
import jax
import jax.numpy as jnp
from jax import lax
from jax.experimental import pallas as pl
from jax.experimental.pallas import tpu as pltpu
from jax.sharding import Mesh
from jax.sharding import PartitionSpec as P

HEADS = 4
EPSILON = 1e-06
TEMPER = 4.0
D = 512
INNER = 256
ROWS = 128
HEAD = INNER // HEADS
SCALE = TEMPER / HEAD
STAGE_LAYERS = 4
F32 = jnp.float32
BF16 = jnp.bfloat16
STASH = {
    "normed": ((ROWS, D), BF16),
    "inverse": ((ROWS, ROWS), F32),
    "qkv": ((3, ROWS, INNER), BF16),
    "scales": ((2, ROWS, INNER), F32),
    "attn": ((HEADS * ROWS, ROWS), BF16),
    "mixed": ((ROWS, INNER), BF16),
}
TERMS = {
    "normed": ((ROWS, D), BF16),
    "mixed": ((ROWS, INNER), BF16),
    "grad_qkv": ((ROWS, 3 * INNER), BF16),
    "grad_out": ((ROWS, D), BF16),
}


def dot(a, b, over_a=1, over_b=0):
    return lax.dot_general(a, b, (((over_a,), (over_b,)), ((), ())), preferred_element_type=F32)


def head_masks():
    lane = lax.broadcasted_iota(jnp.int32, (1, INNER), 1)
    return [jnp.where(lane // HEAD == h, 1.0, 0.0).astype(F32) for h in range(HEADS)]


def head_mean_matrix():
    row = lax.broadcasted_iota(jnp.int32, (INNER, INNER), 0) // HEAD
    col = lax.broadcasted_iota(jnp.int32, (INNER, INNER), 1) // HEAD
    return jnp.where(row == col, 1.0 / HEAD, 0.0).astype(BF16)


def spread(values, masks):
    return jnp.concatenate([values * m.astype(values.dtype) for m in masks], axis=0)


def gathered(stacked, masks):
    total = stacked[:ROWS] * masks[0]
    for h in range(1, HEADS):
        total = total + stacked[h * ROWS : (h + 1) * ROWS] * masks[h]
    return total


def multiplicities(batch, tile_lists, counts, virtual):
    def times(tile, key_tile):
        seen = (virtual[batch] == key_tile).astype(F32)
        for slot in range(2):
            named = tile_lists[tile, slot, batch] == key_tile
            seen = seen + (named & (slot < counts[tile, batch])).astype(F32)
        return seen

    row = lax.broadcasted_iota(jnp.int32, (ROWS, ROWS), 0) < ROWS // 2
    col = lax.broadcasted_iota(jnp.int32, (ROWS, ROWS), 1) < ROWS // 2
    one = jnp.where(
        row,
        jnp.where(col, times(0, 0), times(0, 1)),
        jnp.where(col, times(1, 0), times(1, 1)),
    )
    return jnp.concatenate([one] * HEADS, axis=0)


def forward_layer(layer, hidden, weight, times, masks, mean_matrix, stash):
    widened = hidden.astype(F32)
    inverse = lax.rsqrt(jnp.mean(widened * widened, axis=-1, keepdims=True) + EPSILON)
    normed = (widened * inverse).astype(BF16)
    q = dot(normed, weight(0))
    k = dot(normed, weight(1))
    v = dot(normed, weight(2)).astype(BF16)
    scale_q = lax.rsqrt(dot((q * q).astype(BF16), mean_matrix) + EPSILON) * SCALE
    scale_k = lax.rsqrt(dot((k * k).astype(BF16), mean_matrix) + EPSILON)
    qn = (q * scale_q).astype(BF16)
    kn = (k * scale_k).astype(BF16)
    scores = dot(spread(qn, masks), kn, 1, 1)
    exponent = jnp.exp(scores) * times
    attn = (exponent * (1.0 / jnp.sum(exponent, axis=-1, keepdims=True))).astype(BF16)
    mixed = gathered(dot(attn, v), masks).astype(BF16)
    stash["normed"][layer] = normed
    stash["inverse"][layer] = jnp.broadcast_to(inverse, (ROWS, ROWS))
    stash["qkv"][layer, 0] = qn
    stash["qkv"][layer, 1] = kn
    stash["qkv"][layer, 2] = v
    stash["scales"][layer, 0] = scale_q
    stash["scales"][layer, 1] = scale_k
    stash["attn"][layer] = attn
    stash["mixed"][layer] = mixed
    out = weight(3)
    added = jnp.concatenate([dot(mixed, out[:INNER]), dot(mixed, out[INNER:])], axis=1)
    return (widened + added).astype(BF16)


def backward_layer(layer, grad, weight, masks, mean_matrix, stash):
    inverse = stash["inverse"][layer][:, :1]
    qn = stash["qkv"][layer, 0]
    kn = stash["qkv"][layer, 1]
    v = stash["qkv"][layer, 2]
    attn = stash["attn"][layer]
    out = weight(3)
    low, high = grad[:, :INNER], grad[:, INNER:]
    grad_mixed = (dot(low, out[:INNER], 1, 1) + dot(high, out[INNER:], 1, 1)).astype(BF16)
    stacked = spread(grad_mixed, masks)
    grad_attn = dot(stacked, v, 1, 1)
    attn_wide = attn.astype(F32)
    inner = jnp.sum(attn_wide * grad_attn, axis=-1, keepdims=True)
    grad_scores = (attn_wide * (grad_attn - inner)).astype(BF16)
    grad_v = dot(attn, stacked, 0, 0).astype(BF16)
    grad_qn = gathered(dot(grad_scores, kn), masks)
    grad_kn = dot(grad_scores, spread(qn, masks), 0, 0)
    qw, kw = qn.astype(F32), kn.astype(F32)
    mean_q = dot((grad_qn * qw).astype(BF16), mean_matrix) * (1.0 / (SCALE * SCALE))
    mean_k = dot((grad_kn * kw).astype(BF16), mean_matrix)
    grad_q = (stash["scales"][layer, 0] * (grad_qn - qw * mean_q)).astype(BF16)
    grad_k = (stash["scales"][layer, 1] * (grad_kn - kw * mean_k)).astype(BF16)
    grad_normed = dot(grad_q, weight(0), 1, 1) + dot(grad_k, weight(1), 1, 1) + dot(grad_v, weight(2), 1, 1)
    wide = stash["normed"][layer].astype(F32)
    mean = jnp.mean(grad_normed * wide, axis=-1, keepdims=True)
    result = (grad.astype(F32) + inverse * (grad_normed - wide * mean)).astype(BF16)
    return result, jnp.concatenate([grad_q, grad_k, grad_v], axis=1)


class Weights:
    def __init__(self, own, beside, near2, far2, near3, far3, place, sems, me, core, order):
        self.place, self.me, self.order = place, me, order

        def halves(r, near, far):
            return [(near, place.at[r, pl.ds(2 * core, 2)]), (far, place.at[r, pl.ds(2 * (1 - core), 2)])]

        pairs = [
            [(own, place.at[0])],
            [(beside, place.at[1])],
            halves(2, near2, far2),
            halves(3, near3, far3),
        ]
        self.copies = [
            [pltpu.make_async_copy(src, dst, sems.at[r, i]) for i, (src, dst) in enumerate(listed)]
            for r, listed in enumerate(pairs)
        ]

    def each(self, layer, act):
        for r in range(STAGE_LAYERS):

            @pl.when((layer ^ self.me) == r)
            def _(r=r):
                for copy in self.copies[r]:
                    act(copy)

    def start(self):
        for layer in self.order:
            self.each(layer, lambda copy: copy.start())

    def wait(self, layer):
        self.each(layer, lambda copy: copy.wait())

    def layer(self, index):
        r = index ^ self.me
        return lambda block: self.place[r, block]


class Sheets:
    def __init__(self, names, outside, inside, sems, inward):
        self.copies = []
        for layer in range(STAGE_LAYERS):
            listed = []
            for i in range(len(names)):
                a, b = outside[i].at[layer], inside[i].at[layer]
                listed.append(pltpu.make_async_copy(*((a, b) if inward else (b, a)), sems.at[i, layer]))
            self.copies.append(listed)
        self.refs = dict(zip(names, inside))

    def start(self, layer):
        for copy in self.copies[layer]:
            copy.start()

    def wait(self, layer):
        for copy in self.copies[layer]:
            copy.wait()


def weight_gradients(layer, normed, mixed, grad_qkv, grad_out, place, core):
    full = dot(normed, grad_qkv, 0, 0).astype(BF16)
    for block in range(3):
        place[(block // 2) ^ core, layer, block % 2] = full[:, block * INNER : (block + 1) * INNER]
    last = dot(mixed, grad_out, 0, 0).astype(BF16)
    place[1 ^ core, layer, 1, :INNER] = last[:, :INNER]
    place[1 ^ core, layer, 1, INNER:] = last[:, INNER:]


def pack_kernel(info, qkv, out, own, half, sems):
    blocks = [[(qkv.at[0, :, pl.ds(b * INNER, INNER)], slice(None))] for b in range(3)]
    blocks.append([(out.at[0, :, pl.ds(i * INNER, INNER)], pl.ds(i * INNER, INNER)) for i in range(2)])
    copies = []
    for block in range(4):
        for i, (source, rows) in enumerate(blocks[block]):
            copies.append(pltpu.make_async_copy(source, own.at[block, rows], sems.at[0, block + i]))
    for copy in copies:
        copy.start()
    for side in range(2):

        @pl.when(info[2] == side)
        def _(side=side):
            chosen = []
            for slot in range(2):
                for i, (source, rows) in enumerate(blocks[2 * side + slot]):
                    chosen.append(pltpu.make_async_copy(source, half.at[slot, rows], sems.at[1, slot + i]))
            for copy in chosen:
                copy.start()
            for copy in chosen:
                copy.wait()

    for copy in copies:
        copy.wait()


def unpack_kernel(info, mine, other, qkv, out, sems):
    for side in range(2):

        @pl.when(info[2] == side)
        def _(side=side):
            low, high = (mine, other) if side == 0 else (other, mine)
            pairs = [
                (low.at[0], qkv.at[0, :, pl.ds(0, INNER)]),
                (low.at[1], qkv.at[0, :, pl.ds(INNER, INNER)]),
                (high.at[0], qkv.at[0, :, pl.ds(2 * INNER, INNER)]),
                (high.at[1, pl.ds(0, INNER)], out.at[0, :, pl.ds(0, INNER)]),
                (high.at[1, pl.ds(INNER, INNER)], out.at[0, :, pl.ds(INNER, INNER)]),
            ]
            copies = [pltpu.make_async_copy(src, dst, sems.at[i]) for i, (src, dst) in enumerate(pairs)]
            for copy in copies:
                copy.start()
            for copy in copies:
                copy.wait()


def forward_kernel(info, tile_lists, counts, virtual, hidden_in, *rest):
    weights = Weights(*rest[:6], *rest[-4:-2], info[1], info[2], range(STAGE_LAYERS))
    hidden_out, outside, inside = rest[6], rest[7 : 7 + len(STASH)], rest[7 + len(STASH) : 7 + 2 * len(STASH)]
    sheets = Sheets(STASH, outside, inside, rest[-2], False)
    weights.start()
    masks, mean_matrix = head_masks(), head_mean_matrix()
    times = rest[-1]
    times[...] = multiplicities(info[0], tile_lists, counts, virtual)
    hidden = hidden_in[0]
    for layer in range(STAGE_LAYERS):
        weights.wait(layer)
        hidden = forward_layer(layer, hidden, weights.layer(layer), times[...], masks, mean_matrix, sheets.refs)
        sheets.start(layer)
    hidden_out[...] = hidden
    for layer in range(STAGE_LAYERS):
        sheets.wait(layer)


def chain_kernel(info, tile_lists, counts, virtual, hidden_in, grad_in, *rest):
    weights = Weights(*rest[:6], *rest[-4:-2], info[1], info[2], range(STAGE_LAYERS))
    grad_out, outside = rest[6], rest[7 : 7 + len(TERMS)]
    stash = dict(zip(STASH, rest[7 + len(TERMS) :][: len(STASH)]))
    extra = rest[7 + len(TERMS) + len(STASH) :][:2]
    sheets = Sheets(TERMS, outside, (stash["normed"], stash["mixed"], *extra), rest[-2], False)
    weights.start()
    masks, mean_matrix = head_masks(), head_mean_matrix()
    times = rest[-1]
    times[...] = multiplicities(info[0], tile_lists, counts, virtual)
    hidden = hidden_in[...]
    for layer in range(STAGE_LAYERS):
        weights.wait(layer)
        hidden = forward_layer(layer, hidden, weights.layer(layer), times[...], masks, mean_matrix, stash)
    grad = grad_in[0]
    for layer in reversed(range(STAGE_LAYERS)):
        sheets.refs["grad_out"][layer] = grad
        grad, grad_qkv = backward_layer(layer, grad, weights.layer(layer), masks, mean_matrix, stash)
        sheets.refs["grad_qkv"][layer] = grad_qkv
        sheets.start(layer)
    grad_out[...] = grad
    for layer in range(STAGE_LAYERS):
        sheets.wait(layer)


def gradient_kernel(info, *rest):
    outside, (keep, send), inside = rest[: len(TERMS)], rest[len(TERMS) :][:2], rest[len(TERMS) + 2 : -3]
    place, in_sems, out_sems = rest[-3:]
    sheets = Sheets(TERMS, outside, inside, in_sems, True)
    results = Sheets(("keep", "send"), (keep, send), (place.at[0], place.at[1]), out_sems, False)
    for layer in range(STAGE_LAYERS):
        sheets.start(layer)
    for layer in range(STAGE_LAYERS):
        sheets.wait(layer)
        weight_gradients(layer, *(sheets.refs[n][layer] for n in TERMS), place, info[2])
        results.start(layer)
    for layer in range(STAGE_LAYERS):
        results.wait(layer)


def backward_kernel(info, grad_in, *rest):
    order = tuple(reversed(range(STAGE_LAYERS)))
    count = len(STASH)
    outside, given, (keep, send) = rest[:count], rest[count:][:6], rest[count + 6 :][:2]
    inside = rest[count + 8 :][:count]
    weight_place, weight_sems, place, in_sems, out_sems = rest[-5:]
    weights = Weights(*given, weight_place, weight_sems, info[1], info[2], order)
    sheets = Sheets(STASH, outside, inside, in_sems, True)
    results = Sheets(("keep", "send"), (keep, send), (place.at[0], place.at[1]), out_sems, False)
    for layer in order:
        sheets.start(layer)
        weights.each(layer, lambda copy: copy.start())
    masks, mean_matrix = head_masks(), head_mean_matrix()
    grad = grad_in[...]
    for layer in order:
        sheets.wait(layer)
        weights.wait(layer)
        before = grad
        grad, grad_qkv = backward_layer(layer, grad, weights.layer(layer), masks, mean_matrix, sheets.refs)
        weight_gradients(
            layer, sheets.refs["normed"][layer], sheets.refs["mixed"][layer], grad_qkv, before, place, info[2]
        )
        results.start(layer)
    for layer in order:
        results.wait(layer)


ANYWHERE = pl.BlockSpec(memory_space=pl.ANY)
IN_HBM = pl.BlockSpec(memory_space=pltpu.HBM)
HIDDEN = jax.ShapeDtypeStruct((ROWS, D), BF16)
HIDDEN_BLOCK = pl.BlockSpec((ROWS, D), lambda *_: (0, 0))
BATCH_BLOCK = pl.BlockSpec((1, ROWS, D), lambda step, info, *_: (info[0], 0, 0))
GRAD_HALF = jax.ShapeDtypeStruct((STAGE_LAYERS, 2, D, INNER), BF16)
WEIGHT_SCRATCH = [
    pltpu.VMEM((STAGE_LAYERS, 4, D, INNER), BF16),
    pltpu.SemaphoreType.DMA((STAGE_LAYERS, 2)),
]
GRAD_PLACE = pltpu.VMEM((2, STAGE_LAYERS, 2, D, INNER), BF16)
TIMES = pltpu.VMEM((HEADS * ROWS, ROWS), F32)


def layered(sizes, make):
    return [make((STAGE_LAYERS, *shape), kind) for shape, kind in sizes.values()]


def semaphores(count):
    return pltpu.SemaphoreType.DMA((count, STAGE_LAYERS))


def call(kernel, prefetched, in_specs, out_specs, out_shape, scratch, args, megabytes=20):
    return pl.pallas_call(
        kernel,
        grid_spec=pltpu.PrefetchScalarGridSpec(
            num_scalar_prefetch=prefetched,
            grid=(1,),
            in_specs=in_specs,
            out_specs=out_specs,
            scratch_shapes=scratch,
        ),
        out_shape=out_shape,
        compiler_params=pltpu.CompilerParams(vmem_limit_bytes=megabytes * 2**20),
    )(*args)


def run_pack(info, w_qkv, w_out):
    shapes = [jax.ShapeDtypeStruct((blocks, D, INNER), BF16) for blocks in (4, 2)]
    sems = [pltpu.SemaphoreType.DMA((2, 5))]
    return call(pack_kernel, 1, [IN_HBM] * 2, [ANYWHERE] * 2, shapes, sems, (info, w_qkv, w_out), 60)


def run_unpack(info, mine, other):
    shapes = [jax.ShapeDtypeStruct((1, *shape), BF16) for shape in ((D, 3 * INNER), (INNER, D))]
    sems = [pltpu.SemaphoreType.DMA((5,))]
    return call(unpack_kernel, 1, [ANYWHERE] * 2, [IN_HBM] * 2, shapes, sems, (info, mine, other), 1)


def run_forward(info, tables, nodes, weights):
    return call(
        forward_kernel,
        4,
        [BATCH_BLOCK] + [ANYWHERE] * 6,
        [HIDDEN_BLOCK] + [ANYWHERE] * len(STASH),
        [HIDDEN] + layered(STASH, jax.ShapeDtypeStruct),
        layered(STASH, pltpu.VMEM) + WEIGHT_SCRATCH + [semaphores(len(STASH)), TIMES],
        (info, *tables, nodes, *weights),
        59,
    )


def run_chain(info, tables, hidden, cotangent, weights):
    return call(
        chain_kernel,
        4,
        [HIDDEN_BLOCK, BATCH_BLOCK] + [ANYWHERE] * 6,
        [HIDDEN_BLOCK] + [ANYWHERE] * len(TERMS),
        [HIDDEN] + layered(TERMS, jax.ShapeDtypeStruct),
        layered(STASH, pltpu.VMEM) + layered(TERMS, pltpu.VMEM)[2:] + WEIGHT_SCRATCH + [semaphores(len(TERMS)), TIMES],
        (info, *tables, hidden, cotangent, *weights),
        50,
    )


def run_gradients(info, terms):
    return call(
        gradient_kernel,
        1,
        [ANYWHERE] * len(TERMS),
        [ANYWHERE] * 2,
        [GRAD_HALF] * 2,
        layered(TERMS, pltpu.VMEM) + [GRAD_PLACE, semaphores(len(TERMS)), semaphores(2)],
        (info, *terms),
    )


def run_backward(info, grad, stash, weights):
    return call(
        backward_kernel,
        1,
        [HIDDEN_BLOCK] + [ANYWHERE] * (len(STASH) + 6),
        [ANYWHERE] * 2,
        [GRAD_HALF] * 2,
        layered(STASH, pltpu.VMEM) + WEIGHT_SCRATCH + [GRAD_PLACE, semaphores(len(STASH)), semaphores(2)],
        (info, grad, *stash, *weights),
        20,
    )


def swapped(value, axis):
    return lax.ppermute(value, axis, [(0, 1), (1, 0)])


def fetched(value, flip_y, flip_x):
    axes = ("yl", "xl", "xh", "core")
    pairs = []
    for y in range(2):
        for x in range(2):
            for upper in range(2):
                for core in range(2):
                    there = upper ^ (core if flip_x else 0)
                    source = ((y * 2 + x) * 2 + upper) * 2 + core
                    target = (((y ^ flip_y) * 2 + (x ^ flip_x)) * 2 + there) * 2 + core
                    pairs.append((source, target))
    return lax.ppermute(value, axes, pairs)


def per_device(nodes, cotangent, w_qkv, w_out, tile_lists, counts, virtual):
    stage = lax.axis_index("yh")
    y, x, core = lax.axis_index("yl"), lax.axis_index("xl"), lax.axis_index("core")
    me = y * 2 + x
    batch = jnp.where(stage == 0, y, 1 - y) * 2 + x
    info = jnp.stack([batch, me, core]).astype(jnp.int32)
    tables = (tile_lists.transpose(1, 2, 0), counts.transpose(1, 0), virtual)
    own, half = run_pack(info, w_qkv, w_out)
    near2 = fetched(half, 1, 0)
    near3 = fetched(half, 1, 1)
    beside = fetched(own, 0, 1)
    far2, far3 = swapped(near2, "core"), swapped(near3, "core")
    weights = (own, beside, near2, far2, near3, far3)

    hidden, *stash = run_forward(info, tables, nodes, weights)
    across = [(0, 3), (1, 2), (2, 1), (3, 0)]
    hidden = lax.ppermute(hidden, ("yh", "yl"), across)
    grad, *terms = run_chain(info, tables, hidden, cotangent, weights)
    grad = lax.ppermute(grad, ("yh", "yl"), across)
    keep, send = lax.cond(
        stage == 0,
        lambda: tuple(run_backward(info, grad, stash, weights)),
        lambda: tuple(run_gradients(info, terms)),
    )

    def added(value, axis):
        return jnp.sum(value.astype(F32), axis=axis).astype(BF16)

    def repeated(value, times):
        return jnp.broadcast_to(value, (times, *value.shape))

    far, near = lax.axis_size("zh"), lax.axis_size("zl")
    piece = D // near
    total = (keep.astype(F32) + swapped(send, "core").astype(F32)).astype(BF16)
    total = lax.all_to_all(total.reshape(8, D, INNER), ("yl", "xl", "xh"), 0, 0, tiled=True)
    total = added(total, 0).reshape(near, piece, INNER)
    total = added(lax.all_to_all(total, "zl", 0, 0, tiled=True), 0)
    total = added(lax.all_to_all(repeated(total, far), "zh", 0, 0, tiled=True), 0)
    total = lax.all_to_all(repeated(total, 2 * near), ("xh", "zl"), 0, 0, tiled=True)
    mine = total.reshape(2, D, INNER)
    grad_qkv, grad_out = run_unpack(info, mine, swapped(mine, "core"))
    return (grad_qkv, grad_out)


def solution(mesh):
    depth = mesh.shape["dp"] // 4
    near = min(depth, 4)
    names = ("yh", "yl", "xl", "zh", "zl", "xh", "core")
    cut = Mesh(mesh.devices.reshape(2, 2, 2, depth // near, near, 2, 2), names)
    section, dp = P(("yh", "yl", "xl")), P(("zh", "zl", "xh", "core"))
    return jax.shard_map(
        per_device,
        mesh=cut,
        in_specs=(dp, dp, section, section, dp, dp, dp),
        out_specs=(section, section),
        check_vma=False,
    )
```

```python
import functools

import jax
import jax.numpy as jnp
from jax import lax
from jax.experimental import pallas as pl
from jax.experimental.pallas import tpu as pltpu
from jax.sharding import Mesh
from jax.sharding import PartitionSpec as P

HEADS = 4
EPSILON = 1e-06
TEMPER = 4.0
D = 512
INNER = 256
ROWS = 128
HEAD = INNER // HEADS
SCALE = TEMPER / HEAD
STAGE_LAYERS = 4
F32 = jnp.float32
BF16 = jnp.bfloat16
STASH = {
    "normed": ((ROWS, D), BF16),
    "inverse": ((ROWS, ROWS), F32),
    "qkv": ((3, ROWS, INNER), BF16),
    "scales": ((2, ROWS, INNER), F32),
    "attn": ((HEADS * ROWS, ROWS), BF16),
    "mixed": ((ROWS, INNER), BF16),
}
TERMS = {
    "normed": ((ROWS, D), BF16),
    "mixed": ((ROWS, INNER), BF16),
    "grad_qkv": ((ROWS, 3 * INNER), BF16),
    "grad_out": ((ROWS, D), BF16),
}


def dot(a, b, over_a=1, over_b=0):
    return lax.dot_general(a, b, (((over_a,), (over_b,)), ((), ())), preferred_element_type=F32)


def head_masks():
    lane = lax.broadcasted_iota(jnp.int32, (1, INNER), 1)
    return [jnp.where(lane // HEAD == h, 1.0, 0.0).astype(F32) for h in range(HEADS)]


def head_mean_matrix():
    row = lax.broadcasted_iota(jnp.int32, (INNER, INNER), 0) // HEAD
    col = lax.broadcasted_iota(jnp.int32, (INNER, INNER), 1) // HEAD
    return jnp.where(row == col, 1.0 / HEAD, 0.0).astype(BF16)


def spread(values, masks):
    return jnp.concatenate([values * m.astype(values.dtype) for m in masks], axis=0)


def gathered(stacked, masks):
    total = stacked[:ROWS] * masks[0]
    for h in range(1, HEADS):
        total = total + stacked[h * ROWS : (h + 1) * ROWS] * masks[h]
    return total


def multiplicities(batch, tile_lists, counts, virtual):
    def times(tile, key_tile):
        seen = (virtual[batch] == key_tile).astype(F32)
        for slot in range(2):
            named = tile_lists[tile, slot, batch] == key_tile
            seen = seen + (named & (slot < counts[tile, batch])).astype(F32)
        return seen

    row = lax.broadcasted_iota(jnp.int32, (ROWS, ROWS), 0) < ROWS // 2
    col = lax.broadcasted_iota(jnp.int32, (ROWS, ROWS), 1) < ROWS // 2
    one = jnp.where(
        row,
        jnp.where(col, times(0, 0), times(0, 1)),
        jnp.where(col, times(1, 0), times(1, 1)),
    )
    return jnp.concatenate([one] * HEADS, axis=0)


def forward_layer(layer, hidden, weight, times, masks, mean_matrix, stash):
    widened = hidden.astype(F32)
    inverse = lax.rsqrt(jnp.mean(widened * widened, axis=-1, keepdims=True) + EPSILON)
    normed = (widened * inverse).astype(BF16)
    q = dot(normed, weight(0))
    k = dot(normed, weight(1))
    v = dot(normed, weight(2)).astype(BF16)
    scale_q = lax.rsqrt(dot((q * q).astype(BF16), mean_matrix) + EPSILON) * SCALE
    scale_k = lax.rsqrt(dot((k * k).astype(BF16), mean_matrix) + EPSILON)
    qn = (q * scale_q).astype(BF16)
    kn = (k * scale_k).astype(BF16)
    scores = dot(spread(qn, masks), kn, 1, 1)
    exponent = jnp.exp(scores) * times
    share = 1.0 / jnp.sum(exponent, axis=-1, keepdims=True)
    mixed = gathered(dot(exponent.astype(BF16), v) * share, masks).astype(BF16)
    attn = (exponent * share).astype(BF16)
    stash["normed"][layer] = normed
    stash["inverse"][layer] = jnp.broadcast_to(inverse, (ROWS, ROWS))
    stash["qkv"][layer, 0] = qn
    stash["qkv"][layer, 1] = kn
    stash["qkv"][layer, 2] = v
    stash["scales"][layer, 0] = scale_q
    stash["scales"][layer, 1] = scale_k
    stash["attn"][layer] = attn
    stash["mixed"][layer] = mixed
    out = weight(3)
    added = jnp.concatenate([dot(mixed, out[:INNER]), dot(mixed, out[INNER:])], axis=1)
    return (widened + added).astype(BF16)


def backward_layer(layer, grad, weight, masks, mean_matrix, stash):
    inverse = stash["inverse"][layer][:, :1]
    qn = stash["qkv"][layer, 0]
    kn = stash["qkv"][layer, 1]
    v = stash["qkv"][layer, 2]
    attn = stash["attn"][layer]
    out = weight(3)
    low, high = grad[:, :INNER], grad[:, INNER:]
    grad_mixed = (dot(low, out[:INNER], 1, 1) + dot(high, out[INNER:], 1, 1)).astype(BF16)
    stacked = spread(grad_mixed, masks)
    grad_attn = dot(stacked, v, 1, 1)
    attn_wide = attn.astype(F32)
    product = grad_mixed.astype(F32) * stash["mixed"][layer].astype(F32)
    inner = jnp.concatenate([jnp.sum(product * m, axis=-1, keepdims=True) for m in masks], axis=0)
    grad_scores = (attn_wide * (grad_attn - inner)).astype(BF16)
    grad_v = dot(attn, stacked, 0, 0).astype(BF16)
    grad_qn = gathered(dot(grad_scores, kn), masks)
    grad_kn = dot(grad_scores, spread(qn, masks), 0, 0)
    qw, kw = qn.astype(F32), kn.astype(F32)
    mean_q = dot((grad_qn * qw).astype(BF16), mean_matrix) * (1.0 / (SCALE * SCALE))
    mean_k = dot((grad_kn * kw).astype(BF16), mean_matrix)
    grad_q = (stash["scales"][layer, 0] * (grad_qn - qw * mean_q)).astype(BF16)
    grad_k = (stash["scales"][layer, 1] * (grad_kn - kw * mean_k)).astype(BF16)
    grad_normed = dot(grad_q, weight(0), 1, 1) + dot(grad_k, weight(1), 1, 1) + dot(grad_v, weight(2), 1, 1)
    wide = stash["normed"][layer].astype(F32)
    mean = jnp.mean(grad_normed * wide, axis=-1, keepdims=True)
    result = (grad.astype(F32) + inverse * (grad_normed - wide * mean)).astype(BF16)
    return result, jnp.concatenate([grad_q, grad_k, grad_v], axis=1)


class Weights:
    def __init__(self, own, beside, near2, far2, near3, far3, place, sems, me, core, order):
        self.place, self.me, self.order = place, me, order

        def halves(r, near, far):
            return [(near, place.at[r, pl.ds(2 * core, 2)]), (far, place.at[r, pl.ds(2 * (1 - core), 2)])]

        pairs = [
            [(own, place.at[0])],
            [(beside, place.at[1])],
            halves(2, near2, far2),
            halves(3, near3, far3),
        ]
        self.copies = [
            [pltpu.make_async_copy(src, dst, sems.at[r, i]) for i, (src, dst) in enumerate(listed)]
            for r, listed in enumerate(pairs)
        ]

    def each(self, layer, act):
        for r in range(STAGE_LAYERS):

            @pl.when((layer ^ self.me) == r)
            def _(r=r):
                for copy in self.copies[r]:
                    act(copy)

    def start(self):
        for layer in self.order:
            self.each(layer, lambda copy: copy.start())

    def wait(self, layer):
        self.each(layer, lambda copy: copy.wait())

    def layer(self, index):
        r = index ^ self.me
        return lambda block: self.place[r, block]


class Sheets:
    def __init__(self, names, outside, inside, sems, inward):
        self.copies = []
        for layer in range(STAGE_LAYERS):
            listed = []
            for i in range(len(names)):
                a, b = outside[i].at[layer], inside[i].at[layer]
                listed.append(pltpu.make_async_copy(*((a, b) if inward else (b, a)), sems.at[i, layer]))
            self.copies.append(listed)
        self.refs = dict(zip(names, inside))

    def start(self, layer):
        for copy in self.copies[layer]:
            copy.start()

    def wait(self, layer):
        for copy in self.copies[layer]:
            copy.wait()


def half_gradients(layer, side, normed, mixed, grad_qkv, grad_out, place):
    @pl.when(side == 0)
    def _():
        full = dot(normed, grad_qkv[:, : 2 * INNER], 0, 0).astype(BF16)
        place[layer, 0] = full[:, :INNER]
        place[layer, 1] = full[:, INNER:]

    @pl.when(side == 1)
    def _():
        place[layer, 0] = dot(normed, grad_qkv[:, 2 * INNER :], 0, 0).astype(BF16)
        last = dot(mixed, grad_out, 0, 0).astype(BF16)
        place[layer, 1, :INNER] = last[:, :INNER]
        place[layer, 1, INNER:] = last[:, INNER:]


def pack_kernel(info, qkv, out, own, half, sems):
    blocks = [[(qkv.at[0, :, pl.ds(b * INNER, INNER)], slice(None))] for b in range(3)]
    blocks.append([(out.at[0, :, pl.ds(i * INNER, INNER)], pl.ds(i * INNER, INNER)) for i in range(2)])
    copies = []
    for block in range(4):
        for i, (source, rows) in enumerate(blocks[block]):
            copies.append(pltpu.make_async_copy(source, own.at[block, rows], sems.at[0, block + i]))
    for copy in copies:
        copy.start()
    for side in range(2):

        @pl.when(info[2] == side)
        def _(side=side):
            chosen = []
            for slot in range(2):
                for i, (source, rows) in enumerate(blocks[2 * side + slot]):
                    chosen.append(pltpu.make_async_copy(source, half.at[slot, rows], sems.at[1, slot + i]))
            for copy in chosen:
                copy.start()
            for copy in chosen:
                copy.wait()

    for copy in copies:
        copy.wait()


def unpack_kernel(info, mine, other, qkv, out, sems):
    for side in range(2):

        @pl.when(info[2] == side)
        def _(side=side):
            low, high = (mine, other) if side == 0 else (other, mine)
            pairs = [
                (low.at[0], qkv.at[0, :, pl.ds(0, INNER)]),
                (low.at[1], qkv.at[0, :, pl.ds(INNER, INNER)]),
                (high.at[0], qkv.at[0, :, pl.ds(2 * INNER, INNER)]),
                (high.at[1, pl.ds(0, INNER)], out.at[0, :, pl.ds(0, INNER)]),
                (high.at[1, pl.ds(INNER, INNER)], out.at[0, :, pl.ds(INNER, INNER)]),
            ]
            copies = [pltpu.make_async_copy(src, dst, sems.at[i]) for i, (src, dst) in enumerate(pairs)]
            for copy in copies:
                copy.start()
            for copy in copies:
                copy.wait()


def forward_kernel(info, tile_lists, counts, virtual, hidden_in, *rest):
    weights = Weights(*rest[:6], *rest[-4:-2], info[1], info[2], range(STAGE_LAYERS))
    hidden_out, outside, inside = rest[6], rest[7 : 7 + len(STASH)], rest[7 + len(STASH) : 7 + 2 * len(STASH)]
    sheets = Sheets(STASH, outside, inside, rest[-2], False)
    weights.start()
    masks, mean_matrix = head_masks(), head_mean_matrix()
    times = rest[-1]
    times[...] = multiplicities(info[0], tile_lists, counts, virtual)
    hidden = hidden_in[0]
    for layer in range(STAGE_LAYERS):
        weights.wait(layer)
        hidden = forward_layer(layer, hidden, weights.layer(layer), times[...], masks, mean_matrix, sheets.refs)
        sheets.start(layer)
    hidden_out[...] = hidden
    for layer in range(STAGE_LAYERS):
        sheets.wait(layer)


def chain_kernel(info, tile_lists, counts, virtual, hidden_in, grad_in, *rest):
    weights = Weights(*rest[:6], *rest[-4:-2], info[1], info[2], range(STAGE_LAYERS))
    grad_out, outside = rest[6], rest[7 : 7 + len(TERMS)]
    stash = dict(zip(STASH, rest[7 + len(TERMS) :][: len(STASH)]))
    extra = rest[7 + len(TERMS) + len(STASH) :][:2]
    sheets = Sheets(TERMS, outside, (stash["normed"], stash["mixed"], *extra), rest[-2], False)
    weights.start()
    masks, mean_matrix = head_masks(), head_mean_matrix()
    times = rest[-1]
    times[...] = multiplicities(info[0], tile_lists, counts, virtual)
    hidden = hidden_in[...]
    for layer in range(STAGE_LAYERS):
        weights.wait(layer)
        hidden = forward_layer(layer, hidden, weights.layer(layer), times[...], masks, mean_matrix, stash)
    grad = grad_in[0]
    for layer in reversed(range(STAGE_LAYERS)):
        sheets.refs["grad_out"][layer] = grad
        grad, grad_qkv = backward_layer(layer, grad, weights.layer(layer), masks, mean_matrix, stash)
        sheets.refs["grad_qkv"][layer] = grad_qkv
        sheets.start(layer)
    grad_out[...] = grad
    for layer in range(STAGE_LAYERS):
        sheets.wait(layer)


def gradient_kernel(keep, info, *rest):
    count = len(TERMS)
    given, result, inside = rest[: -count - 4], rest[-count - 4], rest[-count - 3 : -3]
    place, in_sems, out_sems = rest[-3:]
    side = info[2] if keep else 1 - info[2]
    choices = [Sheets(TERMS, (*given[i : i + 2], *given[-2:]), inside, in_sems, True) for i in range(0, len(given) - 2, 2)]
    results = Sheets(("half",), (result,), (place,), out_sems, False)

    def each(act):
        for i, sheets in enumerate(choices):
            if len(choices) == 1:
                act(sheets)
            else:
                pl.when(info[3] == i)(functools.partial(act, sheets))

    refs = choices[0].refs
    for layer in range(STAGE_LAYERS):
        each(lambda sheets: sheets.start(layer))
    for layer in range(STAGE_LAYERS):
        each(lambda sheets: sheets.wait(layer))
        half_gradients(layer, side, *(refs[n][layer] for n in TERMS), place)
        results.start(layer)
    for layer in range(STAGE_LAYERS):
        results.wait(layer)


def backward_kernel(info, grad_in, *rest):
    order = tuple(reversed(range(STAGE_LAYERS)))
    count = len(STASH)
    outside, given, outputs = rest[:count], rest[count:][:6], rest[count + 6 :][:3]
    inside = rest[count + 9 :][:count]
    weight_place, weight_sems, place, terms_qkv, terms_out, in_sems, out_sems = rest[-7:]
    weights = Weights(*given, weight_place, weight_sems, info[1], info[2], order)
    sheets = Sheets(STASH, outside, inside, in_sems, True)
    results = Sheets(("send", "grad_qkv", "grad_out"), outputs, (place, terms_qkv, terms_out), out_sems, False)
    for layer in order:
        sheets.start(layer)
        weights.each(layer, lambda copy: copy.start())
    masks, mean_matrix = head_masks(), head_mean_matrix()
    grad = grad_in[...]
    for layer in order:
        sheets.wait(layer)
        weights.wait(layer)
        before = grad
        grad, grad_qkv = backward_layer(layer, grad, weights.layer(layer), masks, mean_matrix, sheets.refs)
        terms_qkv[layer] = grad_qkv
        terms_out[layer] = before
        half_gradients(
            layer, 1 - info[2], sheets.refs["normed"][layer], sheets.refs["mixed"][layer], grad_qkv, before, place
        )
        results.start(layer)
    for layer in order:
        results.wait(layer)


ANYWHERE = pl.BlockSpec(memory_space=pl.ANY)
IN_HBM = pl.BlockSpec(memory_space=pltpu.HBM)
HIDDEN = jax.ShapeDtypeStruct((ROWS, D), BF16)
HIDDEN_BLOCK = pl.BlockSpec((ROWS, D), lambda *_: (0, 0))
BATCH_BLOCK = pl.BlockSpec((1, ROWS, D), lambda step, info, *_: (info[0], 0, 0))
GRAD_HALF = jax.ShapeDtypeStruct((STAGE_LAYERS, 2, D, INNER), BF16)
WEIGHT_SCRATCH = [
    pltpu.VMEM((STAGE_LAYERS, 4, D, INNER), BF16),
    pltpu.SemaphoreType.DMA((STAGE_LAYERS, 2)),
]
GRAD_PLACE = pltpu.VMEM((STAGE_LAYERS, 2, D, INNER), BF16)
TIMES = pltpu.VMEM((HEADS * ROWS, ROWS), F32)


def layered(sizes, make):
    return [make((STAGE_LAYERS, *shape), kind) for shape, kind in sizes.values()]


def semaphores(count):
    return pltpu.SemaphoreType.DMA((count, STAGE_LAYERS))


def call(kernel, prefetched, in_specs, out_specs, out_shape, scratch, args, megabytes=48):
    return pl.pallas_call(
        kernel,
        grid_spec=pltpu.PrefetchScalarGridSpec(
            num_scalar_prefetch=prefetched,
            grid=(1,),
            in_specs=in_specs,
            out_specs=out_specs,
            scratch_shapes=scratch,
        ),
        out_shape=out_shape,
        compiler_params=pltpu.CompilerParams(vmem_limit_bytes=megabytes * 2**20),
    )(*args)


def run_pack(info, w_qkv, w_out):
    shapes = [jax.ShapeDtypeStruct((blocks, D, INNER), BF16) for blocks in (4, 2)]
    sems = [pltpu.SemaphoreType.DMA((2, 5))]
    return call(pack_kernel, 1, [IN_HBM] * 2, [ANYWHERE] * 2, shapes, sems, (info, w_qkv, w_out), 1)


def run_unpack(info, mine, other):
    shapes = [jax.ShapeDtypeStruct((1, *shape), BF16) for shape in ((D, 3 * INNER), (INNER, D))]
    sems = [pltpu.SemaphoreType.DMA((5,))]
    return call(unpack_kernel, 1, [ANYWHERE] * 2, [IN_HBM] * 2, shapes, sems, (info, mine, other), 1)


def run_forward(info, tables, nodes, weights):
    return call(
        forward_kernel,
        4,
        [BATCH_BLOCK] + [ANYWHERE] * 6,
        [HIDDEN_BLOCK] + [ANYWHERE] * len(STASH),
        [HIDDEN] + layered(STASH, jax.ShapeDtypeStruct),
        layered(STASH, pltpu.VMEM) + WEIGHT_SCRATCH + [semaphores(len(STASH)), TIMES],
        (info, *tables, nodes, *weights),
        58,
    )


def run_chain(info, tables, hidden, cotangent, weights):
    return call(
        chain_kernel,
        4,
        [HIDDEN_BLOCK, BATCH_BLOCK] + [ANYWHERE] * 6,
        [HIDDEN_BLOCK] + [ANYWHERE] * len(TERMS),
        [HIDDEN] + layered(TERMS, jax.ShapeDtypeStruct),
        layered(STASH, pltpu.VMEM) + layered(TERMS, pltpu.VMEM)[2:] + WEIGHT_SCRATCH + [semaphores(len(TERMS)), TIMES],
        (info, *tables, hidden, cotangent, *weights),
        50,
    )


def run_gradients(info, terms, keep):
    return call(
        functools.partial(gradient_kernel, keep),
        1,
        [ANYWHERE] * len(terms),
        ANYWHERE,
        GRAD_HALF,
        layered(TERMS, pltpu.VMEM) + [GRAD_PLACE, semaphores(len(TERMS)), semaphores(1)],
        (info, *terms),
    )


def run_backward(info, grad, stash, weights):
    terms = layered(TERMS, jax.ShapeDtypeStruct)[2:]
    return call(
        backward_kernel,
        1,
        [HIDDEN_BLOCK] + [ANYWHERE] * (len(STASH) + 6),
        [ANYWHERE] * 3,
        [GRAD_HALF] + terms,
        layered(STASH, pltpu.VMEM)
        + WEIGHT_SCRATCH
        + [GRAD_PLACE]
        + layered(TERMS, pltpu.VMEM)[2:]
        + [semaphores(len(STASH)), semaphores(3)],
        (info, grad, *stash, *weights),
        48,
    )


def swapped(value, axis):
    return lax.ppermute(value, axis, [(0, 1), (1, 0)])


def fetched(value, flip_y, flip_x):
    axes = ("yl", "xl", "xh", "core")
    pairs = []
    for y in range(2):
        for x in range(2):
            for upper in range(2):
                for core in range(2):
                    there = upper ^ (core if flip_x else 0)
                    source = ((y * 2 + x) * 2 + upper) * 2 + core
                    target = (((y ^ flip_y) * 2 + (x ^ flip_x)) * 2 + there) * 2 + core
                    pairs.append((source, target))
    return lax.ppermute(value, axes, pairs)


def per_device(nodes, cotangent, w_qkv, w_out, tile_lists, counts, virtual):
    stage = lax.axis_index("yh")
    y, x, core = lax.axis_index("yl"), lax.axis_index("xl"), lax.axis_index("core")
    me = y * 2 + x
    batch = jnp.where(stage == 0, y, 1 - y) * 2 + x
    info = jnp.stack([batch, me, core, stage]).astype(jnp.int32)
    tables = (tile_lists.transpose(1, 2, 0), counts.transpose(1, 0), virtual)
    own, half = run_pack(info, w_qkv, w_out)
    near2 = fetched(half, 1, 0)
    near3 = fetched(half, 1, 1)
    beside = fetched(own, 0, 1)
    far2, far3 = swapped(near2, "core"), swapped(near3, "core")
    weights = (own, beside, near2, far2, near3, far3)

    hidden, *stash = run_forward(info, tables, nodes, weights)
    across = [(0, 3), (1, 2), (2, 1), (3, 0)]
    hidden = lax.ppermute(hidden, ("yh", "yl"), across)
    grad, *terms = run_chain(info, tables, hidden, cotangent, weights)
    grad = lax.ppermute(grad, ("yh", "yl"), across)
    send, grad_qkv, grad_out = lax.cond(
        stage == 0,
        lambda: tuple(run_backward(info, grad, stash, weights)),
        lambda: (run_gradients(info, terms, False), *terms[2:]),
    )
    first = dict(zip(STASH, stash))
    keep = run_gradients(info, (first["normed"], first["mixed"], *terms[:2], grad_qkv, grad_out), True)

    def added(value, axis):
        return jnp.sum(value.astype(F32), axis=axis).astype(BF16)

    def repeated(value, times):
        return jnp.broadcast_to(value, (times, *value.shape))

    far, near = lax.axis_size("zh"), lax.axis_size("zl")
    piece = D // near
    total = (keep.astype(F32) + swapped(send, "core").astype(F32)).astype(BF16)
    total = lax.all_to_all(total.reshape(8, D, INNER), ("yl", "xl", "xh"), 0, 0, tiled=True)
    total = added(total, 0).reshape(near, piece, INNER)
    total = added(lax.all_to_all(total, "zl", 0, 0, tiled=True), 0)
    total = added(lax.all_to_all(repeated(total, far), "zh", 0, 0, tiled=True), 0)
    total = lax.all_to_all(repeated(total, 2 * near), ("xh", "zl"), 0, 0, tiled=True)
    mine = total.reshape(2, D, INNER)
    grad_qkv, grad_out = run_unpack(info, mine, swapped(mine, "core"))
    return (grad_qkv, grad_out)


def solution(mesh):
    depth = mesh.shape["dp"] // 4
    near = min(depth, 4)
    names = ("yh", "yl", "xl", "zh", "zl", "xh", "core")
    cut = Mesh(mesh.devices.reshape(2, 2, 2, depth // near, near, 2, 2), names)
    section, dp = P(("yh", "yl", "xl")), P(("zh", "zl", "xh", "core"))
    return jax.shard_map(
        per_device,
        mesh=cut,
        in_specs=(dp, dp, section, section, dp, dp, dp),
        out_specs=(section, section),
        check_vma=False,
    )
```

```python
import functools

import jax
import jax.numpy as jnp
from jax import lax
from jax.experimental import pallas as pl
from jax.experimental.pallas import tpu as pltpu
from jax.sharding import Mesh
from jax.sharding import PartitionSpec as P

HEADS = 4
EPSILON = 1e-06
TEMPER = 4.0
D = 512
INNER = 256
ROWS = 128
HEAD = INNER // HEADS
SCALE = TEMPER / HEAD
STAGE_LAYERS = 4
F32 = jnp.float32
BF16 = jnp.bfloat16
STASH = {
    "normed": ((ROWS, D), BF16),
    "inverse": ((ROWS, ROWS), F32),
    "qkv": ((3, ROWS, INNER), BF16),
    "scales": ((2, ROWS, INNER), F32),
    "attn": ((HEADS * ROWS, ROWS), BF16),
    "mixed": ((ROWS, INNER), BF16),
}
TERMS = {
    "normed": ((ROWS, D), BF16),
    "mixed": ((ROWS, INNER), BF16),
    "grad_qkv": ((ROWS, 3 * INNER), BF16),
    "grad_out": ((ROWS, D), BF16),
}


def dot(a, b, over_a=1, over_b=0):
    return lax.dot_general(a, b, (((over_a,), (over_b,)), ((), ())), preferred_element_type=F32)


def head_masks():
    lane = lax.broadcasted_iota(jnp.int32, (1, INNER), 1)
    return [jnp.where(lane // HEAD == h, 1.0, 0.0).astype(F32) for h in range(HEADS)]


def head_mean_matrix():
    row = lax.broadcasted_iota(jnp.int32, (INNER, INNER), 0) // HEAD
    col = lax.broadcasted_iota(jnp.int32, (INNER, INNER), 1) // HEAD
    return jnp.where(row == col, 1.0 / HEAD, 0.0).astype(BF16)


def spread(values, masks):
    return jnp.concatenate([values * m.astype(values.dtype) for m in masks], axis=0)


def gathered(stacked, masks):
    total = stacked[:ROWS] * masks[0]
    for h in range(1, HEADS):
        total = total + stacked[h * ROWS : (h + 1) * ROWS] * masks[h]
    return total


def multiplicities(batch, tile_lists, counts, virtual):
    def times(tile, key_tile):
        seen = (virtual[batch] == key_tile).astype(F32)
        for slot in range(2):
            named = tile_lists[tile, slot, batch] == key_tile
            seen = seen + (named & (slot < counts[tile, batch])).astype(F32)
        return seen

    row = lax.broadcasted_iota(jnp.int32, (ROWS, ROWS), 0) < ROWS // 2
    col = lax.broadcasted_iota(jnp.int32, (ROWS, ROWS), 1) < ROWS // 2
    one = jnp.where(
        row,
        jnp.where(col, times(0, 0), times(0, 1)),
        jnp.where(col, times(1, 0), times(1, 1)),
    )
    return jnp.concatenate([one] * HEADS, axis=0)


def forward_layer(layer, hidden, weight, times, masks, mean_matrix, stash):
    widened = hidden.astype(F32)
    inverse = lax.rsqrt(jnp.mean(widened * widened, axis=-1, keepdims=True) + EPSILON)
    normed = (widened * inverse).astype(BF16)
    q = dot(normed, weight(0))
    k = dot(normed, weight(1))
    v = dot(normed, weight(2)).astype(BF16)
    scale_q = lax.rsqrt(dot((q * q).astype(BF16), mean_matrix) + EPSILON) * SCALE
    scale_k = lax.rsqrt(dot((k * k).astype(BF16), mean_matrix) + EPSILON)
    qn = (q * scale_q).astype(BF16)
    kn = (k * scale_k).astype(BF16)
    scores = dot(spread(qn, masks), kn, 1, 1)
    exponent = jnp.exp(scores) * times
    share = 1.0 / jnp.sum(exponent, axis=-1, keepdims=True)
    mixed = gathered(dot(exponent.astype(BF16), v) * share, masks).astype(BF16)
    attn = (exponent * share).astype(BF16)
    stash["normed"][layer] = normed
    stash["inverse"][layer] = jnp.broadcast_to(inverse, (ROWS, ROWS))
    stash["qkv"][layer, 0] = qn
    stash["qkv"][layer, 1] = kn
    stash["qkv"][layer, 2] = v
    stash["scales"][layer, 0] = scale_q
    stash["scales"][layer, 1] = scale_k
    stash["attn"][layer] = attn
    stash["mixed"][layer] = mixed
    out = weight(3)
    added = jnp.concatenate([dot(mixed, out[:INNER]), dot(mixed, out[INNER:])], axis=1)
    return (widened + added).astype(BF16)


def backward_layer(layer, grad, weight, masks, mean_matrix, stash):
    inverse = stash["inverse"][layer][:, :1]
    qn = stash["qkv"][layer, 0]
    kn = stash["qkv"][layer, 1]
    v = stash["qkv"][layer, 2]
    attn = stash["attn"][layer]
    out = weight(3)
    low, high = grad[:, :INNER], grad[:, INNER:]
    grad_mixed = (dot(low, out[:INNER], 1, 1) + dot(high, out[INNER:], 1, 1)).astype(BF16)
    stacked = spread(grad_mixed, masks)
    grad_attn = dot(stacked, v, 1, 1)
    attn_wide = attn.astype(F32)
    product = grad_mixed.astype(F32) * stash["mixed"][layer].astype(F32)
    inner = jnp.concatenate([jnp.sum(product * m, axis=-1, keepdims=True) for m in masks], axis=0)
    grad_scores = (attn_wide * (grad_attn - inner)).astype(BF16)
    grad_v = dot(attn, stacked, 0, 0).astype(BF16)
    grad_qn = gathered(dot(grad_scores, kn), masks)
    grad_kn = dot(grad_scores, spread(qn, masks), 0, 0)
    qw, kw = qn.astype(F32), kn.astype(F32)
    mean_q = dot((grad_qn * qw).astype(BF16), mean_matrix) * (1.0 / (SCALE * SCALE))
    mean_k = dot((grad_kn * kw).astype(BF16), mean_matrix)
    grad_q = (stash["scales"][layer, 0] * (grad_qn - qw * mean_q)).astype(BF16)
    grad_k = (stash["scales"][layer, 1] * (grad_kn - kw * mean_k)).astype(BF16)
    grad_normed = dot(grad_q, weight(0), 1, 1) + dot(grad_k, weight(1), 1, 1) + dot(grad_v, weight(2), 1, 1)
    wide = stash["normed"][layer].astype(F32)
    mean = jnp.mean(grad_normed * wide, axis=-1, keepdims=True)
    result = (grad.astype(F32) + inverse * (grad_normed - wide * mean)).astype(BF16)
    return result, jnp.concatenate([grad_q, grad_k, grad_v], axis=1)


class Weights:
    def __init__(self, own, beside, near2, far2, near3, far3, place, sems, me, core, order):
        self.place, self.me, self.order = place, me, order

        def halves(r, near, far):
            return [(near, place.at[r, pl.ds(2 * core, 2)]), (far, place.at[r, pl.ds(2 * (1 - core), 2)])]

        pairs = [
            [(own, place.at[0])],
            [(beside, place.at[1])],
            halves(2, near2, far2),
            halves(3, near3, far3),
        ]
        self.copies = [
            [pltpu.make_async_copy(src, dst, sems.at[r, i]) for i, (src, dst) in enumerate(listed)]
            for r, listed in enumerate(pairs)
        ]

    def each(self, layer, act):
        for r in range(STAGE_LAYERS):

            @pl.when((layer ^ self.me) == r)
            def _(r=r):
                for copy in self.copies[r]:
                    act(copy)

    def start(self):
        for layer in self.order:
            self.each(layer, lambda copy: copy.start())

    def wait(self, layer):
        self.each(layer, lambda copy: copy.wait())

    def layer(self, index):
        r = index ^ self.me
        return lambda block: self.place[r, block]


class Sheets:
    def __init__(self, names, outside, inside, sems, inward):
        self.copies = []
        for layer in range(STAGE_LAYERS):
            listed = []
            for i in range(len(names)):
                a, b = outside[i].at[layer], inside[i].at[layer]
                listed.append(pltpu.make_async_copy(*((a, b) if inward else (b, a)), sems.at[i, layer]))
            self.copies.append(listed)
        self.refs = dict(zip(names, inside))

    def start(self, layer):
        for copy in self.copies[layer]:
            copy.start()

    def wait(self, layer):
        for copy in self.copies[layer]:
            copy.wait()


def weight_gradients(slot, normed, mixed, grad_qkv, grad_out, place, core):
    full = dot(normed, grad_qkv, 0, 0).astype(BF16)
    for block in range(3):
        place[(block // 2) ^ core, slot, block % 2] = full[:, block * INNER : (block + 1) * INNER]
    last = dot(mixed, grad_out, 0, 0).astype(BF16)
    place[1 ^ core, slot, 1, :INNER] = last[:, :INNER]
    place[1 ^ core, slot, 1, INNER:] = last[:, INNER:]


def both(a, b):
    return jnp.concatenate([a, b], axis=0)


class Results:
    def __init__(self, outs, place, sems):
        self.copies = [
            [pltpu.make_async_copy(place.at[side, slot], outs[side].at[slot], sems.at[side, slot]) for side in range(2)]
            for slot in range(2)
        ]

    def start(self, slot):
        for copy in self.copies[slot]:
            copy.start()

    def wait(self, slot):
        for copy in self.copies[slot]:
            copy.wait()


def pack_kernel(info, qkv, out, own, half, sems):
    blocks = [[(qkv.at[0, :, pl.ds(b * INNER, INNER)], slice(None))] for b in range(3)]
    blocks.append([(out.at[0, :, pl.ds(i * INNER, INNER)], pl.ds(i * INNER, INNER)) for i in range(2)])
    copies = []
    for block in range(4):
        for i, (source, rows) in enumerate(blocks[block]):
            copies.append(pltpu.make_async_copy(source, own.at[block, rows], sems.at[0, block + i]))
    for copy in copies:
        copy.start()
    for side in range(2):

        @pl.when(info[2] == side)
        def _(side=side):
            chosen = []
            for slot in range(2):
                for i, (source, rows) in enumerate(blocks[2 * side + slot]):
                    chosen.append(pltpu.make_async_copy(source, half.at[slot, rows], sems.at[1, slot + i]))
            for copy in chosen:
                copy.start()
            for copy in chosen:
                copy.wait()

    for copy in copies:
        copy.wait()


def unpack_kernel(info, mine, other, qkv, out, sems):
    for side in range(2):

        @pl.when(info[2] == side)
        def _(side=side):
            low, high = (mine, other) if side == 0 else (other, mine)
            pairs = [
                (low.at[0], qkv.at[0, :, pl.ds(0, INNER)]),
                (low.at[1], qkv.at[0, :, pl.ds(INNER, INNER)]),
                (high.at[0], qkv.at[0, :, pl.ds(2 * INNER, INNER)]),
                (high.at[1, pl.ds(0, INNER)], out.at[0, :, pl.ds(0, INNER)]),
                (high.at[1, pl.ds(INNER, INNER)], out.at[0, :, pl.ds(INNER, INNER)]),
            ]
            copies = [pltpu.make_async_copy(src, dst, sems.at[i]) for i, (src, dst) in enumerate(pairs)]
            for copy in copies:
                copy.start()
            for copy in copies:
                copy.wait()


def forward_kernel(info, tile_lists, counts, virtual, hidden_in, *rest):
    weights = Weights(*rest[:6], *rest[-4:-2], info[1], info[2], range(STAGE_LAYERS))
    hidden_out, outside, inside = rest[6], rest[7 : 7 + len(STASH)], rest[7 + len(STASH) : 7 + 2 * len(STASH)]
    sheets = Sheets(STASH, outside, inside, rest[-2], False)
    weights.start()
    masks, mean_matrix = head_masks(), head_mean_matrix()
    times = rest[-1]
    times[...] = multiplicities(info[0], tile_lists, counts, virtual)
    hidden = hidden_in[0]
    for layer in range(STAGE_LAYERS):
        weights.wait(layer)
        hidden = forward_layer(layer, hidden, weights.layer(layer), times[...], masks, mean_matrix, sheets.refs)
        sheets.start(layer)
    hidden_out[...] = hidden
    for layer in range(STAGE_LAYERS):
        sheets.wait(layer)


def run_chain(hidden, grad, weights, times, masks, mean_matrix, stash, terms_qkv, terms_out, done):
    for layer in range(STAGE_LAYERS):
        weights.wait(layer)
        hidden = forward_layer(layer, hidden, weights.layer(layer), times[...], masks, mean_matrix, stash)
    for layer in reversed(range(STAGE_LAYERS)):
        terms_out[layer] = grad
        grad, grad_qkv = backward_layer(layer, grad, weights.layer(layer), masks, mean_matrix, stash)
        terms_qkv[layer] = grad_qkv
        done(layer)
    return grad


def middle_kernel(info, tile_lists, counts, virtual, hidden_in, grad_in, nodes_in, *rest):
    given, grad_out, rest = rest[:6], rest[6], rest[7:]
    terms_outside, stash_outside, inside = rest[: len(TERMS)], rest[len(TERMS) :][: len(STASH)], rest[len(TERMS) + len(STASH) :]
    stash_inside, (terms_qkv, terms_out) = inside[: len(STASH)], inside[len(STASH) :][:2]
    place, weight_sems, terms_sems, stash_sems, times = inside[len(STASH) + 2 :]
    weights = Weights(*given, place, weight_sems, info[1], info[2], range(STAGE_LAYERS))
    stash = dict(zip(STASH, stash_inside))
    weights.start()
    masks, mean_matrix = head_masks(), head_mean_matrix()

    @pl.when(info[3] == 1)
    def _():
        times[...] = multiplicities(info[0], tile_lists, counts, virtual)
        sheets = Sheets(TERMS, terms_outside, (stash["normed"], stash["mixed"], terms_qkv, terms_out), terms_sems, False)
        grad_out[...] = run_chain(
            hidden_in[...], grad_in[0], weights, times, masks, mean_matrix, stash, terms_qkv, terms_out, sheets.start
        )
        for layer in range(STAGE_LAYERS):
            sheets.wait(layer)

    @pl.when(info[3] == 0)
    def _():
        times[...] = multiplicities(info[4], tile_lists, counts, virtual)
        sheets = Sheets(STASH, stash_outside, stash_inside, stash_sems, False)
        hidden = nodes_in[0]
        for layer in range(STAGE_LAYERS):
            weights.wait(layer)
            hidden = forward_layer(layer, hidden, weights.layer(layer), times[...], masks, mean_matrix, stash)
            sheets.start(layer)
        for layer in range(STAGE_LAYERS):
            sheets.wait(layer)


def later_kernel(info, tile_lists, counts, virtual, hidden_in, grad_in, *rest):
    given, outside, outs, inside = rest[:6], rest[6:10], rest[10:12], rest[12:]
    stash = dict(zip(STASH, inside[: len(STASH)]))
    terms_qkv, terms_out, *first = inside[len(STASH) :][:6]
    weight_place, weight_sems, place, terms_sems, out_sems, times = inside[len(STASH) + 6 :]
    low = 2 * info[5]
    copies = [
        pltpu.make_async_copy(outside[i].at[low + slot], first[i].at[slot], terms_sems.at[i, slot])
        for i in range(len(TERMS))
        for slot in range(2)
    ]
    weights = Weights(*given, weight_place, weight_sems, info[1], info[2], range(STAGE_LAYERS))
    weights.start()
    for copy in copies:
        copy.start()
    masks, mean_matrix = head_masks(), head_mean_matrix()
    times[...] = multiplicities(info[4], tile_lists, counts, virtual)
    run_chain(
        hidden_in[...], grad_in[0], weights, times, masks, mean_matrix, stash, terms_qkv, terms_out, lambda layer: None
    )
    for copy in copies:
        copy.wait()
    results = Results(outs, place, out_sems)
    second = (stash["normed"], stash["mixed"], terms_qkv, terms_out)
    for slot in range(2):
        weight_gradients(slot, *(both(first[i][slot], second[i][low + slot]) for i in range(len(TERMS))), place, info[2])
        results.start(slot)
    for slot in range(2):
        results.wait(slot)


def backward_kernel(info, grad_in, grad_in2, *rest):
    order = tuple(reversed(range(STAGE_LAYERS)))
    count = len(STASH)
    outside, outside2, given, outs = rest[:count], rest[count:][:count], rest[2 * count :][:6], rest[2 * count + 6 :][:2]
    inside = rest[2 * count + 8 :]
    weight_place, weight_sems, place, kept_qkv, kept_out, sems, sems2, out_sems = inside[2 * count :]
    weights = Weights(*given, weight_place, weight_sems, info[1], info[2], order)
    sheets = [
        Sheets(STASH, outside, inside[:count], sems, True),
        Sheets(STASH, outside2, inside[count:][:count], sems2, True),
    ]
    results = Results(outs, place, out_sems)
    for layer in order:
        for one in sheets:
            one.start(layer)
        weights.each(layer, lambda copy: copy.start())
    masks, mean_matrix = head_masks(), head_mean_matrix()

    def step(layer, grads):
        for one in sheets:
            one.wait(layer)
        weights.wait(layer)
        return tuple(
            zip(*(backward_layer(layer, g, weights.layer(layer), masks, mean_matrix, one.refs) for g, one in zip(grads, sheets)))
        )

    def finish(layer, grad_qkv, grad_out):
        normed, mixed = (both(*(one.refs[n][layer] for one in sheets)) for n in ("normed", "mixed"))
        weight_gradients(layer % 2, normed, mixed, grad_qkv, grad_out, place, info[2])
        results.start(layer % 2)

    grads = (grad_in[...], grad_in2[...])
    for layer in (3, 2):
        kept_out[layer - 2] = both(*grads)
        grads, terms = step(layer, grads)
        kept_qkv[layer - 2] = both(*terms)
    kept_out[2] = both(*grads)

    @pl.when(info[5] == 1)
    def _():
        for layer in (3, 2):
            finish(layer, kept_qkv[layer - 2], kept_out[layer - 2])
        for layer in (1, 0):
            for one in sheets:
                one.wait(layer)
            weights.wait(layer)

    @pl.when(info[5] == 0)
    def _():
        now = (kept_out[2, :ROWS], kept_out[2, ROWS:])
        for layer in (1, 0):
            before = both(*now)
            now, terms = step(layer, now)
            finish(layer, both(*terms), before)

    for slot in range(2):
        results.wait(slot)


ANYWHERE = pl.BlockSpec(memory_space=pl.ANY)
IN_HBM = pl.BlockSpec(memory_space=pltpu.HBM)
HIDDEN = jax.ShapeDtypeStruct((ROWS, D), BF16)
HIDDEN_BLOCK = pl.BlockSpec((ROWS, D), lambda *_: (0, 0))
BATCH_BLOCK = pl.BlockSpec((1, ROWS, D), lambda step, info, *_: (info[0], 0, 0))
SECOND_BLOCK = pl.BlockSpec((1, ROWS, D), lambda step, info, *_: (info[4], 0, 0))
GRAD_HALF = jax.ShapeDtypeStruct((2, 2, D, INNER), BF16)
WEIGHT_SCRATCH = [
    pltpu.VMEM((STAGE_LAYERS, 4, D, INNER), BF16),
    pltpu.SemaphoreType.DMA((STAGE_LAYERS, 2)),
]
GRAD_PLACE = pltpu.VMEM((2, 2, 2, D, INNER), BF16)
TIMES = pltpu.VMEM((HEADS * ROWS, ROWS), F32)


def layered(sizes, make):
    return [make((STAGE_LAYERS, *shape), kind) for shape, kind in sizes.values()]


def semaphores(count):
    return pltpu.SemaphoreType.DMA((count, STAGE_LAYERS))


def call(kernel, prefetched, in_specs, out_specs, out_shape, scratch, args, megabytes=48):
    return pl.pallas_call(
        kernel,
        grid_spec=pltpu.PrefetchScalarGridSpec(
            num_scalar_prefetch=prefetched,
            grid=(1,),
            in_specs=in_specs,
            out_specs=out_specs,
            scratch_shapes=scratch,
        ),
        out_shape=out_shape,
        compiler_params=pltpu.CompilerParams(vmem_limit_bytes=megabytes * 2**20),
    )(*args)


def run_pack(info, w_qkv, w_out):
    shapes = [jax.ShapeDtypeStruct((blocks, D, INNER), BF16) for blocks in (4, 2)]
    sems = [pltpu.SemaphoreType.DMA((2, 5))]
    return call(pack_kernel, 1, [IN_HBM] * 2, [ANYWHERE] * 2, shapes, sems, (info, w_qkv, w_out), 1)


def run_unpack(info, mine, other):
    shapes = [jax.ShapeDtypeStruct((1, *shape), BF16) for shape in ((D, 3 * INNER), (INNER, D))]
    sems = [pltpu.SemaphoreType.DMA((5,))]
    return call(unpack_kernel, 1, [ANYWHERE] * 2, [IN_HBM] * 2, shapes, sems, (info, mine, other), 1)


def run_forward(info, tables, nodes, weights):
    return call(
        forward_kernel,
        4,
        [BATCH_BLOCK] + [ANYWHERE] * 6,
        [HIDDEN_BLOCK] + [ANYWHERE] * len(STASH),
        [HIDDEN] + layered(STASH, jax.ShapeDtypeStruct),
        layered(STASH, pltpu.VMEM) + WEIGHT_SCRATCH + [semaphores(len(STASH)), TIMES],
        (info, *tables, nodes, *weights),
        58,
    )


def run_middle(info, tables, hidden, cotangent, nodes, weights):
    return call(
        middle_kernel,
        4,
        [HIDDEN_BLOCK, BATCH_BLOCK, SECOND_BLOCK] + [ANYWHERE] * 6,
        [HIDDEN_BLOCK] + [ANYWHERE] * (len(TERMS) + len(STASH)),
        [HIDDEN] + layered(TERMS, jax.ShapeDtypeStruct) + layered(STASH, jax.ShapeDtypeStruct),
        layered(STASH, pltpu.VMEM)
        + layered(TERMS, pltpu.VMEM)[2:]
        + WEIGHT_SCRATCH
        + [semaphores(len(TERMS)), semaphores(len(STASH)), TIMES],
        (info, *tables, hidden, cotangent, nodes, *weights),
        50,
    )


def run_later(info, tables, hidden, cotangent, weights, terms):
    return call(
        later_kernel,
        4,
        [HIDDEN_BLOCK, SECOND_BLOCK] + [ANYWHERE] * (6 + len(TERMS)),
        [ANYWHERE] * 2,
        [GRAD_HALF] * 2,
        layered(STASH, pltpu.VMEM)
        + layered(TERMS, pltpu.VMEM)[2:]
        + [pltpu.VMEM((2, *shape), kind) for shape, kind in TERMS.values()]
        + WEIGHT_SCRATCH
        + [GRAD_PLACE, pltpu.SemaphoreType.DMA((len(TERMS), 2)), pltpu.SemaphoreType.DMA((2, 2)), TIMES],
        (info, *tables, hidden, cotangent, *weights, *terms),
    )


def run_backward(info, grads, stash, stash2, weights):
    return call(
        backward_kernel,
        1,
        [HIDDEN_BLOCK] * 2 + [ANYWHERE] * (2 * len(STASH) + 6),
        [ANYWHERE] * 2,
        [GRAD_HALF] * 2,
        layered(STASH, pltpu.VMEM) * 2
        + WEIGHT_SCRATCH
        + [GRAD_PLACE, pltpu.VMEM((2, 2 * ROWS, 3 * INNER), BF16), pltpu.VMEM((3, 2 * ROWS, D), BF16)]
        + [semaphores(len(STASH)), semaphores(len(STASH)), pltpu.SemaphoreType.DMA((2, 2))],
        (info, *grads, *stash, *stash2, *weights),
    )


def swapped(value, axis):
    return lax.ppermute(value, axis, [(0, 1), (1, 0)])


def fetched(value, flip_y, flip_x):
    axes = ("yl", "xl", "xh", "core")
    pairs = []
    for y in range(2):
        for x in range(2):
            for upper in range(2):
                for core in range(2):
                    there = upper ^ (core if flip_x else 0)
                    source = ((y * 2 + x) * 2 + upper) * 2 + core
                    target = (((y ^ flip_y) * 2 + (x ^ flip_x)) * 2 + there) * 2 + core
                    pairs.append((source, target))
    return lax.ppermute(value, axes, pairs)


def per_device(nodes, cotangent, w_qkv, w_out, tile_lists, counts, virtual):
    stage = lax.axis_index("yh")
    y, x, core = lax.axis_index("yl"), lax.axis_index("xl"), lax.axis_index("core")
    me = y * 2 + x
    batch = jnp.where(stage == 0, y, 1 - y) * 2 + x
    info = jnp.stack([batch, me, core, stage, batch ^ 2, y]).astype(jnp.int32)
    tables = (tile_lists.transpose(1, 2, 0), counts.transpose(1, 0), virtual)
    own, half = run_pack(info, w_qkv, w_out)
    near2 = fetched(half, 1, 0)
    near3 = fetched(half, 1, 1)
    beside = fetched(own, 0, 1)
    far2, far3 = swapped(near2, "core"), swapped(near3, "core")
    weights = (own, beside, near2, far2, near3, far3)

    hidden, *stash = run_forward(info, tables, nodes, weights)
    pair = ("yh", "yl")
    across, crossed = [(0, 3), (1, 2), (2, 1), (3, 0)], [(0, 2), (1, 3), (2, 0), (3, 1)]
    first, second = lax.ppermute(hidden, pair, across), lax.ppermute(hidden, pair, crossed)
    grad, *rest = run_middle(info, tables, first, cotangent, nodes, weights)
    terms, stash2 = rest[: len(TERMS)], rest[len(TERMS) :]
    grads = (lax.ppermute(grad, pair, across), lax.ppermute(grad, pair, crossed))
    keep, send = lax.cond(
        stage == 0,
        lambda: tuple(run_backward(info, grads, stash, stash2, weights)),
        lambda: tuple(run_later(info, tables, second, cotangent, weights, terms)),
    )

    def added(value, axis):
        return jnp.sum(value.astype(F32), axis=axis).astype(BF16)

    def repeated(value, times):
        return jnp.broadcast_to(value, (times, *value.shape))

    far, near = lax.axis_size("zh"), lax.axis_size("zl")
    piece = D // near
    total = (keep.astype(F32) + swapped(send, "core").astype(F32)).astype(BF16)
    total = lax.all_to_all(total.reshape(4, D, INNER), ("xl", "xh"), 0, 0, tiled=True)
    total = added(total, 0).reshape(near, piece, INNER)
    total = added(lax.all_to_all(total, "zl", 0, 0, tiled=True), 0)
    total = added(lax.all_to_all(repeated(total, far), "zh", 0, 0, tiled=True), 0)
    total = lax.all_to_all(repeated(total, 2 * near), ("xh", "zl"), 0, 0, tiled=True)
    mine = total.reshape(2, D, INNER)
    grad_qkv, grad_out = run_unpack(info, mine, swapped(mine, "core"))
    return (grad_qkv, grad_out)


def solution(mesh):
    depth = mesh.shape["dp"] // 4
    near = min(depth, 4)
    names = ("yh", "yl", "xl", "zh", "zl", "xh", "core")
    cut = Mesh(mesh.devices.reshape(2, 2, 2, depth // near, near, 2, 2), names)
    section, dp = P(("yh", "yl", "xl")), P(("zh", "zl", "xh", "core"))
    return jax.shard_map(
        per_device,
        mesh=cut,
        in_specs=(dp, dp, section, section, dp, dp, dp),
        out_specs=(section, section),
        check_vma=False,
    )
```

```python
import functools

import jax
import jax.numpy as jnp
from jax import lax
from jax.experimental import pallas as pl
from jax.experimental.pallas import tpu as pltpu
from jax.sharding import Mesh
from jax.sharding import PartitionSpec as P

HEADS = 4
EPSILON = 1e-06
TEMPER = 4.0
D = 512
INNER = 256
ROWS = 128
HEAD = INNER // HEADS
SCALE = TEMPER / HEAD
STAGE_LAYERS = 4
F32 = jnp.float32
BF16 = jnp.bfloat16
STASH = {
    "normed": ((ROWS, D), BF16),
    "inverse": ((ROWS, ROWS), F32),
    "qkv": ((3, ROWS, INNER), BF16),
    "scales": ((2, ROWS, INNER), F32),
    "attn": ((HEADS * ROWS, ROWS), BF16),
    "mixed": ((ROWS, INNER), BF16),
}
TERMS = {
    "normed": ((ROWS, D), BF16),
    "mixed": ((ROWS, INNER), BF16),
    "grad_qkv": ((ROWS, 3 * INNER), BF16),
    "grad_out": ((ROWS, D), BF16),
}


def dot(a, b, over_a=1, over_b=0):
    return lax.dot_general(a, b, (((over_a,), (over_b,)), ((), ())), preferred_element_type=F32)


def head_masks():
    lane = lax.broadcasted_iota(jnp.int32, (1, INNER), 1)
    return [jnp.where(lane // HEAD == h, 1.0, 0.0).astype(F32) for h in range(HEADS)]


def head_mean_matrix():
    row = lax.broadcasted_iota(jnp.int32, (INNER, INNER), 0) // HEAD
    col = lax.broadcasted_iota(jnp.int32, (INNER, INNER), 1) // HEAD
    return jnp.where(row == col, 1.0 / HEAD, 0.0).astype(BF16)


def spread(values, masks):
    return jnp.concatenate([values * m.astype(values.dtype) for m in masks], axis=0)


def gathered(stacked, masks):
    total = stacked[:ROWS] * masks[0]
    for h in range(1, HEADS):
        total = total + stacked[h * ROWS : (h + 1) * ROWS] * masks[h]
    return total


def multiplicities(batch, tile_lists, counts, virtual):
    def times(tile, key_tile):
        seen = (virtual[batch] == key_tile).astype(F32)
        for slot in range(2):
            named = tile_lists[tile, slot, batch] == key_tile
            seen = seen + (named & (slot < counts[tile, batch])).astype(F32)
        return seen

    row = lax.broadcasted_iota(jnp.int32, (ROWS, ROWS), 0) < ROWS // 2
    col = lax.broadcasted_iota(jnp.int32, (ROWS, ROWS), 1) < ROWS // 2
    one = jnp.where(
        row,
        jnp.where(col, times(0, 0), times(0, 1)),
        jnp.where(col, times(1, 0), times(1, 1)),
    )
    return jnp.concatenate([one] * HEADS, axis=0)


def forward_layer(layer, hidden, weight, times, masks, mean_matrix, stash):
    widened = hidden.astype(F32)
    inverse = lax.rsqrt(jnp.mean(widened * widened, axis=-1, keepdims=True) + EPSILON)
    normed = (widened * inverse).astype(BF16)
    q = dot(normed, weight(0))
    k = dot(normed, weight(1))
    v = dot(normed, weight(2)).astype(BF16)
    scale_q = lax.rsqrt(dot((q * q).astype(BF16), mean_matrix) + EPSILON) * SCALE
    scale_k = lax.rsqrt(dot((k * k).astype(BF16), mean_matrix) + EPSILON)
    qn = (q * scale_q).astype(BF16)
    kn = (k * scale_k).astype(BF16)
    scores = dot(spread(qn, masks), kn, 1, 1)
    exponent = jnp.exp(scores) * times
    share = 1.0 / jnp.sum(exponent, axis=-1, keepdims=True)
    mixed = gathered(dot(exponent.astype(BF16), v) * share, masks).astype(BF16)
    attn = (exponent * share).astype(BF16)
    stash["normed"][layer] = normed
    stash["inverse"][layer] = jnp.broadcast_to(inverse, (ROWS, ROWS))
    stash["qkv"][layer, 0] = qn
    stash["qkv"][layer, 1] = kn
    stash["qkv"][layer, 2] = v
    stash["scales"][layer, 0] = scale_q
    stash["scales"][layer, 1] = scale_k
    stash["attn"][layer] = attn
    stash["mixed"][layer] = mixed
    out = weight(3)
    added = jnp.concatenate([dot(mixed, out[:INNER]), dot(mixed, out[INNER:])], axis=1)
    return (widened + added).astype(BF16)


def backward_layer(layer, grad, weight, masks, mean_matrix, stash):
    inverse = stash["inverse"][layer][:, :1]
    qn = stash["qkv"][layer, 0]
    kn = stash["qkv"][layer, 1]
    v = stash["qkv"][layer, 2]
    attn = stash["attn"][layer]
    out = weight(3)
    low, high = grad[:, :INNER], grad[:, INNER:]
    grad_mixed = (dot(low, out[:INNER], 1, 1) + dot(high, out[INNER:], 1, 1)).astype(BF16)
    stacked = spread(grad_mixed, masks)
    grad_attn = dot(stacked, v, 1, 1)
    attn_wide = attn.astype(F32)
    product = grad_mixed.astype(F32) * stash["mixed"][layer].astype(F32)
    inner = jnp.concatenate([jnp.sum(product * m, axis=-1, keepdims=True) for m in masks], axis=0)
    grad_scores = (attn_wide * (grad_attn - inner)).astype(BF16)
    grad_v = dot(attn, stacked, 0, 0).astype(BF16)
    grad_qn = gathered(dot(grad_scores, kn), masks)
    grad_kn = dot(grad_scores, spread(qn, masks), 0, 0)
    qw, kw = qn.astype(F32), kn.astype(F32)
    mean_q = dot((grad_qn * qw).astype(BF16), mean_matrix) * (1.0 / (SCALE * SCALE))
    mean_k = dot((grad_kn * kw).astype(BF16), mean_matrix)
    grad_q = (stash["scales"][layer, 0] * (grad_qn - qw * mean_q)).astype(BF16)
    grad_k = (stash["scales"][layer, 1] * (grad_kn - kw * mean_k)).astype(BF16)
    grad_normed = dot(grad_q, weight(0), 1, 1) + dot(grad_k, weight(1), 1, 1) + dot(grad_v, weight(2), 1, 1)
    wide = stash["normed"][layer].astype(F32)
    mean = jnp.mean(grad_normed * wide, axis=-1, keepdims=True)
    result = (grad.astype(F32) + inverse * (grad_normed - wide * mean)).astype(BF16)
    return result, jnp.concatenate([grad_q, grad_k, grad_v], axis=1)


class Weights:
    def __init__(self, own, beside, near2, far2, near3, far3, place, sems, me, core, order):
        self.place, self.me, self.order = place, me, order

        def halves(r, near, far):
            return [(near, place.at[r, pl.ds(2 * core, 2)]), (far, place.at[r, pl.ds(2 * (1 - core), 2)])]

        pairs = [
            [(own, place.at[0])],
            [(beside, place.at[1])],
            halves(2, near2, far2),
            halves(3, near3, far3),
        ]
        self.copies = [
            [pltpu.make_async_copy(src, dst, sems.at[r, i]) for i, (src, dst) in enumerate(listed)]
            for r, listed in enumerate(pairs)
        ]

    def each(self, layer, act):
        for r in range(STAGE_LAYERS):

            @pl.when((layer ^ self.me) == r)
            def _(r=r):
                for copy in self.copies[r]:
                    act(copy)

    def start(self):
        for layer in self.order:
            self.each(layer, lambda copy: copy.start())

    def wait(self, layer):
        self.each(layer, lambda copy: copy.wait())

    def layer(self, index):
        r = index ^ self.me
        return lambda block: self.place[r, block]


class Sheets:
    def __init__(self, names, outside, inside, sems, inward):
        self.copies = []
        for layer in range(STAGE_LAYERS):
            listed = []
            for i in range(len(names)):
                a, b = outside[i].at[layer], inside[i].at[layer]
                listed.append(pltpu.make_async_copy(*((a, b) if inward else (b, a)), sems.at[i, layer]))
            self.copies.append(listed)
        self.refs = dict(zip(names, inside))

    def start(self, layer):
        for copy in self.copies[layer]:
            copy.start()

    def wait(self, layer):
        for copy in self.copies[layer]:
            copy.wait()


def weight_gradients(slot, normed, mixed, grad_qkv, grad_out, place, core):
    full = dot(normed, grad_qkv, 0, 0).astype(BF16)
    for block in range(3):
        place[(block // 2) ^ core, slot, block % 2] = full[:, block * INNER : (block + 1) * INNER]
    last = dot(mixed, grad_out, 0, 0).astype(BF16)
    place[1 ^ core, slot, 1, :INNER] = last[:, :INNER]
    place[1 ^ core, slot, 1, INNER:] = last[:, INNER:]


def both(a, b):
    return jnp.concatenate([a, b], axis=0)


class Results:
    def __init__(self, outs, place, sems):
        self.copies = [
            [pltpu.make_async_copy(place.at[side, slot], outs[side].at[slot], sems.at[side, slot]) for side in range(2)]
            for slot in range(2)
        ]

    def start(self, slot):
        for copy in self.copies[slot]:
            copy.start()

    def wait(self, slot):
        for copy in self.copies[slot]:
            copy.wait()


def pack_kernel(info, qkv, out, own, half, sems):
    blocks = [[(qkv.at[0, :, pl.ds(b * INNER, INNER)], slice(None))] for b in range(3)]
    blocks.append([(out.at[0, :, pl.ds(i * INNER, INNER)], pl.ds(i * INNER, INNER)) for i in range(2)])
    copies = []
    for block in range(4):
        for i, (source, rows) in enumerate(blocks[block]):
            copies.append(pltpu.make_async_copy(source, own.at[block, rows], sems.at[0, block + i]))
    for copy in copies:
        copy.start()
    for side in range(2):

        @pl.when(info[2] == side)
        def _(side=side):
            chosen = []
            for slot in range(2):
                for i, (source, rows) in enumerate(blocks[2 * side + slot]):
                    chosen.append(pltpu.make_async_copy(source, half.at[slot, rows], sems.at[1, slot + i]))
            for copy in chosen:
                copy.start()
            for copy in chosen:
                copy.wait()

    for copy in copies:
        copy.wait()


def unpack_kernel(info, mine, other, qkv, out, sems):
    for side in range(2):

        @pl.when(info[2] == side)
        def _(side=side):
            low, high = (mine, other) if side == 0 else (other, mine)
            pairs = [
                (low.at[0], qkv.at[0, :, pl.ds(0, INNER)]),
                (low.at[1], qkv.at[0, :, pl.ds(INNER, INNER)]),
                (high.at[0], qkv.at[0, :, pl.ds(2 * INNER, INNER)]),
                (high.at[1, pl.ds(0, INNER)], out.at[0, :, pl.ds(0, INNER)]),
                (high.at[1, pl.ds(INNER, INNER)], out.at[0, :, pl.ds(INNER, INNER)]),
            ]
            copies = [pltpu.make_async_copy(src, dst, sems.at[i]) for i, (src, dst) in enumerate(pairs)]
            for copy in copies:
                copy.start()
            for copy in copies:
                copy.wait()


def forward_kernel(info, tile_lists, counts, virtual, hidden_in, *rest):
    weights = Weights(*rest[:6], *rest[-4:-2], info[1], info[2], range(STAGE_LAYERS))
    hidden_out, outside, inside = rest[6], rest[7 : 7 + len(STASH)], rest[7 + len(STASH) : 7 + 2 * len(STASH)]
    sheets = Sheets(STASH, outside, inside, rest[-2], False)
    weights.start()
    masks, mean_matrix = head_masks(), head_mean_matrix()
    times = rest[-1]
    times[...] = multiplicities(info[0], tile_lists, counts, virtual)
    hidden = hidden_in[0]
    for layer in range(STAGE_LAYERS):
        weights.wait(layer)
        hidden = forward_layer(layer, hidden, weights.layer(layer), times[...], masks, mean_matrix, sheets.refs)
        sheets.start(layer)
    hidden_out[...] = hidden
    for layer in range(STAGE_LAYERS):
        sheets.wait(layer)


def run_chain(hidden, grad, weights, times, masks, mean_matrix, stash, terms_qkv, terms_out, done):
    for layer in range(STAGE_LAYERS):
        weights.wait(layer)
        hidden = forward_layer(layer, hidden, weights.layer(layer), times[...], masks, mean_matrix, stash)
    for layer in reversed(range(STAGE_LAYERS)):
        terms_out[layer] = grad
        grad, grad_qkv = backward_layer(layer, grad, weights.layer(layer), masks, mean_matrix, stash)
        terms_qkv[layer] = grad_qkv
        done(layer)
    return grad


def middle_kernel(info, tile_lists, counts, virtual, hidden_in, sent, grad_in, nodes_in, *rest):
    given, grad_out, rest = rest[:6], rest[6], rest[7:]
    terms_outside, stash_outside, inside = rest[: len(TERMS)], rest[len(TERMS) :][: len(STASH)], rest[len(TERMS) + len(STASH) :]
    stash_inside, (terms_qkv, terms_out) = inside[: len(STASH)], inside[len(STASH) :][:2]
    place, weight_sems, terms_sems, stash_sems, times = inside[len(STASH) + 2 :]
    weights = Weights(*given, place, weight_sems, info[1], info[2], range(STAGE_LAYERS))
    stash = dict(zip(STASH, stash_inside))
    weights.start()
    masks, mean_matrix = head_masks(), head_mean_matrix()

    @pl.when(info[3] == 1)
    def _():
        times[...] = multiplicities(info[0], tile_lists, counts, virtual)
        sheets = Sheets(TERMS, terms_outside, (stash["normed"], stash["mixed"], terms_qkv, terms_out), terms_sems, False)
        grad_out[...] = run_chain(
            hidden_in[...], grad_in[0], weights, times, masks, mean_matrix, stash, terms_qkv, terms_out, sheets.start
        )
        for layer in range(STAGE_LAYERS):
            sheets.wait(layer)

    @pl.when(info[3] == 0)
    def _():
        times[...] = multiplicities(info[4], tile_lists, counts, virtual)
        sheets = Sheets(STASH, stash_outside, stash_inside, stash_sems, False)
        grad_out[...] = sent[...]
        hidden = nodes_in[0]
        for layer in range(STAGE_LAYERS):
            weights.wait(layer)
            hidden = forward_layer(layer, hidden, weights.layer(layer), times[...], masks, mean_matrix, stash)
            sheets.start(layer)
        for layer in range(STAGE_LAYERS):
            sheets.wait(layer)


def later_kernel(info, tile_lists, counts, virtual, hidden_in, grad_in, *rest):
    given, outside, outs, inside = rest[:6], rest[6:10], rest[10:12], rest[12:]
    stash = dict(zip(STASH, inside[: len(STASH)]))
    terms_qkv, terms_out, *first = inside[len(STASH) :][:6]
    weight_place, weight_sems, place, terms_sems, out_sems, times = inside[len(STASH) + 6 :]
    low = 2 * info[5]
    copies = [
        pltpu.make_async_copy(outside[i].at[low + slot], first[i].at[slot], terms_sems.at[i, slot])
        for i in range(len(TERMS))
        for slot in range(2)
    ]
    weights = Weights(*given, weight_place, weight_sems, info[1], info[2], range(STAGE_LAYERS))
    weights.start()
    for copy in copies:
        copy.start()
    masks, mean_matrix = head_masks(), head_mean_matrix()
    times[...] = multiplicities(info[4], tile_lists, counts, virtual)
    run_chain(
        hidden_in[...], grad_in[0], weights, times, masks, mean_matrix, stash, terms_qkv, terms_out, lambda layer: None
    )
    for copy in copies:
        copy.wait()
    results = Results(outs, place, out_sems)
    second = (stash["normed"], stash["mixed"], terms_qkv, terms_out)
    for slot in range(2):
        weight_gradients(slot, *(both(first[i][slot], second[i][low + slot]) for i in range(len(TERMS))), place, info[2])
        results.start(slot)
    for slot in range(2):
        results.wait(slot)


def backward_kernel(info, grad_in, grad_in2, *rest):
    order = tuple(reversed(range(STAGE_LAYERS)))
    count = len(STASH)
    outside, outside2, given, outs = rest[:count], rest[count:][:count], rest[2 * count :][:6], rest[2 * count + 6 :][:2]
    inside = rest[2 * count + 8 :]
    weight_place, weight_sems, place, kept_qkv, kept_out, sems, sems2, out_sems = inside[2 * count :]
    weights = Weights(*given, weight_place, weight_sems, info[1], info[2], order)
    sheets = [
        Sheets(STASH, outside, inside[:count], sems, True),
        Sheets(STASH, outside2, inside[count:][:count], sems2, True),
    ]
    results = Results(outs, place, out_sems)
    for layer in order:
        for one in sheets:
            one.start(layer)
        weights.each(layer, lambda copy: copy.start())
    masks, mean_matrix = head_masks(), head_mean_matrix()

    def step(layer, grads):
        for one in sheets:
            one.wait(layer)
        weights.wait(layer)
        return tuple(
            zip(*(backward_layer(layer, g, weights.layer(layer), masks, mean_matrix, one.refs) for g, one in zip(grads, sheets)))
        )

    def finish(layer, grad_qkv, grad_out):
        normed, mixed = (both(*(one.refs[n][layer] for one in sheets)) for n in ("normed", "mixed"))
        weight_gradients(layer % 2, normed, mixed, grad_qkv, grad_out, place, info[2])
        results.start(layer % 2)

    grads = (grad_in[...], grad_in2[...])
    for layer in (3, 2):
        kept_out[layer - 2] = both(*grads)
        grads, terms = step(layer, grads)
        kept_qkv[layer - 2] = both(*terms)
    kept_out[2] = both(*grads)

    @pl.when(info[5] == 1)
    def _():
        for layer in (3, 2):
            finish(layer, kept_qkv[layer - 2], kept_out[layer - 2])
        for layer in (1, 0):
            for one in sheets:
                one.wait(layer)
            weights.wait(layer)

    @pl.when(info[5] == 0)
    def _():
        now = (kept_out[2, :ROWS], kept_out[2, ROWS:])
        for layer in (1, 0):
            before = both(*now)
            now, terms = step(layer, now)
            finish(layer, both(*terms), before)

    for slot in range(2):
        results.wait(slot)


ANYWHERE = pl.BlockSpec(memory_space=pl.ANY)
IN_HBM = pl.BlockSpec(memory_space=pltpu.HBM)
HIDDEN = jax.ShapeDtypeStruct((ROWS, D), BF16)
HIDDEN_BLOCK = pl.BlockSpec((ROWS, D), lambda *_: (0, 0))
BATCH_BLOCK = pl.BlockSpec((1, ROWS, D), lambda step, info, *_: (info[0], 0, 0))
SECOND_BLOCK = pl.BlockSpec((1, ROWS, D), lambda step, info, *_: (info[4], 0, 0))
GRAD_HALF = jax.ShapeDtypeStruct((2, 2, D, INNER), BF16)
WEIGHT_SCRATCH = [
    pltpu.VMEM((STAGE_LAYERS, 4, D, INNER), BF16),
    pltpu.SemaphoreType.DMA((STAGE_LAYERS, 2)),
]
GRAD_PLACE = pltpu.VMEM((2, 2, 2, D, INNER), BF16)
TIMES = pltpu.VMEM((HEADS * ROWS, ROWS), F32)


def layered(sizes, make):
    return [make((STAGE_LAYERS, *shape), kind) for shape, kind in sizes.values()]


def semaphores(count):
    return pltpu.SemaphoreType.DMA((count, STAGE_LAYERS))


def call(kernel, prefetched, in_specs, out_specs, out_shape, scratch, args, megabytes=48):
    return pl.pallas_call(
        kernel,
        grid_spec=pltpu.PrefetchScalarGridSpec(
            num_scalar_prefetch=prefetched,
            grid=(1,),
            in_specs=in_specs,
            out_specs=out_specs,
            scratch_shapes=scratch,
        ),
        out_shape=out_shape,
        compiler_params=pltpu.CompilerParams(vmem_limit_bytes=megabytes * 2**20),
    )(*args)


def run_pack(info, w_qkv, w_out):
    shapes = [jax.ShapeDtypeStruct((blocks, D, INNER), BF16) for blocks in (4, 2)]
    sems = [pltpu.SemaphoreType.DMA((2, 5))]
    return call(pack_kernel, 1, [IN_HBM] * 2, [ANYWHERE] * 2, shapes, sems, (info, w_qkv, w_out), 1)


def run_unpack(info, mine, other):
    shapes = [jax.ShapeDtypeStruct((1, *shape), BF16) for shape in ((D, 3 * INNER), (INNER, D))]
    sems = [pltpu.SemaphoreType.DMA((5,))]
    return call(unpack_kernel, 1, [ANYWHERE] * 2, [IN_HBM] * 2, shapes, sems, (info, mine, other), 1)


def run_forward(info, tables, nodes, weights):
    return call(
        forward_kernel,
        4,
        [BATCH_BLOCK] + [ANYWHERE] * 6,
        [HIDDEN_BLOCK] + [ANYWHERE] * len(STASH),
        [HIDDEN] + layered(STASH, jax.ShapeDtypeStruct),
        layered(STASH, pltpu.VMEM) + WEIGHT_SCRATCH + [semaphores(len(STASH)), TIMES],
        (info, *tables, nodes, *weights),
        58,
    )


def run_middle(info, tables, hidden, sent, cotangent, nodes, weights):
    return call(
        middle_kernel,
        4,
        [HIDDEN_BLOCK, HIDDEN_BLOCK, BATCH_BLOCK, SECOND_BLOCK] + [ANYWHERE] * 6,
        [HIDDEN_BLOCK] + [ANYWHERE] * (len(TERMS) + len(STASH)),
        [HIDDEN] + layered(TERMS, jax.ShapeDtypeStruct) + layered(STASH, jax.ShapeDtypeStruct),
        layered(STASH, pltpu.VMEM)
        + layered(TERMS, pltpu.VMEM)[2:]
        + WEIGHT_SCRATCH
        + [semaphores(len(TERMS)), semaphores(len(STASH)), TIMES],
        (info, *tables, hidden, sent, cotangent, nodes, *weights),
        50,
    )


def run_later(info, tables, hidden, cotangent, weights, terms):
    return call(
        later_kernel,
        4,
        [HIDDEN_BLOCK, SECOND_BLOCK] + [ANYWHERE] * (6 + len(TERMS)),
        [ANYWHERE] * 2,
        [GRAD_HALF] * 2,
        layered(STASH, pltpu.VMEM)
        + layered(TERMS, pltpu.VMEM)[2:]
        + [pltpu.VMEM((2, *shape), kind) for shape, kind in TERMS.values()]
        + WEIGHT_SCRATCH
        + [GRAD_PLACE, pltpu.SemaphoreType.DMA((len(TERMS), 2)), pltpu.SemaphoreType.DMA((2, 2)), TIMES],
        (info, *tables, hidden, cotangent, *weights, *terms),
    )


def run_backward(info, grads, stash, stash2, weights):
    return call(
        backward_kernel,
        1,
        [HIDDEN_BLOCK] * 2 + [ANYWHERE] * (2 * len(STASH) + 6),
        [ANYWHERE] * 2,
        [GRAD_HALF] * 2,
        layered(STASH, pltpu.VMEM) * 2
        + WEIGHT_SCRATCH
        + [GRAD_PLACE, pltpu.VMEM((2, 2 * ROWS, 3 * INNER), BF16), pltpu.VMEM((3, 2 * ROWS, D), BF16)]
        + [semaphores(len(STASH)), semaphores(len(STASH)), pltpu.SemaphoreType.DMA((2, 2))],
        (info, *grads, *stash, *stash2, *weights),
    )


def swapped(value, axis):
    return lax.ppermute(value, axis, [(0, 1), (1, 0)])


def fetched(value, flip_y, flip_x):
    axes = ("yl", "xl", "xh", "core")
    pairs = []
    for y in range(2):
        for x in range(2):
            for upper in range(2):
                for core in range(2):
                    there = upper ^ (core if flip_x else 0)
                    source = ((y * 2 + x) * 2 + upper) * 2 + core
                    target = (((y ^ flip_y) * 2 + (x ^ flip_x)) * 2 + there) * 2 + core
                    pairs.append((source, target))
    return lax.ppermute(value, axes, pairs)


def per_device(nodes, cotangent, w_qkv, w_out, tile_lists, counts, virtual):
    stage = lax.axis_index("yh")
    y, x, core = lax.axis_index("yl"), lax.axis_index("xl"), lax.axis_index("core")
    me = y * 2 + x
    batch = jnp.where(stage == 0, y, 1 - y) * 2 + x
    info = jnp.stack([batch, me, core, stage, batch ^ 2, y]).astype(jnp.int32)
    tables = (tile_lists.transpose(1, 2, 0), counts.transpose(1, 0), virtual)
    own, half = run_pack(info, w_qkv, w_out)
    near2 = fetched(half, 1, 0)
    near3 = fetched(half, 1, 1)
    beside = fetched(own, 0, 1)
    far2, far3 = swapped(near2, "core"), swapped(near3, "core")
    weights = (own, beside, near2, far2, near3, far3)

    hidden, *stash = run_forward(info, tables, nodes, weights)
    pair = ("yh", "yl")
    across, crossed = [(0, 3), (1, 2), (2, 1), (3, 0)], [(0, 2), (1, 3), (2, 0), (3, 1)]
    received = lax.ppermute(hidden, pair, across)
    grad, *rest = run_middle(info, tables, received, hidden, cotangent, nodes, weights)
    terms, stash2 = rest[: len(TERMS)], rest[len(TERMS) :]
    grads = (lax.ppermute(grad, pair, across), lax.ppermute(grad, pair, crossed))
    keep, send = lax.cond(
        stage == 0,
        lambda: tuple(run_backward(info, grads, stash, stash2, weights)),
        lambda: tuple(run_later(info, tables, grads[1], cotangent, weights, terms)),
    )

    def added(value, axis):
        return jnp.sum(value.astype(F32), axis=axis).astype(BF16)

    def repeated(value, times):
        return jnp.broadcast_to(value, (times, *value.shape))

    far, pairs, near = (lax.axis_size(axis) for axis in ("zh", "za", "zb"))
    total = (keep.astype(F32) + swapped(send, "core").astype(F32)).astype(BF16)
    total = lax.all_to_all(total.reshape(4 * near, D // near, INNER), ("xl", "xh", "zb"), 0, 0, tiled=True)
    total = added(total.reshape(4 * near, D // near, INNER), 0).reshape(pairs, D // (near * pairs), INNER)
    total = added(lax.all_to_all(total, "za", 0, 0, tiled=True), 0)
    total = added(lax.all_to_all(repeated(total, far), "zh", 0, 0, tiled=True), 0)
    total = lax.all_to_all(repeated(total, 2 * near * pairs), ("xh", "zb", "za"), 0, 0, tiled=True)
    mine = total.reshape(2, D, INNER)
    grad_qkv, grad_out = run_unpack(info, mine, swapped(mine, "core"))
    return (grad_qkv, grad_out)


def solution(mesh):
    depth = mesh.shape["dp"] // 4
    near = min(depth, 2)
    pairs = min(depth // near, 2)
    far = depth // (near * pairs)
    names = ("yh", "yl", "xl", "zh", "za", "zb", "xh", "core")
    cut = Mesh(mesh.devices.reshape(2, 2, 2, far, pairs, near, 2, 2), names)
    section, dp = P(("yh", "yl", "xl")), P(("zh", "za", "zb", "xh", "core"))
    return jax.shard_map(
        per_device,
        mesh=cut,
        in_specs=(dp, dp, section, section, dp, dp, dp),
        out_specs=(section, section),
        check_vma=False,
    )
```

```python
import functools

import jax
import jax.numpy as jnp
from jax import lax
from jax.experimental import pallas as pl
from jax.experimental.pallas import tpu as pltpu
from jax.sharding import Mesh
from jax.sharding import PartitionSpec as P

HEADS = 4
EPSILON = 1e-06
TEMPER = 4.0
D = 512
INNER = 256
ROWS = 128
HEAD = INNER // HEADS
SCALE = TEMPER / HEAD
STAGE_LAYERS = 4
F32 = jnp.float32
BF16 = jnp.bfloat16
STASH = {
    "normed": ((ROWS, D), BF16),
    "inverse": ((ROWS, ROWS), F32),
    "qkv": ((3, ROWS, INNER), BF16),
    "scales": ((2, ROWS, INNER), F32),
    "attn": ((HEADS * ROWS, ROWS), BF16),
    "mixed": ((ROWS, INNER), BF16),
}
TERMS = {
    "normed": ((ROWS, D), BF16),
    "mixed": ((ROWS, INNER), BF16),
    "grad_qkv": ((ROWS, 3 * INNER), BF16),
    "grad_out": ((ROWS, D), BF16),
}


def dot(a, b, over_a=1, over_b=0):
    return lax.dot_general(a, b, (((over_a,), (over_b,)), ((), ())), preferred_element_type=F32)


def head_masks():
    lane = lax.broadcasted_iota(jnp.int32, (1, INNER), 1)
    return [jnp.where(lane // HEAD == h, 1.0, 0.0).astype(F32) for h in range(HEADS)]


def head_mean_matrix():
    row = lax.broadcasted_iota(jnp.int32, (INNER, INNER), 0) // HEAD
    col = lax.broadcasted_iota(jnp.int32, (INNER, INNER), 1) // HEAD
    return jnp.where(row == col, 1.0 / HEAD, 0.0).astype(BF16)


def spread(values, masks):
    return jnp.concatenate([values * m.astype(values.dtype) for m in masks], axis=0)


def gathered(stacked, masks):
    total = stacked[:ROWS] * masks[0]
    for h in range(1, HEADS):
        total = total + stacked[h * ROWS : (h + 1) * ROWS] * masks[h]
    return total


def multiplicities(batch, tile_lists, counts, virtual):
    def times(tile, key_tile):
        seen = (virtual[batch] == key_tile).astype(F32)
        for slot in range(2):
            named = tile_lists[tile, slot, batch] == key_tile
            seen = seen + (named & (slot < counts[tile, batch])).astype(F32)
        return seen

    row = lax.broadcasted_iota(jnp.int32, (ROWS, ROWS), 0) < ROWS // 2
    col = lax.broadcasted_iota(jnp.int32, (ROWS, ROWS), 1) < ROWS // 2
    one = jnp.where(
        row,
        jnp.where(col, times(0, 0), times(0, 1)),
        jnp.where(col, times(1, 0), times(1, 1)),
    )
    return jnp.concatenate([one] * HEADS, axis=0)


def forward_layer(layer, hidden, weight, times, masks, mean_matrix, stash):
    widened = hidden.astype(F32)
    inverse = lax.rsqrt(jnp.mean(widened * widened, axis=-1, keepdims=True) + EPSILON)
    normed = (widened * inverse).astype(BF16)
    q = dot(normed, weight(0))
    k = dot(normed, weight(1))
    v = dot(normed, weight(2)).astype(BF16)
    scale_q = lax.rsqrt(dot((q * q).astype(BF16), mean_matrix) + EPSILON) * SCALE
    scale_k = lax.rsqrt(dot((k * k).astype(BF16), mean_matrix) + EPSILON)
    qn = (q * scale_q).astype(BF16)
    kn = (k * scale_k).astype(BF16)
    scores = dot(spread(qn, masks), kn, 1, 1)
    exponent = jnp.exp(scores) * times
    share = 1.0 / jnp.sum(exponent, axis=-1, keepdims=True)
    mixed = gathered(dot(exponent.astype(BF16), v) * share, masks).astype(BF16)
    attn = (exponent * share).astype(BF16)
    stash["normed"][layer] = normed
    stash["inverse"][layer] = jnp.broadcast_to(inverse, (ROWS, ROWS))
    stash["qkv"][layer, 0] = qn
    stash["qkv"][layer, 1] = kn
    stash["qkv"][layer, 2] = v
    stash["scales"][layer, 0] = scale_q
    stash["scales"][layer, 1] = scale_k
    stash["attn"][layer] = attn
    stash["mixed"][layer] = mixed
    out = weight(3)
    added = jnp.concatenate([dot(mixed, out[:INNER]), dot(mixed, out[INNER:])], axis=1)
    return (widened + added).astype(BF16)


def backward_layer(layer, grad, weight, masks, mean_matrix, stash):
    inverse = stash["inverse"][layer][:, :1]
    qn = stash["qkv"][layer, 0]
    kn = stash["qkv"][layer, 1]
    v = stash["qkv"][layer, 2]
    attn = stash["attn"][layer]
    out = weight(3)
    low, high = grad[:, :INNER], grad[:, INNER:]
    grad_mixed = (dot(low, out[:INNER], 1, 1) + dot(high, out[INNER:], 1, 1)).astype(BF16)
    stacked = spread(grad_mixed, masks)
    grad_attn = dot(stacked, v, 1, 1)
    attn_wide = attn.astype(F32)
    product = grad_mixed.astype(F32) * stash["mixed"][layer].astype(F32)
    inner = jnp.concatenate([jnp.sum(product * m, axis=-1, keepdims=True) for m in masks], axis=0)
    grad_scores = (attn_wide * (grad_attn - inner)).astype(BF16)
    grad_v = dot(attn, stacked, 0, 0).astype(BF16)
    grad_qn = gathered(dot(grad_scores, kn), masks)
    grad_kn = dot(grad_scores, spread(qn, masks), 0, 0)
    qw, kw = qn.astype(F32), kn.astype(F32)
    mean_q = dot((grad_qn * qw).astype(BF16), mean_matrix) * (1.0 / (SCALE * SCALE))
    mean_k = dot((grad_kn * kw).astype(BF16), mean_matrix)
    grad_q = (stash["scales"][layer, 0] * (grad_qn - qw * mean_q)).astype(BF16)
    grad_k = (stash["scales"][layer, 1] * (grad_kn - kw * mean_k)).astype(BF16)
    grad_normed = dot(grad_q, weight(0), 1, 1) + dot(grad_k, weight(1), 1, 1) + dot(grad_v, weight(2), 1, 1)
    wide = stash["normed"][layer].astype(F32)
    mean = jnp.mean(grad_normed * wide, axis=-1, keepdims=True)
    result = (grad.astype(F32) + inverse * (grad_normed - wide * mean)).astype(BF16)
    return result, jnp.concatenate([grad_q, grad_k, grad_v], axis=1)


class Weights:
    def __init__(self, own, beside, near2, far2, near3, far3, place, sems, me, core, order):
        self.place, self.me, self.order = place, me, order

        def halves(r, near, far):
            return [(near, place.at[r, pl.ds(2 * core, 2)]), (far, place.at[r, pl.ds(2 * (1 - core), 2)])]

        pairs = [
            [(own, place.at[0])],
            [(beside, place.at[1])],
            halves(2, near2, far2),
            halves(3, near3, far3),
        ]
        self.copies = [
            [pltpu.make_async_copy(src, dst, sems.at[r, i]) for i, (src, dst) in enumerate(listed)]
            for r, listed in enumerate(pairs)
        ]

    def each(self, layer, act):
        for r in range(STAGE_LAYERS):

            @pl.when((layer ^ self.me) == r)
            def _(r=r):
                for copy in self.copies[r]:
                    act(copy)

    def start(self):
        for layer in self.order:
            self.each(layer, lambda copy: copy.start())

    def wait(self, layer):
        self.each(layer, lambda copy: copy.wait())

    def layer(self, index):
        r = index ^ self.me
        return lambda block: self.place[r, block]


class Sheets:
    def __init__(self, names, outside, inside, sems, inward):
        self.copies = []
        for layer in range(STAGE_LAYERS):
            listed = []
            for i in range(len(names)):
                a, b = outside[i].at[layer], inside[i].at[layer]
                listed.append(pltpu.make_async_copy(*((a, b) if inward else (b, a)), sems.at[i, layer]))
            self.copies.append(listed)
        self.refs = dict(zip(names, inside))

    def start(self, layer):
        for copy in self.copies[layer]:
            copy.start()

    def wait(self, layer):
        for copy in self.copies[layer]:
            copy.wait()


def weight_gradients(slot, normed, mixed, grad_qkv, grad_out, place, core):
    full = dot(normed, grad_qkv, 0, 0).astype(BF16)
    for block in range(3):
        place[(block // 2) ^ core, slot, block % 2] = full[:, block * INNER : (block + 1) * INNER]
    last = dot(mixed, grad_out, 0, 0).astype(BF16)
    place[1 ^ core, slot, 1, :INNER] = last[:, :INNER]
    place[1 ^ core, slot, 1, INNER:] = last[:, INNER:]


def both(a, b):
    return jnp.concatenate([a, b], axis=0)


class Results:
    def __init__(self, outs, place, sems):
        self.copies = [
            [pltpu.make_async_copy(place.at[side, slot], outs[side].at[slot], sems.at[side, slot]) for side in range(2)]
            for slot in range(2)
        ]

    def start(self, slot):
        for copy in self.copies[slot]:
            copy.start()

    def wait(self, slot):
        for copy in self.copies[slot]:
            copy.wait()


def pack_kernel(info, qkv, out, own, half, sems):
    blocks = [[(qkv.at[0, :, pl.ds(b * INNER, INNER)], slice(None))] for b in range(3)]
    blocks.append([(out.at[0, :, pl.ds(i * INNER, INNER)], pl.ds(i * INNER, INNER)) for i in range(2)])
    copies = []
    for block in range(4):
        for i, (source, rows) in enumerate(blocks[block]):
            copies.append(pltpu.make_async_copy(source, own.at[block, rows], sems.at[0, block + i]))
    for copy in copies:
        copy.start()
    for side in range(2):

        @pl.when(info[2] == side)
        def _(side=side):
            chosen = []
            for slot in range(2):
                for i, (source, rows) in enumerate(blocks[2 * side + slot]):
                    chosen.append(pltpu.make_async_copy(source, half.at[slot, rows], sems.at[1, slot + i]))
            for copy in chosen:
                copy.start()
            for copy in chosen:
                copy.wait()

    for copy in copies:
        copy.wait()


def unpack_kernel(info, mine, other, qkv, out, sems):
    for side in range(2):

        @pl.when(info[2] == side)
        def _(side=side):
            low, high = (mine, other) if side == 0 else (other, mine)
            pairs = [
                (low.at[0], qkv.at[0, :, pl.ds(0, INNER)]),
                (low.at[1], qkv.at[0, :, pl.ds(INNER, INNER)]),
                (high.at[0], qkv.at[0, :, pl.ds(2 * INNER, INNER)]),
                (high.at[1, pl.ds(0, INNER)], out.at[0, :, pl.ds(0, INNER)]),
                (high.at[1, pl.ds(INNER, INNER)], out.at[0, :, pl.ds(INNER, INNER)]),
            ]
            copies = [pltpu.make_async_copy(src, dst, sems.at[i]) for i, (src, dst) in enumerate(pairs)]
            for copy in copies:
                copy.start()
            for copy in copies:
                copy.wait()


def forward_kernel(info, tile_lists, counts, virtual, hidden_in, *rest):
    weights = Weights(*rest[:6], *rest[-4:-2], info[1], info[2], range(STAGE_LAYERS))
    hidden_out, outside, inside = rest[6], rest[7 : 7 + len(STASH)], rest[7 + len(STASH) : 7 + 2 * len(STASH)]
    sheets = Sheets(STASH, outside, inside, rest[-2], False)
    weights.start()
    masks, mean_matrix = head_masks(), head_mean_matrix()
    times = rest[-1]
    times[...] = multiplicities(info[0], tile_lists, counts, virtual)
    hidden = hidden_in[0]
    for layer in range(STAGE_LAYERS):
        weights.wait(layer)
        hidden = forward_layer(layer, hidden, weights.layer(layer), times[...], masks, mean_matrix, sheets.refs)
        sheets.start(layer)
    hidden_out[...] = hidden
    for layer in range(STAGE_LAYERS):
        sheets.wait(layer)


def run_chain(hidden, grad, weights, times, masks, mean_matrix, stash, terms_qkv, terms_out, done):
    for layer in range(STAGE_LAYERS):
        weights.wait(layer)
        hidden = forward_layer(layer, hidden, weights.layer(layer), times[...], masks, mean_matrix, stash)
    for layer in reversed(range(STAGE_LAYERS)):
        terms_out[layer] = grad
        grad, grad_qkv = backward_layer(layer, grad, weights.layer(layer), masks, mean_matrix, stash)
        terms_qkv[layer] = grad_qkv
        done(layer)
    return grad


def middle_kernel(info, tile_lists, counts, virtual, hidden_in, sent, grad_in, nodes_in, *rest):
    given, grad_out, rest = rest[:6], rest[6], rest[7:]
    terms_outside, stash_outside, inside = rest[: len(TERMS)], rest[len(TERMS) :][: len(STASH)], rest[len(TERMS) + len(STASH) :]
    stash_inside, (terms_qkv, terms_out) = inside[: len(STASH)], inside[len(STASH) :][:2]
    place, weight_sems, terms_sems, stash_sems, times, grad_place, grad_sem = inside[len(STASH) + 2 :]
    weights = Weights(*given, place, weight_sems, info[1], info[2], range(STAGE_LAYERS))
    stash = dict(zip(STASH, stash_inside))
    weights.start()
    masks, mean_matrix = head_masks(), head_mean_matrix()

    @pl.when(info[3] == 1)
    def _():
        times[...] = multiplicities(info[0], tile_lists, counts, virtual)
        sheets = Sheets(TERMS, terms_outside, (stash["normed"], stash["mixed"], terms_qkv, terms_out), terms_sems, False)
        grad_place[...] = run_chain(
            hidden_in[...], grad_in[0], weights, times, masks, mean_matrix, stash, terms_qkv, terms_out, sheets.start
        )
        copy = pltpu.make_async_copy(grad_place, grad_out, grad_sem)
        copy.start()
        copy.wait()
        for layer in range(STAGE_LAYERS):
            sheets.wait(layer)

    @pl.when(info[3] == 0)
    def _():
        times[...] = multiplicities(info[4], tile_lists, counts, virtual)
        sheets = Sheets(STASH, stash_outside, stash_inside, stash_sems, False)
        hidden = nodes_in[0]
        for layer in range(STAGE_LAYERS):
            weights.wait(layer)
            hidden = forward_layer(layer, hidden, weights.layer(layer), times[...], masks, mean_matrix, stash)
            sheets.start(layer)
        for layer in range(STAGE_LAYERS):
            sheets.wait(layer)


def later_kernel(info, tile_lists, counts, virtual, hidden_in, grad_in, *rest):
    given, outside, outs, inside = rest[:6], rest[6:10], rest[10:12], rest[12:]
    stash = dict(zip(STASH, inside[: len(STASH)]))
    terms_qkv, terms_out, *first = inside[len(STASH) :][:6]
    weight_place, weight_sems, place, terms_sems, out_sems, times = inside[len(STASH) + 6 :]
    low = 2 * info[5]
    copies = [
        pltpu.make_async_copy(outside[i].at[low + slot], first[i].at[slot], terms_sems.at[i, slot])
        for i in range(len(TERMS))
        for slot in range(2)
    ]
    weights = Weights(*given, weight_place, weight_sems, info[1], info[2], range(STAGE_LAYERS))
    weights.start()
    for copy in copies:
        copy.start()
    masks, mean_matrix = head_masks(), head_mean_matrix()
    times[...] = multiplicities(info[4], tile_lists, counts, virtual)
    run_chain(
        hidden_in[...], grad_in[0], weights, times, masks, mean_matrix, stash, terms_qkv, terms_out, lambda layer: None
    )
    for copy in copies:
        copy.wait()
    results = Results(outs, place, out_sems)
    second = (stash["normed"], stash["mixed"], terms_qkv, terms_out)
    for slot in range(2):
        weight_gradients(slot, *(both(first[i][slot], second[i][low + slot]) for i in range(len(TERMS))), place, info[2])
        results.start(slot)
    for slot in range(2):
        results.wait(slot)


def backward_kernel(info, grad_in, grad_in2, *rest):
    order = tuple(reversed(range(STAGE_LAYERS)))
    count = len(STASH)
    outside, outside2, given, outs = rest[:count], rest[count:][:count], rest[2 * count :][:6], rest[2 * count + 6 :][:2]
    inside = rest[2 * count + 8 :]
    weight_place, weight_sems, place, kept_qkv, kept_out, sems, sems2, out_sems = inside[2 * count :]
    weights = Weights(*given, weight_place, weight_sems, info[1], info[2], order)
    sheets = [
        Sheets(STASH, outside, inside[:count], sems, True),
        Sheets(STASH, outside2, inside[count:][:count], sems2, True),
    ]
    results = Results(outs, place, out_sems)
    for layer in order:
        for one in sheets:
            one.start(layer)
        weights.each(layer, lambda copy: copy.start())
    masks, mean_matrix = head_masks(), head_mean_matrix()

    def step(layer, grads):
        for one in sheets:
            one.wait(layer)
        weights.wait(layer)
        return tuple(
            zip(*(backward_layer(layer, g, weights.layer(layer), masks, mean_matrix, one.refs) for g, one in zip(grads, sheets)))
        )

    def finish(layer, grad_qkv, grad_out):
        normed, mixed = (both(*(one.refs[n][layer] for one in sheets)) for n in ("normed", "mixed"))
        weight_gradients(layer % 2, normed, mixed, grad_qkv, grad_out, place, info[2])
        results.start(layer % 2)

    grads = (grad_in[...], grad_in2[...])
    for layer in (3, 2):
        kept_out[layer - 2] = both(*grads)
        grads, terms = step(layer, grads)
        kept_qkv[layer - 2] = both(*terms)
    kept_out[2] = both(*grads)

    @pl.when(info[5] == 1)
    def _():
        for layer in (3, 2):
            finish(layer, kept_qkv[layer - 2], kept_out[layer - 2])
        for layer in (1, 0):
            for one in sheets:
                one.wait(layer)
            weights.wait(layer)

    @pl.when(info[5] == 0)
    def _():
        now = (kept_out[2, :ROWS], kept_out[2, ROWS:])
        for layer in (1, 0):
            before = both(*now)
            now, terms = step(layer, now)
            finish(layer, both(*terms), before)

    for slot in range(2):
        results.wait(slot)


ANYWHERE = pl.BlockSpec(memory_space=pl.ANY)
IN_HBM = pl.BlockSpec(memory_space=pltpu.HBM)
HIDDEN = jax.ShapeDtypeStruct((ROWS, D), BF16)
HIDDEN_BLOCK = pl.BlockSpec((ROWS, D), lambda *_: (0, 0))
BATCH_BLOCK = pl.BlockSpec((1, ROWS, D), lambda step, info, *_: (info[0], 0, 0))
SECOND_BLOCK = pl.BlockSpec((1, ROWS, D), lambda step, info, *_: (info[4], 0, 0))
GRAD_HALF = jax.ShapeDtypeStruct((2, 2, D, INNER), BF16)
WEIGHT_SCRATCH = [
    pltpu.VMEM((STAGE_LAYERS, 4, D, INNER), BF16),
    pltpu.SemaphoreType.DMA((STAGE_LAYERS, 2)),
]
GRAD_PLACE = pltpu.VMEM((2, 2, 2, D, INNER), BF16)
TIMES = pltpu.VMEM((HEADS * ROWS, ROWS), F32)


def layered(sizes, make):
    return [make((STAGE_LAYERS, *shape), kind) for shape, kind in sizes.values()]


def semaphores(count):
    return pltpu.SemaphoreType.DMA((count, STAGE_LAYERS))


def call(kernel, prefetched, in_specs, out_specs, out_shape, scratch, args, megabytes=48, aliases=None):
    return pl.pallas_call(
        kernel,
        grid_spec=pltpu.PrefetchScalarGridSpec(
            num_scalar_prefetch=prefetched,
            grid=(1,),
            in_specs=in_specs,
            out_specs=out_specs,
            scratch_shapes=scratch,
        ),
        out_shape=out_shape,
        compiler_params=pltpu.CompilerParams(vmem_limit_bytes=megabytes * 2**20),
        input_output_aliases=aliases or {},
    )(*args)


def run_pack(info, w_qkv, w_out):
    shapes = [jax.ShapeDtypeStruct((blocks, D, INNER), BF16) for blocks in (4, 2)]
    sems = [pltpu.SemaphoreType.DMA((2, 5))]
    return call(pack_kernel, 1, [IN_HBM] * 2, [ANYWHERE] * 2, shapes, sems, (info, w_qkv, w_out), 1)


def run_unpack(info, mine, other):
    shapes = [jax.ShapeDtypeStruct((1, *shape), BF16) for shape in ((D, 3 * INNER), (INNER, D))]
    sems = [pltpu.SemaphoreType.DMA((5,))]
    return call(unpack_kernel, 1, [ANYWHERE] * 2, [IN_HBM] * 2, shapes, sems, (info, mine, other), 1)


def run_forward(info, tables, nodes, weights):
    return call(
        forward_kernel,
        4,
        [BATCH_BLOCK] + [ANYWHERE] * 6,
        [HIDDEN_BLOCK] + [ANYWHERE] * len(STASH),
        [HIDDEN] + layered(STASH, jax.ShapeDtypeStruct),
        layered(STASH, pltpu.VMEM) + WEIGHT_SCRATCH + [semaphores(len(STASH)), TIMES],
        (info, *tables, nodes, *weights),
        58,
    )


def run_middle(info, tables, hidden, sent, cotangent, nodes, weights):
    return call(
        middle_kernel,
        4,
        [HIDDEN_BLOCK, ANYWHERE, BATCH_BLOCK, SECOND_BLOCK] + [ANYWHERE] * 6,
        [ANYWHERE] * (1 + len(TERMS) + len(STASH)),
        [HIDDEN] + layered(TERMS, jax.ShapeDtypeStruct) + layered(STASH, jax.ShapeDtypeStruct),
        layered(STASH, pltpu.VMEM)
        + layered(TERMS, pltpu.VMEM)[2:]
        + WEIGHT_SCRATCH
        + [semaphores(len(TERMS)), semaphores(len(STASH)), TIMES, pltpu.VMEM((ROWS, D), BF16), pltpu.SemaphoreType.DMA],
        (info, *tables, hidden, sent, cotangent, nodes, *weights),
        50,
        {5: 0},
    )


def run_later(info, tables, hidden, cotangent, weights, terms):
    return call(
        later_kernel,
        4,
        [HIDDEN_BLOCK, SECOND_BLOCK] + [ANYWHERE] * (6 + len(TERMS)),
        [ANYWHERE] * 2,
        [GRAD_HALF] * 2,
        layered(STASH, pltpu.VMEM)
        + layered(TERMS, pltpu.VMEM)[2:]
        + [pltpu.VMEM((2, *shape), kind) for shape, kind in TERMS.values()]
        + WEIGHT_SCRATCH
        + [GRAD_PLACE, pltpu.SemaphoreType.DMA((len(TERMS), 2)), pltpu.SemaphoreType.DMA((2, 2)), TIMES],
        (info, *tables, hidden, cotangent, *weights, *terms),
    )


def run_backward(info, grads, stash, stash2, weights):
    return call(
        backward_kernel,
        1,
        [HIDDEN_BLOCK] * 2 + [ANYWHERE] * (2 * len(STASH) + 6),
        [ANYWHERE] * 2,
        [GRAD_HALF] * 2,
        layered(STASH, pltpu.VMEM) * 2
        + WEIGHT_SCRATCH
        + [GRAD_PLACE, pltpu.VMEM((2, 2 * ROWS, 3 * INNER), BF16), pltpu.VMEM((3, 2 * ROWS, D), BF16)]
        + [semaphores(len(STASH)), semaphores(len(STASH)), pltpu.SemaphoreType.DMA((2, 2))],
        (info, *grads, *stash, *stash2, *weights),
    )


def swapped(value, axis):
    return lax.ppermute(value, axis, [(0, 1), (1, 0)])


def fetched(value, flip_y, flip_x):
    axes = ("yl", "xl", "xh", "core")
    pairs = []
    for y in range(2):
        for x in range(2):
            for upper in range(2):
                for core in range(2):
                    there = upper ^ (core if flip_x else 0)
                    source = ((y * 2 + x) * 2 + upper) * 2 + core
                    target = (((y ^ flip_y) * 2 + (x ^ flip_x)) * 2 + there) * 2 + core
                    pairs.append((source, target))
    return lax.ppermute(value, axes, pairs)


def per_device(nodes, cotangent, w_qkv, w_out, tile_lists, counts, virtual):
    stage = lax.axis_index("yh")
    y, x, core = lax.axis_index("yl"), lax.axis_index("xl"), lax.axis_index("core")
    me = y * 2 + x
    batch = jnp.where(stage == 0, y, 1 - y) * 2 + x
    info = jnp.stack([batch, me, core, stage, batch ^ 2, y]).astype(jnp.int32)
    tables = (tile_lists.transpose(1, 2, 0), counts.transpose(1, 0), virtual)
    own, half = run_pack(info, w_qkv, w_out)
    near2 = fetched(half, 1, 0)
    near3 = fetched(half, 1, 1)
    beside = fetched(own, 0, 1)
    far2, far3 = swapped(near2, "core"), swapped(near3, "core")
    weights = (own, beside, near2, far2, near3, far3)

    hidden, *stash = run_forward(info, tables, nodes, weights)
    pair = ("yh", "yl")
    across, crossed = [(0, 3), (1, 2), (2, 1), (3, 0)], [(0, 2), (1, 3), (2, 0), (3, 1)]
    received = lax.ppermute(hidden, pair, across)
    grad, *rest = run_middle(info, tables, received, hidden, cotangent, nodes, weights)
    terms, stash2 = rest[: len(TERMS)], rest[len(TERMS) :]
    grads = (lax.ppermute(grad, pair, across), lax.ppermute(grad, pair, crossed))
    keep, send = lax.cond(
        stage == 0,
        lambda: tuple(run_backward(info, grads, stash, stash2, weights)),
        lambda: tuple(run_later(info, tables, grads[1], cotangent, weights, terms)),
    )

    def added(value, axis):
        return jnp.sum(value.astype(F32), axis=axis).astype(BF16)

    def repeated(value, times):
        return jnp.broadcast_to(value, (times, *value.shape))

    far, pairs, near = (lax.axis_size(axis) for axis in ("zh", "za", "zb"))
    total = (keep.astype(F32) + swapped(send, "core").astype(F32)).astype(BF16)
    around = near * pairs
    total = total.reshape(4 * around, D // around, INNER)
    total = added(lax.all_to_all(total, ("xl", "xh", "zb", "za"), 0, 0, tiled=True), 0)
    total = added(lax.all_to_all(repeated(total, far), "zh", 0, 0, tiled=True), 0)
    total = lax.all_to_all(repeated(total, 2 * around), ("xh", "zb", "za"), 0, 0, tiled=True)
    mine = total.reshape(2, D, INNER)
    grad_qkv, grad_out = run_unpack(info, mine, swapped(mine, "core"))
    return (grad_qkv, grad_out)


def solution(mesh):
    depth = mesh.shape["dp"] // 4
    near = min(depth, 2)
    pairs = min(depth // near, 2)
    far = depth // (near * pairs)
    names = ("yh", "yl", "xl", "zh", "za", "zb", "xh", "core")
    cut = Mesh(mesh.devices.reshape(2, 2, 2, far, pairs, near, 2, 2), names)
    section, dp = P(("yh", "yl", "xl")), P(("zh", "za", "zb", "xh", "core"))
    return jax.shard_map(
        per_device,
        mesh=cut,
        in_specs=(dp, dp, section, section, dp, dp, dp),
        out_specs=(section, section),
        check_vma=False,
    )
```

```python
import functools

import jax
import jax.numpy as jnp
from jax import lax
from jax.experimental import pallas as pl
from jax.experimental.pallas import tpu as pltpu
from jax.sharding import Mesh
from jax.sharding import PartitionSpec as P

HEADS = 4
EPSILON = 1e-06
TEMPER = 4.0
D = 512
INNER = 256
ROWS = 128
HEAD = INNER // HEADS
SCALE = TEMPER / HEAD
STAGE_LAYERS = 4
F32 = jnp.float32
BF16 = jnp.bfloat16
STASH = {
    "normed": ((ROWS, D), BF16),
    "inverse": ((ROWS, ROWS), F32),
    "qkv": ((3, ROWS, INNER), BF16),
    "scales": ((2, ROWS, INNER), F32),
    "attn": ((HEADS * ROWS, ROWS), BF16),
    "mixed": ((ROWS, INNER), BF16),
}
TERMS = {
    "normed": ((ROWS, D), BF16),
    "mixed": ((ROWS, INNER), BF16),
    "grad_qkv": ((ROWS, 3 * INNER), BF16),
    "grad_out": ((ROWS, D), BF16),
}


def dot(a, b, over_a=1, over_b=0):
    return lax.dot_general(a, b, (((over_a,), (over_b,)), ((), ())), preferred_element_type=F32)


def head_masks():
    lane = lax.broadcasted_iota(jnp.int32, (1, INNER), 1)
    return [jnp.where(lane // HEAD == h, 1.0, 0.0).astype(F32) for h in range(HEADS)]


def head_mean_matrix():
    row = lax.broadcasted_iota(jnp.int32, (INNER, INNER), 0) // HEAD
    col = lax.broadcasted_iota(jnp.int32, (INNER, INNER), 1) // HEAD
    return jnp.where(row == col, 1.0 / HEAD, 0.0).astype(BF16)


def spread(values, masks):
    return jnp.concatenate([values * m.astype(values.dtype) for m in masks], axis=0)


def gathered(stacked, masks):
    total = stacked[:ROWS] * masks[0]
    for h in range(1, HEADS):
        total = total + stacked[h * ROWS : (h + 1) * ROWS] * masks[h]
    return total


def multiplicities(batch, tile_lists, counts, virtual):
    def times(tile, key_tile):
        seen = (virtual[batch] == key_tile).astype(F32)
        for slot in range(2):
            named = tile_lists[tile, slot, batch] == key_tile
            seen = seen + (named & (slot < counts[tile, batch])).astype(F32)
        return seen

    row = lax.broadcasted_iota(jnp.int32, (ROWS, ROWS), 0) < ROWS // 2
    col = lax.broadcasted_iota(jnp.int32, (ROWS, ROWS), 1) < ROWS // 2
    one = jnp.where(
        row,
        jnp.where(col, times(0, 0), times(0, 1)),
        jnp.where(col, times(1, 0), times(1, 1)),
    )
    return jnp.concatenate([one] * HEADS, axis=0)


def forward_layer(layer, hidden, weight, times, masks, mean_matrix, stash):
    widened = hidden.astype(F32)
    inverse = lax.rsqrt(jnp.mean(widened * widened, axis=-1, keepdims=True) + EPSILON)
    normed = (widened * inverse).astype(BF16)
    q = dot(normed, weight(0))
    k = dot(normed, weight(1))
    v = dot(normed, weight(2)).astype(BF16)
    scale_q = lax.rsqrt(dot((q * q).astype(BF16), mean_matrix) + EPSILON) * SCALE
    scale_k = lax.rsqrt(dot((k * k).astype(BF16), mean_matrix) + EPSILON)
    qn = (q * scale_q).astype(BF16)
    kn = (k * scale_k).astype(BF16)
    scores = dot(spread(qn, masks), kn, 1, 1)
    exponent = jnp.exp(scores) * times
    share = 1.0 / jnp.sum(exponent, axis=-1, keepdims=True)
    mixed = gathered(dot(exponent.astype(BF16), v) * share, masks).astype(BF16)
    attn = (exponent * share).astype(BF16)
    stash["normed"][layer] = normed
    stash["inverse"][layer] = jnp.broadcast_to(inverse, (ROWS, ROWS))
    stash["qkv"][layer, 0] = qn
    stash["qkv"][layer, 1] = kn
    stash["qkv"][layer, 2] = v
    stash["scales"][layer, 0] = scale_q
    stash["scales"][layer, 1] = scale_k
    stash["attn"][layer] = attn
    stash["mixed"][layer] = mixed
    out = weight(3)
    added = jnp.concatenate([dot(mixed, out[:INNER]), dot(mixed, out[INNER:])], axis=1)
    return (widened + added).astype(BF16)


def backward_layer(layer, grad, weight, masks, mean_matrix, stash):
    inverse = stash["inverse"][layer][:, :1]
    qn = stash["qkv"][layer, 0]
    kn = stash["qkv"][layer, 1]
    v = stash["qkv"][layer, 2]
    attn = stash["attn"][layer]
    out = weight(3)
    low, high = grad[:, :INNER], grad[:, INNER:]
    grad_mixed = (dot(low, out[:INNER], 1, 1) + dot(high, out[INNER:], 1, 1)).astype(BF16)
    stacked = spread(grad_mixed, masks)
    grad_attn = dot(stacked, v, 1, 1)
    attn_wide = attn.astype(F32)
    product = grad_mixed.astype(F32) * stash["mixed"][layer].astype(F32)
    inner = jnp.concatenate([jnp.sum(product * m, axis=-1, keepdims=True) for m in masks], axis=0)
    grad_scores = (attn_wide * (grad_attn - inner)).astype(BF16)
    grad_v = dot(attn, stacked, 0, 0).astype(BF16)
    grad_qn = gathered(dot(grad_scores, kn), masks)
    grad_kn = dot(grad_scores, spread(qn, masks), 0, 0)
    qw, kw = qn.astype(F32), kn.astype(F32)
    mean_q = dot((grad_qn * qw).astype(BF16), mean_matrix) * (1.0 / (SCALE * SCALE))
    mean_k = dot((grad_kn * kw).astype(BF16), mean_matrix)
    grad_q = (stash["scales"][layer, 0] * (grad_qn - qw * mean_q)).astype(BF16)
    grad_k = (stash["scales"][layer, 1] * (grad_kn - kw * mean_k)).astype(BF16)
    grad_normed = dot(grad_q, weight(0), 1, 1) + dot(grad_k, weight(1), 1, 1) + dot(grad_v, weight(2), 1, 1)
    wide = stash["normed"][layer].astype(F32)
    mean = jnp.mean(grad_normed * wide, axis=-1, keepdims=True)
    result = (grad.astype(F32) + inverse * (grad_normed - wide * mean)).astype(BF16)
    return result, jnp.concatenate([grad_q, grad_k, grad_v], axis=1)


class Weights:
    def __init__(self, own, beside, near2, far2, near3, far3, place, sems, me, core, order):
        self.place, self.me, self.order = place, me, order

        def halves(r, near, far):
            return [(near, place.at[r, pl.ds(2 * core, 2)]), (far, place.at[r, pl.ds(2 * (1 - core), 2)])]

        pairs = [
            [(own, place.at[0])],
            [(beside, place.at[1])],
            halves(2, near2, far2),
            halves(3, near3, far3),
        ]
        self.copies = [
            [pltpu.make_async_copy(src, dst, sems.at[r, i]) for i, (src, dst) in enumerate(listed)]
            for r, listed in enumerate(pairs)
        ]

    def each(self, layer, act):
        for r in range(STAGE_LAYERS):

            @pl.when((layer ^ self.me) == r)
            def _(r=r):
                for copy in self.copies[r]:
                    act(copy)

    def start(self):
        for layer in self.order:
            self.each(layer, lambda copy: copy.start())

    def wait(self, layer):
        self.each(layer, lambda copy: copy.wait())

    def layer(self, index):
        r = index ^ self.me
        return lambda block: self.place[r, block]


class Sheets:
    def __init__(self, names, outside, inside, sems, inward):
        self.copies = []
        for layer in range(STAGE_LAYERS):
            listed = []
            for i in range(len(names)):
                a, b = outside[i].at[layer], inside[i].at[layer]
                listed.append(pltpu.make_async_copy(*((a, b) if inward else (b, a)), sems.at[i, layer]))
            self.copies.append(listed)
        self.refs = dict(zip(names, inside))

    def start(self, layer):
        for copy in self.copies[layer]:
            copy.start()

    def wait(self, layer):
        for copy in self.copies[layer]:
            copy.wait()


def weight_gradients(slot, normed, mixed, grad_qkv, grad_out, place, core):
    full = dot(normed, grad_qkv, 0, 0).astype(BF16)
    for block in range(3):
        place[(block // 2) ^ core, slot, block % 2] = full[:, block * INNER : (block + 1) * INNER]
    last = dot(mixed, grad_out, 0, 0).astype(BF16)
    place[1 ^ core, slot, 1, :INNER] = last[:, :INNER]
    place[1 ^ core, slot, 1, INNER:] = last[:, INNER:]


def both(a, b):
    return jnp.concatenate([a, b], axis=0)


class Results:
    def __init__(self, outs, place, sems):
        self.copies = [
            [pltpu.make_async_copy(place.at[side, slot], outs[side].at[slot], sems.at[side, slot]) for side in range(2)]
            for slot in range(2)
        ]

    def start(self, slot):
        for copy in self.copies[slot]:
            copy.start()

    def wait(self, slot):
        for copy in self.copies[slot]:
            copy.wait()


def pack_kernel(info, qkv, out, own, half, sems):
    blocks = [[(qkv.at[0, :, pl.ds(b * INNER, INNER)], slice(None))] for b in range(3)]
    blocks.append([(out.at[0, :, pl.ds(i * INNER, INNER)], pl.ds(i * INNER, INNER)) for i in range(2)])
    copies = []
    for block in range(4):
        for i, (source, rows) in enumerate(blocks[block]):
            copies.append(pltpu.make_async_copy(source, own.at[block, rows], sems.at[0, block + i]))
    for copy in copies:
        copy.start()
    for side in range(2):

        @pl.when(info[2] == side)
        def _(side=side):
            chosen = []
            for slot in range(2):
                for i, (source, rows) in enumerate(blocks[2 * side + slot]):
                    chosen.append(pltpu.make_async_copy(source, half.at[slot, rows], sems.at[1, slot + i]))
            for copy in chosen:
                copy.start()
            for copy in chosen:
                copy.wait()

    for copy in copies:
        copy.wait()


def unpack_kernel(info, mine, other, qkv, out, sems):
    for side in range(2):

        @pl.when(info[2] == side)
        def _(side=side):
            low, high = (mine, other) if side == 0 else (other, mine)
            pairs = [
                (low.at[0], qkv.at[0, :, pl.ds(0, INNER)]),
                (low.at[1], qkv.at[0, :, pl.ds(INNER, INNER)]),
                (high.at[0], qkv.at[0, :, pl.ds(2 * INNER, INNER)]),
                (high.at[1, pl.ds(0, INNER)], out.at[0, :, pl.ds(0, INNER)]),
                (high.at[1, pl.ds(INNER, INNER)], out.at[0, :, pl.ds(INNER, INNER)]),
            ]
            copies = [pltpu.make_async_copy(src, dst, sems.at[i]) for i, (src, dst) in enumerate(pairs)]
            for copy in copies:
                copy.start()
            for copy in copies:
                copy.wait()


def forward_kernel(info, tile_lists, counts, virtual, hidden_in, *rest):
    weights = Weights(*rest[:6], *rest[-4:-2], info[1], info[2], range(STAGE_LAYERS))
    hidden_out, outside, inside = rest[6], rest[7 : 7 + len(STASH)], rest[7 + len(STASH) : 7 + 2 * len(STASH)]
    sheets = Sheets(STASH, outside, inside, rest[-2], False)
    weights.start()
    masks, mean_matrix = head_masks(), head_mean_matrix()
    times = rest[-1]
    times[...] = multiplicities(info[0], tile_lists, counts, virtual)
    hidden = hidden_in[0]
    for layer in range(STAGE_LAYERS):
        weights.wait(layer)
        hidden = forward_layer(layer, hidden, weights.layer(layer), times[...], masks, mean_matrix, sheets.refs)
        sheets.start(layer)
    hidden_out[...] = hidden
    for layer in range(STAGE_LAYERS):
        sheets.wait(layer)


def run_chain(hidden, grad, weights, times, masks, mean_matrix, stash, terms_qkv, terms_out, done):
    for layer in range(STAGE_LAYERS):
        weights.wait(layer)
        hidden = forward_layer(layer, hidden, weights.layer(layer), times[...], masks, mean_matrix, stash)
    for layer in reversed(range(STAGE_LAYERS)):
        terms_out[layer] = grad
        grad, grad_qkv = backward_layer(layer, grad, weights.layer(layer), masks, mean_matrix, stash)
        terms_qkv[layer] = grad_qkv
        done(layer)
    return grad


def middle_kernel(info, tile_lists, counts, virtual, hidden_in, sent, grad_in, nodes_in, *rest):
    given, grad_out, rest = rest[:6], rest[6], rest[7:]
    terms_outside, stash_outside, inside = rest[: len(TERMS)], rest[len(TERMS) :][: len(STASH)], rest[len(TERMS) + len(STASH) :]
    stash_inside, (terms_qkv, terms_out) = inside[: len(STASH)], inside[len(STASH) :][:2]
    place, weight_sems, terms_sems, stash_sems, times = inside[len(STASH) + 2 :]
    weights = Weights(*given, place, weight_sems, info[1], info[2], range(STAGE_LAYERS))
    stash = dict(zip(STASH, stash_inside))
    weights.start()
    masks, mean_matrix = head_masks(), head_mean_matrix()

    @pl.when(info[3] == 1)
    def _():
        times[...] = multiplicities(info[0], tile_lists, counts, virtual)
        sheets = Sheets(TERMS, terms_outside, (stash["normed"], stash["mixed"], terms_qkv, terms_out), terms_sems, False)
        grad_out[...] = run_chain(
            hidden_in[...], grad_in[0], weights, times, masks, mean_matrix, stash, terms_qkv, terms_out, sheets.start
        )
        for layer in range(STAGE_LAYERS):
            sheets.wait(layer)

    @pl.when(info[3] == 0)
    def _():
        times[...] = multiplicities(info[4], tile_lists, counts, virtual)
        sheets = Sheets(STASH, stash_outside, stash_inside, stash_sems, False)
        grad_out[...] = sent[...]
        hidden = nodes_in[0]
        for layer in range(STAGE_LAYERS):
            weights.wait(layer)
            hidden = forward_layer(layer, hidden, weights.layer(layer), times[...], masks, mean_matrix, stash)
            sheets.start(layer)
        for layer in range(STAGE_LAYERS):
            sheets.wait(layer)


def later_kernel(info, tile_lists, counts, virtual, hidden_in, grad_in, *rest):
    given, outside, outs, inside = rest[:6], rest[6:10], rest[10:12], rest[12:]
    stash = dict(zip(STASH, inside[: len(STASH)]))
    terms_qkv, terms_out, *first = inside[len(STASH) :][:6]
    weight_place, weight_sems, place, terms_sems, out_sems, times = inside[len(STASH) + 6 :]
    low = 2 * info[5]
    copies = [
        pltpu.make_async_copy(outside[i].at[low + slot], first[i].at[slot], terms_sems.at[i, slot])
        for i in range(len(TERMS))
        for slot in range(2)
    ]
    weights = Weights(*given, weight_place, weight_sems, info[1], info[2], range(STAGE_LAYERS))
    weights.start()
    for copy in copies:
        copy.start()
    masks, mean_matrix = head_masks(), head_mean_matrix()
    times[...] = multiplicities(info[4], tile_lists, counts, virtual)
    run_chain(
        hidden_in[...], grad_in[0], weights, times, masks, mean_matrix, stash, terms_qkv, terms_out, lambda layer: None
    )
    for copy in copies:
        copy.wait()
    results = Results(outs, place, out_sems)
    second = (stash["normed"], stash["mixed"], terms_qkv, terms_out)
    for slot in range(2):
        weight_gradients(slot, *(both(first[i][slot], second[i][low + slot]) for i in range(len(TERMS))), place, info[2])
        results.start(slot)
    for slot in range(2):
        results.wait(slot)


def backward_kernel(info, grad_in, grad_in2, *rest):
    order = tuple(reversed(range(STAGE_LAYERS)))
    count = len(STASH)
    outside, outside2, given, outs = rest[:count], rest[count:][:count], rest[2 * count :][:6], rest[2 * count + 6 :][:2]
    inside = rest[2 * count + 8 :]
    weight_place, weight_sems, place, kept_qkv, kept_out, sems, sems2, out_sems = inside[2 * count :]
    weights = Weights(*given, weight_place, weight_sems, info[1], info[2], order)
    sheets = [
        Sheets(STASH, outside, inside[:count], sems, True),
        Sheets(STASH, outside2, inside[count:][:count], sems2, True),
    ]
    results = Results(outs, place, out_sems)
    for layer in order:
        for one in sheets:
            one.start(layer)
        weights.each(layer, lambda copy: copy.start())
    masks, mean_matrix = head_masks(), head_mean_matrix()

    def step(layer, grads):
        for one in sheets:
            one.wait(layer)
        weights.wait(layer)
        return tuple(
            zip(*(backward_layer(layer, g, weights.layer(layer), masks, mean_matrix, one.refs) for g, one in zip(grads, sheets)))
        )

    def finish(layer, grad_qkv, grad_out):
        normed, mixed = (both(*(one.refs[n][layer] for one in sheets)) for n in ("normed", "mixed"))
        weight_gradients(layer % 2, normed, mixed, grad_qkv, grad_out, place, info[2])
        results.start(layer % 2)

    grads = (grad_in[...], grad_in2[...])
    for layer in (3, 2):
        kept_out[layer - 2] = both(*grads)
        grads, terms = step(layer, grads)
        kept_qkv[layer - 2] = both(*terms)
    kept_out[2] = both(*grads)

    @pl.when(info[5] == 1)
    def _():
        for layer in (3, 2):
            finish(layer, kept_qkv[layer - 2], kept_out[layer - 2])
        for layer in (1, 0):
            for one in sheets:
                one.wait(layer)
            weights.wait(layer)

    @pl.when(info[5] == 0)
    def _():
        now = (kept_out[2, :ROWS], kept_out[2, ROWS:])
        for layer in (1, 0):
            before = both(*now)
            now, terms = step(layer, now)
            finish(layer, both(*terms), before)

    for slot in range(2):
        results.wait(slot)


ANYWHERE = pl.BlockSpec(memory_space=pl.ANY)
IN_HBM = pl.BlockSpec(memory_space=pltpu.HBM)
HIDDEN = jax.ShapeDtypeStruct((ROWS, D), BF16)
HIDDEN_BLOCK = pl.BlockSpec((ROWS, D), lambda *_: (0, 0))
BATCH_BLOCK = pl.BlockSpec((1, ROWS, D), lambda step, info, *_: (info[0], 0, 0))
SECOND_BLOCK = pl.BlockSpec((1, ROWS, D), lambda step, info, *_: (info[4], 0, 0))
GRAD_HALF = jax.ShapeDtypeStruct((2, 2, D, INNER), BF16)
WEIGHT_SCRATCH = [
    pltpu.VMEM((STAGE_LAYERS, 4, D, INNER), BF16),
    pltpu.SemaphoreType.DMA((STAGE_LAYERS, 2)),
]
GRAD_PLACE = pltpu.VMEM((2, 2, 2, D, INNER), BF16)
TIMES = pltpu.VMEM((HEADS * ROWS, ROWS), F32)


def layered(sizes, make):
    return [make((STAGE_LAYERS, *shape), kind) for shape, kind in sizes.values()]


def semaphores(count):
    return pltpu.SemaphoreType.DMA((count, STAGE_LAYERS))


def call(kernel, prefetched, in_specs, out_specs, out_shape, scratch, args, megabytes=48):
    return pl.pallas_call(
        kernel,
        grid_spec=pltpu.PrefetchScalarGridSpec(
            num_scalar_prefetch=prefetched,
            grid=(1,),
            in_specs=in_specs,
            out_specs=out_specs,
            scratch_shapes=scratch,
        ),
        out_shape=out_shape,
        compiler_params=pltpu.CompilerParams(vmem_limit_bytes=megabytes * 2**20),
    )(*args)


def run_pack(info, w_qkv, w_out):
    shapes = [jax.ShapeDtypeStruct((blocks, D, INNER), BF16) for blocks in (4, 2)]
    sems = [pltpu.SemaphoreType.DMA((2, 5))]
    return call(pack_kernel, 1, [IN_HBM] * 2, [ANYWHERE] * 2, shapes, sems, (info, w_qkv, w_out), 1)


def run_unpack(info, mine, other):
    shapes = [jax.ShapeDtypeStruct((1, *shape), BF16) for shape in ((D, 3 * INNER), (INNER, D))]
    sems = [pltpu.SemaphoreType.DMA((5,))]
    return call(unpack_kernel, 1, [ANYWHERE] * 2, [IN_HBM] * 2, shapes, sems, (info, mine, other), 1)


def run_forward(info, tables, nodes, weights):
    return call(
        forward_kernel,
        4,
        [BATCH_BLOCK] + [ANYWHERE] * 6,
        [HIDDEN_BLOCK] + [ANYWHERE] * len(STASH),
        [HIDDEN] + layered(STASH, jax.ShapeDtypeStruct),
        layered(STASH, pltpu.VMEM) + WEIGHT_SCRATCH + [semaphores(len(STASH)), TIMES],
        (info, *tables, nodes, *weights),
        58,
    )


def run_middle(info, tables, hidden, sent, cotangent, nodes, weights):
    return call(
        middle_kernel,
        4,
        [HIDDEN_BLOCK, HIDDEN_BLOCK, BATCH_BLOCK, SECOND_BLOCK] + [ANYWHERE] * 6,
        [HIDDEN_BLOCK] + [ANYWHERE] * (len(TERMS) + len(STASH)),
        [HIDDEN] + layered(TERMS, jax.ShapeDtypeStruct) + layered(STASH, jax.ShapeDtypeStruct),
        layered(STASH, pltpu.VMEM)
        + layered(TERMS, pltpu.VMEM)[2:]
        + WEIGHT_SCRATCH
        + [semaphores(len(TERMS)), semaphores(len(STASH)), TIMES],
        (info, *tables, hidden, sent, cotangent, nodes, *weights),
        50,
    )


def run_later(info, tables, hidden, cotangent, weights, terms):
    return call(
        later_kernel,
        4,
        [HIDDEN_BLOCK, SECOND_BLOCK] + [ANYWHERE] * (6 + len(TERMS)),
        [ANYWHERE] * 2,
        [GRAD_HALF] * 2,
        layered(STASH, pltpu.VMEM)
        + layered(TERMS, pltpu.VMEM)[2:]
        + [pltpu.VMEM((2, *shape), kind) for shape, kind in TERMS.values()]
        + WEIGHT_SCRATCH
        + [GRAD_PLACE, pltpu.SemaphoreType.DMA((len(TERMS), 2)), pltpu.SemaphoreType.DMA((2, 2)), TIMES],
        (info, *tables, hidden, cotangent, *weights, *terms),
    )


def run_backward(info, grads, stash, stash2, weights):
    return call(
        backward_kernel,
        1,
        [HIDDEN_BLOCK] * 2 + [ANYWHERE] * (2 * len(STASH) + 6),
        [ANYWHERE] * 2,
        [GRAD_HALF] * 2,
        layered(STASH, pltpu.VMEM) * 2
        + WEIGHT_SCRATCH
        + [GRAD_PLACE, pltpu.VMEM((2, 2 * ROWS, 3 * INNER), BF16), pltpu.VMEM((3, 2 * ROWS, D), BF16)]
        + [semaphores(len(STASH)), semaphores(len(STASH)), pltpu.SemaphoreType.DMA((2, 2))],
        (info, *grads, *stash, *stash2, *weights),
    )


def swapped(value, axis):
    return lax.ppermute(value, axis, [(0, 1), (1, 0)])


def fetched(value, flip_y, flip_x):
    axes = ("yl", "xl", "xh", "core")
    pairs = []
    for y in range(2):
        for x in range(2):
            for upper in range(2):
                for core in range(2):
                    there = upper ^ (core if flip_x else 0)
                    source = ((y * 2 + x) * 2 + upper) * 2 + core
                    target = (((y ^ flip_y) * 2 + (x ^ flip_x)) * 2 + there) * 2 + core
                    pairs.append((source, target))
    return lax.ppermute(value, axes, pairs)


def per_device(nodes, cotangent, w_qkv, w_out, tile_lists, counts, virtual):
    stage = lax.axis_index("yh")
    y, x, core = lax.axis_index("yl"), lax.axis_index("xl"), lax.axis_index("core")
    me = y * 2 + x
    batch = jnp.where(stage == 0, y, 1 - y) * 2 + x
    info = jnp.stack([batch, me, core, stage, batch ^ 2, y]).astype(jnp.int32)
    tables = (tile_lists.transpose(1, 2, 0), counts.transpose(1, 0), virtual)
    own, half = run_pack(info, w_qkv, w_out)
    near2 = fetched(half, 1, 0)
    near3 = fetched(half, 1, 1)
    beside = fetched(own, 0, 1)
    far2, far3 = swapped(near2, "core"), swapped(near3, "core")
    weights = (own, beside, near2, far2, near3, far3)

    hidden, *stash = run_forward(info, tables, nodes, weights)
    pair = ("yh", "yl")
    across, crossed = [(0, 3), (1, 2), (2, 1), (3, 0)], [(0, 2), (1, 3), (2, 0), (3, 1)]
    received = lax.ppermute(hidden, pair, across)
    grad, *rest = run_middle(info, tables, received, hidden, cotangent, nodes, weights)
    terms, stash2 = rest[: len(TERMS)], rest[len(TERMS) :]
    grads = (lax.ppermute(grad, pair, across), lax.ppermute(grad, pair, crossed))
    keep, send = lax.cond(
        stage == 0,
        lambda: tuple(run_backward(info, grads, stash, stash2, weights)),
        lambda: tuple(run_later(info, tables, grads[1], cotangent, weights, terms)),
    )

    def added(value, axis):
        return jnp.sum(value.astype(F32), axis=axis).astype(BF16)

    def repeated(value, times):
        return jnp.broadcast_to(value, (times, *value.shape))

    far, pairs, near = (lax.axis_size(axis) for axis in ("zh", "za", "zb"))
    total = (keep.astype(F32) + swapped(send, "core").astype(F32)).astype(BF16)
    total = lax.all_to_all(total.reshape(4 * near, D // near, INNER), ("xl", "xh", "zb"), 0, 0, tiled=True)
    total = added(total.reshape(4 * near, D // near, INNER), 0).reshape(pairs, D // (near * pairs), INNER)
    upper = lax.axis_index("za") == 1
    kept, given = jnp.where(upper, total[1], total[0]), jnp.where(upper, total[0], total[1])
    total = (kept.astype(F32) + swapped(given, "za").astype(F32)).astype(BF16)
    total = added(lax.all_to_all(repeated(total, far), "zh", 0, 0, tiled=True), 0)
    total = lax.all_to_all(repeated(total, 2 * near * pairs), ("xh", "zb", "za"), 0, 0, tiled=True)
    mine = total.reshape(2, D, INNER)
    grad_qkv, grad_out = run_unpack(info, mine, swapped(mine, "core"))
    return (grad_qkv, grad_out)


def solution(mesh):
    depth = mesh.shape["dp"] // 4
    near = min(depth, 2)
    pairs = min(depth // near, 2)
    far = depth // (near * pairs)
    names = ("yh", "yl", "xl", "zh", "za", "zb", "xh", "core")
    cut = Mesh(mesh.devices.reshape(2, 2, 2, far, pairs, near, 2, 2), names)
    section, dp = P(("yh", "yl", "xl")), P(("zh", "za", "zb", "xh", "core"))
    return jax.shard_map(
        per_device,
        mesh=cut,
        in_specs=(dp, dp, section, section, dp, dp, dp),
        out_specs=(section, section),
        check_vma=False,
    )
```
